32 devices in a mesh: dp: 8 (over z, y), reg: 4 (over x, core).
Axes of the slice: x: 2, y: 2, z: 4, core: 2. Of those that a mesh axis runs over, the one named last changes fastest.
Arguments:
- tokens: bfloat16 [30720, 768], P(('dp', 'reg')), may hold values from -6 to 6
- cotangent: bfloat16 [30720, 768], P(('dp', 'reg')), may hold values from -6 to 6
- distance_cot: float32 [160], P('dp'), may hold values from -262144 to 262144
- lengths: int32 [160, 2], P('dp'), may hold values from 16 to 128, as said below
- w_qkv: bfloat16 [768, 2304], replicated, may hold values from -0.21875 to 0.21875
- q_bias: float32 [768], replicated, may hold values from -3 to 3
- v_bias: float32 [768], replicated, may hold values from -3 to 3
- w_out: bfloat16 [768, 768], replicated, may hold values from -0.875 to 0.875
- out_bias: float32 [768], replicated, may hold values from -3 to 3
- ln1_gain: float32 [768], replicated, may hold values from 0.1 to 1.9
- ln1_bias: float32 [768], replicated, may hold values from -3 to 3
- w_in: bfloat16 [768, 3072], replicated, may hold values from -0.21875 to 0.21875
- in_bias: float32 [3072], replicated, may hold values from -3 to 3
- w_down: bfloat16 [3072, 768], replicated, may hold values from -0.109375 to 0.109375
- down_bias: float32 [768], replicated, may hold values from -3 to 3
- ln2_gain: float32 [768], replicated, may hold values from 0.1 to 1.9
- ln2_bias: float32 [768], replicated, may hold values from -3 to 3
Outputs:
- layer_out: bfloat16 [30720, 768], P(('dp', 'reg'))
- distance: float32 [160], P(('dp', 'reg'))
- tokens_grad: float32 [30720, 768], P(('dp', 'reg'))
- w_qkv_grad: float32 [768, 2304], replicated
- q_bias_grad: float32 [768], replicated
- v_bias_grad: float32 [768], replicated
- w_out_grad: float32 [768, 768], replicated
- out_bias_grad: float32 [768], replicated
- ln1_gain_grad: float32 [768], replicated
- ln1_bias_grad: float32 [768], replicated
- w_in_grad: float32 [768, 3072], replicated
- in_bias_grad: float32 [3072], replicated
- w_down_grad: float32 [3072, 768], replicated
- down_bias_grad: float32 [768], replicated
- ln2_gain_grad: float32 [768], replicated
- ln2_bias_grad: float32 [768], replicated
The draws below stay inside these ranges and needn't reach their ends.
Inputs may be any that keep to these rules, and one draw needn't show every extreme that they name: `lengths`: column 0 is a pair's word count, 16 to 64; column 1 its region count, 32 to 128. Each aligned block of 20 pairs holds a pair with 64 words and 128 regions.
All inputs are finite; a program needn't handle non-finite values.
Results may differ from the reference program's by a relative error of at most 0.015.
The reference program's roundings to bfloat16 on the way count: a program that leaves them out, or rounds other values in their place, can miss the bound.
Values may be sent and summed in bfloat16 or wider, within the bound.
A program may use at most 320 MiB of HBM per device.

```python
import jax
import jax.numpy as jnp
from jax import lax

D = 768
HEADS = 12
HEAD_DIM = 64
FF = 3072
WORDS = 64
REGIONS = 128
ITERS = 50
GROUP = 20
PAIRS = 160
TOKENS = 30720


def draw_lengths(key, part):
    key = jax.random.fold_in(key, 11)
    first_key, second_key, third_key = jax.random.split(key, 3)
    word_counts = jax.random.randint(first_key, (PAIRS,), max(WORDS // 4, 1), WORDS + 1)
    region_counts = jax.random.randint(second_key, (PAIRS,), max(REGIONS // 4, 1), REGIONS + 1)
    chosen = jax.random.randint(third_key, (PAIRS // GROUP,), 0, GROUP)
    filled = jnp.arange(PAIRS) % GROUP == jnp.repeat(chosen, GROUP)
    word_counts = jnp.where(filled, WORDS, word_counts)
    region_counts = jnp.where(filled, REGIONS, region_counts)
    return jnp.stack([word_counts, region_counts], 1).astype(jnp.int32)


def steps_of(rng, shape, pieces, low, largest):
    level = 1.0
    for axis_at, blocks in pieces:
        heights = jax.random.uniform(jax.random.fold_in(jax.random.fold_in(rng, 6), axis_at), (blocks,), jnp.float32, low / len(pieces), largest / len(pieces))
        level = level * jnp.repeat(jnp.exp(heights), shape[axis_at] // blocks).reshape((-1,) + (1,) * (len(shape) - 1 - axis_at))
    return level


def bell_draw(rng, shape, deviation, bound, pieces=(), dtype=jnp.bfloat16):
    values = jax.random.normal(rng, shape, jnp.float32) * deviation
    if len(pieces) > 0:
        values = steps_of(rng, shape, pieces, -0.22, 0.18) * values
    return jnp.clip(values, min=-bound, max=bound).astype(dtype)


def setup_inputs(seed: int = 0) -> dict:
    arg_keys = jax.random.split(jax.random.key(seed), 18)
    return {
        "tokens": bell_draw(arg_keys[0], (TOKENS, D), 1.0, 6.0, ((0, 32),)),
        "cotangent": bell_draw(arg_keys[1], (TOKENS, D), 1.0, 6.0, ((0, 32),)),
        "distance_cot": bell_draw(arg_keys[2], (PAIRS,), (WORDS * D), 262144.0, ((0, 8),), jnp.float32),
        "lengths": draw_lengths(jax.random.fold_in(arg_keys[17], 71), 0),
        "w_qkv": bell_draw(arg_keys[4], (D, 3 * D), D ** -0.5, 0.21875),
        "q_bias": bell_draw(arg_keys[5], (D,), 0.5, 3.0, (), jnp.float32),
        "v_bias": bell_draw(arg_keys[6], (D,), 0.5, 3.0, (), jnp.float32),
        "w_out": bell_draw(arg_keys[7], (D, D), (D // 16) ** -0.5, 0.875),
        "out_bias": bell_draw(arg_keys[8], (D,), 0.5, 3.0, (), jnp.float32),
        "ln1_gain": jnp.clip(1.0 + 0.18 * jax.random.normal(arg_keys[9], (D,), jnp.float32), 0.1, 1.9),
        "ln1_bias": bell_draw(arg_keys[10], (D,), 0.5, 3.0, (), jnp.float32),
        "w_in": bell_draw(arg_keys[11], (D, FF), D ** -0.5, 0.21875),
        "in_bias": bell_draw(arg_keys[12], (FF,), 0.5, 3.0, (), jnp.float32),
        "w_down": bell_draw(arg_keys[13], (FF, D), FF ** -0.5, 0.109375),
        "down_bias": bell_draw(arg_keys[14], (D,), 0.5, 3.0, (), jnp.float32),
        "ln2_gain": jnp.clip(1.0 + 0.18 * jax.random.normal(arg_keys[15], (D,), jnp.float32), 0.1, 1.9),
        "ln2_bias": bell_draw(arg_keys[16], (D,), 0.5, 3.0, (), jnp.float32),
    }


BETA = 0.5
EPS = 1e-06
HIGH = lax.Precision.HIGHEST

@jax.custom_vjp
def low(v):
    return lax.optimization_barrier(v.astype(jnp.bfloat16)).astype(jnp.float32)

@jax.custom_vjp
def low_back(v):
    return v

def low_keep(v):
    return (low(v), None)

def low_pass(kept, grad):
    return (grad,)

def back_keep(v):
    return (v, None)

def back_low(kept, grad):
    return (low(grad),)
low.defvjp(low_keep, low_pass)
low_back.defvjp(back_keep, back_low)

def layer_norm(hidden, gain, shift):
    center = hidden - lax.optimization_barrier(jnp.mean(hidden, -1, keepdims=True))
    scaled = center * lax.rsqrt(lax.optimization_barrier(jnp.mean(center * center, -1, keepdims=True)) + EPS)
    return scaled * gain + shift

def cost_pieces(joint_mask, word_rows, region_rows):
    word_unit = word_rows * lax.rsqrt(lax.optimization_barrier(jnp.sum(word_rows * word_rows, -1, keepdims=True)) + EPS)
    region_unit = region_rows * lax.rsqrt(lax.optimization_barrier(jnp.sum(region_rows * region_rows, -1, keepdims=True)) + EPS)
    cosine = jnp.einsum('pwd,prd->pwr', word_unit, region_unit, precision=HIGH)
    cost_tile = (1.0 - cosine) * joint_mask
    return (cost_tile, jnp.exp(-cost_tile / BETA) * joint_mask)

def half_first(region_valid, region_len, kernel, transport, word_scale):
    joined = kernel * transport
    region_tot = lax.optimization_barrier(jnp.sum(joined * word_scale[:, :, None], 1))
    region_scale = region_valid / (region_len[:, None] * region_tot + (1.0 - region_valid))
    partial_sum = lax.optimization_barrier(jnp.sum(joined * region_scale[:, None, :], 2))
    return (joined, region_scale, partial_sum)

def half_second(word_valid, word_len, joined, region_scale, word_tot):
    word_scale = word_valid / (word_len[:, None] * word_tot + (1.0 - word_valid))
    transport = joined * region_scale[:, None, :] * word_scale[:, :, None]
    return (transport, word_scale)

def forward_block(params, inputs, lengths):
    w_qkv, q_bias, v_bias, w_out, out_bias, ln1_gain, ln1_bias, w_in, in_bias, w_down, down_bias, ln2_gain, ln2_bias = params
    pair_count = inputs.shape[0]
    slot_rows = WORDS + REGIONS
    position = jnp.arange(slot_rows)[None, :]
    key_valid = jnp.where(position < WORDS, position < lengths[:, 0:1], position - WORDS < lengths[:, 1:2])
    flat_in = inputs.reshape(pair_count * slot_rows, D)
    packed = jnp.dot(flat_in, w_qkv, precision=HIGH) + jnp.concatenate([q_bias, jnp.zeros_like(q_bias), v_bias])
    packed = low(low_back(packed)).reshape(pair_count, slot_rows, 3, HEADS, HEAD_DIM)
    scores = jnp.einsum('pqhd,pkhd->phqk', packed[:, :, 0], packed[:, :, 1], precision=HIGH) * HEAD_DIM ** (-0.5)
    scores = jnp.where(key_valid[:, None, None, :], low_back(scores), -1e+30)
    probs = low(jax.nn.softmax(scores, -1))
    context = jnp.einsum('phqk,pkhd->pqhd', probs, packed[:, :, 2], precision=HIGH).reshape(pair_count * slot_rows, D)
    context = low(low_back(context))
    attended = low_back(jnp.dot(context, w_out, precision=HIGH) + out_bias)
    normed = layer_norm(flat_in + attended, ln1_gain, ln1_bias)
    inner = low_back(jnp.dot(low(normed), w_in, precision=HIGH) + in_bias)
    activated = low(jax.nn.gelu(inner, approximate=False))
    branch = low_back(jnp.dot(activated, w_down, precision=HIGH) + down_bias)
    result = low(layer_norm(normed + branch, ln2_gain, ln2_bias))
    grouped = result.reshape(pair_count, slot_rows, D)
    word_len = lengths[:, 0].astype(jnp.float32)
    region_len = lengths[:, 1].astype(jnp.float32)
    word_valid = (jnp.arange(WORDS)[None, :] < lengths[:, 0:1]).astype(jnp.float32)
    region_valid = (jnp.arange(REGIONS)[None, :] < lengths[:, 1:2]).astype(jnp.float32)
    joint_mask = word_valid[:, :, None] * region_valid[:, None, :]
    cost_tile, kernel = cost_pieces(joint_mask, grouped[:, :WORDS], grouped[:, WORDS:])

    def step(state_in, unused_item):
        transport, word_scale = state_in
        joined, region_scale, partial_sum = half_first(region_valid, region_len, kernel, transport, word_scale)
        return (half_second(word_valid, word_len, joined, region_scale, partial_sum), None)
    (transport, word_scale), unused_out = lax.scan(step, (joint_mask, word_valid / word_len[:, None]), None, length=ITERS)
    distance = lax.optimization_barrier(jnp.sum(transport * cost_tile, (1, 2)))
    return (result, distance)

def reference(tokens, cotangent, distance_cot, lengths, w_qkv, q_bias, v_bias, w_out, out_bias, ln1_gain, ln1_bias, w_in, in_bias, w_down, down_bias, ln2_gain, ln2_bias):
    params = tuple((member.astype(jnp.float32) for member in (w_qkv, q_bias, v_bias, w_out, out_bias, ln1_gain, ln1_bias, w_in, in_bias, w_down, down_bias, ln2_gain, ln2_bias)))
    slot_rows = WORDS + REGIONS
    per_block = max([1] + [candidate for candidate in range(1, PAIRS + 1) if PAIRS % candidate == 0 and candidate * slot_rows <= 4096])
    block_count = PAIRS // per_block
    input_blocks = tokens.astype(jnp.float32).reshape(block_count, per_block, slot_rows, D)
    cot_blocks = cotangent.astype(jnp.float32).reshape(block_count, per_block * slot_rows, D)
    weight_blocks = distance_cot.astype(jnp.float32).reshape(block_count, per_block)
    length_blocks = lengths.reshape(block_count, per_block, 2)
    start_grads = jax.tree.map(jnp.zeros_like, params)

    def block_step(running, slices):
        block_in, cot_in, weight_in, length_in = slices
        outputs, pullback = jax.vjp(lambda weights, rows_in: forward_block(weights, rows_in, length_in), params, block_in)
        grad_params, grad_inputs = pullback((cot_in, weight_in))
        return (jax.tree.map(jnp.add, running, grad_params), (outputs[0], outputs[1], grad_inputs))
    grads, (out_blocks, dist_blocks, input_grads) = lax.scan(block_step, start_grads, (input_blocks, cot_blocks, weight_blocks, length_blocks))
    layer_out = out_blocks.reshape(TOKENS, D).astype(jnp.bfloat16)
    distance = dist_blocks.reshape(PAIRS)
    tokens_grad = input_grads.reshape(TOKENS, D)
    return (layer_out, distance, tokens_grad, grads[0], grads[1], grads[2], grads[3], grads[4], grads[5], grads[6], grads[7], grads[8], grads[9], grads[10], grads[11], grads[12])
```

```python
import functools
import heapq
import math

import jax
import jax.numpy as jnp
from jax import lax
from jax.experimental import pallas as pl
from jax.experimental.pallas import tpu as pltpu
from jax.sharding import PartitionSpec as P

D = 768
HEADS = 12
HEAD_DIM = 64
WORDS = 64
REGIONS = 128
SLOT = WORDS + REGIONS
ITERS = 50
EPS = 1e-06
f32 = jnp.float32
bf16 = jnp.bfloat16
MESH = pl.DeviceIdType.MESH
VMEM_LIMIT = 60 * 2**20

BLK = 1536
COLS = 256
NBLK = 18
HALVES = 5
RBLK = BLK - (BLK >> HALVES)
ORDERS = (
    ("c", "x", "y", "z0", "z1"),
    ("c", "y", "x", "z0", "z1"),
    ("c", "z0", "x", "y", "z1"),
    ("c", "x", "y", "z0", "z1"),
    ("c", "y", "x", "z0", "z1"),
    ("c", "z0", "y", "x", "z1"),
)


def order_of(block):
    return ORDERS[block % len(ORDERS)]


def event_order(ready, extra, rate=85e3, core_rate=470e3, delay=1.8, cost=0.25):
    free = {}
    heap = [(at, block - 1000, block, -1) for block, at in enumerate(ready)]
    heapq.heapify(heap)
    found = []
    count = 0
    last = 2 * HALVES + extra - 1
    while heap:
        now, _, block, event = heapq.heappop(heap)
        if event >= 0:
            found.append((now, block, event))
            now = now + cost
        if event == last:
            continue
        step = event + 1
        if step < HALVES:
            dim, size = order_of(block)[step], BLK >> (step + 1)
        elif step < HALVES + extra:
            dim, size = "far", BLK >> HALVES
        else:
            back = last - step
            dim, size = order_of(block)[back], BLK >> (back + 1)
        sent = size * COLS * 2
        line = "z" if dim in ("z0", "z1") else dim
        took = sent / core_rate if dim == "c" else 2 * sent / rate
        begin = max(now, free.get(line, 0.0))
        free[line] = begin + took
        more = took if dim == "z1" else 0.0
        heapq.heappush(heap, (begin + took + more + delay, count, block, step))
        count += 1
    return found


def mesh_partners(ndp):
    dp = lax.axis_index("dp")
    reg = lax.axis_index("reg")
    names = [("c", "reg", 1), ("x", "reg", 2), ("y", "dp", 1), ("z0", "dp", 2), ("z1", "dp", 4)]
    step = 8
    while step < ndp:
        names.append(("far%d" % step, "dp", step))
        step *= 2
    partners = {}
    for name, axis, step in names:
        at = reg if axis == "reg" else dp
        bit = lax.rem(at // step, 2)
        other = at + step - 2 * step * bit
        partners[name] = (bit, (dp, other) if axis == "reg" else (other, reg))
    return partners


class Exchange:
    def __init__(self, ndp, table, full, landing, far, small, small_in, sems):
        self.partners = mesh_partners(ndp)
        self.fars = [name for name in self.partners if name.startswith("far")]
        self.extra = len(self.fars)
        self.table, self.full, self.landing, self.far = table, full, landing, far
        self.small, self.small_in = small, small_in
        self.rs_send, self.rs_recv, self.ag_send, self.ag_recv, self.far_send, self.far_recv, self.sm_send, self.sm_recv, self.own = sems

    def barrier(self):
        bar = pltpu.get_barrier_semaphore()
        for _, who in self.partners.values():
            pl.semaphore_signal(bar, inc=1, device_id=who, device_id_type=MESH)
        pl.semaphore_wait(bar, len(self.partners))

    def offset(self, block, steps):
        at, size = block * BLK, BLK
        for step in range(steps):
            size //= 2
            at = at + self.partners[order_of(block)[step]][0] * size
        return pl.multiple_of(at, 16) if steps else at

    def halving(self, block, step):
        bit, who = self.partners[order_of(block)[step]]
        size = BLK >> (step + 1)
        src = pl.multiple_of(self.offset(block, step) + (1 - bit) * size, 16)
        land = block * RBLK + (BLK - (BLK >> step))
        return pltpu.make_async_remote_copy(
            self.table.at[pl.ds(src, size)],
            self.landing.at[pl.ds(land, size)],
            self.rs_send.at[block, step],
            self.rs_recv.at[block, step],
            device_id=who,
            device_id_type=MESH,
        )

    def far_step(self, block, index):
        _, who = self.partners[self.fars[index]]
        size = BLK >> HALVES
        src = self.offset(block, HALVES)
        return pltpu.make_async_remote_copy(
            self.table.at[pl.ds(src, size)],
            self.far.at[block, index],
            self.far_send.at[block, index],
            self.far_recv.at[block, index],
            device_id=who,
            device_id_type=MESH,
        )

    def returning(self, block, step):
        _, who = self.partners[order_of(block)[step]]
        size = BLK >> (step + 1)
        src = self.offset(block, step + 1)
        held = self.table if step + 1 == HALVES else self.full
        return pltpu.make_async_remote_copy(
            held.at[pl.ds(src, size)],
            self.full.at[pl.ds(src, size)],
            self.ag_send.at[block, step],
            self.ag_recv.at[block, step],
            device_id=who,
            device_id_type=MESH,
        )

    def keep(self, block):
        at = pl.ds(self.offset(block, HALVES), BLK >> HALVES)
        return pltpu.make_async_copy(self.table.at[at], self.full.at[at], self.own.at[block])

    def produce(self, block):
        self.halving(block, 0).start()

    def start_after(self, block, event):
        step = event + 1
        if step < HALVES:
            self.halving(block, step).start()
        elif step < HALVES + self.extra:
            self.far_step(block, step - HALVES).start()
        elif step < 2 * HALVES + self.extra:
            back = 2 * HALVES + self.extra - 1 - step
            if back + 1 == HALVES:
                self.keep(block).start()
            self.returning(block, back).start()

    def handle(self, block, event):
        if event < HALVES:
            self.halving(block, event).wait_recv()
            size = BLK >> (event + 1)
            off = self.offset(block, event + 1)
            land = block * RBLK + (BLK - (BLK >> event))
            rows = min(size, 192)

            def add(index, carry):
                at = pl.ds(pl.multiple_of(off + index * rows, 16), rows)
                come = self.landing[pl.ds(pl.multiple_of(land + index * rows, 16), rows), :]
                self.table[at, :] = (self.table[at, :].astype(f32) + come.astype(f32)).astype(bf16)
                return carry

            lax.fori_loop(0, size // rows, add, 0)
        elif event < HALVES + self.extra:
            index = event - HALVES
            copy = self.far_step(block, index)
            copy.wait()
            at = pl.ds(self.offset(block, HALVES), BLK >> HALVES)
            self.table[at, :] = (self.table[at, :].astype(f32) + self.far[block, index].astype(f32)).astype(bf16)
        else:
            back = 2 * HALVES + self.extra - 1 - event
            self.returning(block, back).wait_recv()
            if back + 1 == HALVES:
                self.keep(block).wait()
        self.start_after(block, event)

    def small_copy(self, index):
        _, who = self.partners[list(self.partners)[index]]
        return pltpu.make_async_remote_copy(
            self.small,
            self.small_in.at[index],
            self.sm_send.at[index],
            self.sm_recv.at[index],
            device_id=who,
            device_id_type=MESH,
        )

    def small_handle(self, index):
        self.small_copy(index).wait()
        self.small[...] = self.small[...] + self.small_in[index]
        if index + 1 < len(self.partners):
            self.small_copy(index + 1).start()

    def finish(self):
        for block in range(NBLK):
            for step in range(HALVES):
                self.halving(block, step).wait_send()
                self.returning(block, step).wait_send()


def exchange_scratch(ndp):
    extra = max(int(math.log2(ndp)) - 3, 0)
    count = HALVES + extra
    dma = pltpu.SemaphoreType.DMA
    return [
        pltpu.VMEM((NBLK * RBLK, COLS), bf16),
        pltpu.VMEM((NBLK, max(extra, 1), BLK >> HALVES, COLS), bf16),
        pltpu.VMEM((16, D), f32),
        pltpu.VMEM((count, 16, D), f32),
        dma((NBLK, HALVES)),
        dma((NBLK, HALVES)),
        dma((NBLK, HALVES)),
        dma((NBLK, HALVES)),
        dma((NBLK, max(extra, 1))),
        dma((NBLK, max(extra, 1))),
        dma((count,)),
        dma((count,)),
        dma((NBLK,)),
    ]


def sum_table(table, small, ndp):
    extra = max(int(math.log2(ndp)) - 3, 0)
    events = event_order([0.05 * block for block in range(NBLK)], extra)

    def kernel(table_in, small_ref, table_out, small_out, gbuf, lsem, landing, far, sbuf, sland, *sems):
        ex = Exchange(ndp, gbuf, table_out, landing, far, sbuf, sland, sems)
        rows = [pl.ds(block * BLK, BLK) for block in range(NBLK)]
        loads = [pltpu.make_async_copy(table_in.at[at], gbuf.at[at], lsem.at[b]) for b, at in enumerate(rows)]
        for load in loads:
            load.start()
        sbuf[...] = small_ref[...]
        ex.barrier()
        ex.small_copy(0).start()
        for block in range(NBLK):
            loads[block].wait()
            ex.produce(block)
        for index in range(len(ex.partners)):
            ex.small_handle(index)
        small_out[...] = sbuf[...]
        for _, block, event in events:
            ex.handle(block, event)
        ex.finish()

    anywhere = pl.BlockSpec(memory_space=pl.ANY)
    vmem = pl.BlockSpec(memory_space=pltpu.VMEM)
    dma = pltpu.SemaphoreType.DMA
    return pl.pallas_call(
        kernel,
        out_shape=(jax.ShapeDtypeStruct((NBLK * BLK, COLS), bf16), jax.ShapeDtypeStruct((16, D), f32)),
        in_specs=[anywhere, vmem],
        out_specs=(anywhere, vmem),
        scratch_shapes=[pltpu.VMEM((NBLK * BLK, COLS), bf16), dma((NBLK,))] + exchange_scratch(ndp),
        compiler_params=pltpu.CompilerParams(collective_id=1, has_side_effects=True, vmem_limit_bytes=VMEM_LIMIT),
        name="sum_table",
    )(table, small)


def widen(table, rows, grid, in_map, out_map, shape):
    def kernel(a, o):
        o[...] = a[...].astype(f32)

    return pl.pallas_call(
        kernel,
        grid=grid,
        out_shape=jax.ShapeDtypeStruct(shape, f32),
        in_specs=[pl.BlockSpec((rows, COLS), in_map)],
        out_specs=pl.BlockSpec((rows, COLS), out_map),
        name="widen",
    )(table)


def unpack_table(table):
    down = widen(table, 512, (6, 3), lambda j, c: (6 * j + c, 0), lambda j, c: (j, c), (4 * D, D))
    w_in = widen(table, 768, (6, 2), lambda j, c: (4 * j + 2 + c, 0), lambda j, c: (0, 2 * j + c), (D, 4 * D))
    out = widen(table, 768, (3,), lambda c: (24 + c, 0), lambda c: (0, c), (D, D))
    qkv = widen(table, 768, (9,), lambda c: (27 + c, 0), lambda c: (0, c), (D, 3 * D))
    return qkv, out, w_in, down


def pack_table(qkv, out, w_in, down):
    down = down.astype(bf16).reshape(6, 512, 3, 256).transpose(0, 2, 1, 3).reshape(6, 1, BLK, COLS)
    w_in = w_in.astype(bf16).reshape(768, 6, 2, 256).transpose(1, 2, 0, 3).reshape(6, 1, BLK, COLS)
    first = jnp.concatenate([down, w_in], 1).reshape(12 * BLK, COLS)
    tail = jnp.concatenate([out, qkv], 1).astype(bf16).reshape(768, 6, 2, 256).transpose(1, 2, 0, 3)
    return jnp.concatenate([first, tail.reshape(6 * BLK, COLS)], 0)


def align_body(pairs, first, rows_ref, len_ref, dcot_ref, grad_ref, dist_ref, kern, trans, uhist, ahist, acc, alpha, gamma, cosr):
    P = range(pairs)
    eye = lax.broadcasted_iota(jnp.int32, (REGIONS, REGIONS), 0) == lax.broadcasted_iota(jnp.int32, (REGIONS, REGIONS), 1)
    wcol = lax.broadcasted_iota(jnp.int32, (WORDS, 1), 0)
    rrow = lax.broadcasted_iota(jnp.int32, (1, REGIONS), 1)
    nlen = [len_ref[first + p, 0] for p in P]
    mlen = [len_ref[first + p, 1] for p in P]
    nf = [v.astype(f32) for v in nlen]
    mf = [v.astype(f32) for v in mlen]
    dc = [dcot_ref[first + p] for p in P]
    wv = [(wcol < nlen[p]).astype(f32) for p in P]
    rv = [(rrow < mlen[p]).astype(f32) for p in P]
    rxs, rys = [], []
    for p in P:
        x = rows_ref[SLOT * p:SLOT * p + WORDS, :]
        y = rows_ref[SLOT * p + WORDS:SLOT * (p + 1), :]
        xf, yf = x.astype(f32), y.astype(f32)
        rx = lax.rsqrt(jnp.sum(xf * xf, -1, keepdims=True) + EPS)
        ry = lax.rsqrt(jnp.sum(yf * yf, -1, keepdims=True) + EPS)
        ryr = jnp.sum(jnp.where(eye, ry, 0.0), 0, keepdims=True)
        rxs.append(rx); rys.append((ry, ryr))
        cos = lax.dot_general(x, y, (((1,), (1,)), ((), ())), preferred_element_type=f32) * rx * ryr
        joint = wv[p] * rv[p]
        cost = (1.0 - cos) * joint
        cosr[p] = cos
        kern[p] = jnp.exp(-2.0 * cost) * joint
        trans[p] = joint
        ahist[0, p] = jnp.broadcast_to(wv[p] / nf[p], (WORDS, REGIONS))
    def fwd(t, _):
        joined = [kern[p] * trans[p] for p in P]
        a = [ahist[t, p] for p in P]
        s = [jnp.sum(joined[p] * a[p], 0, keepdims=True) for p in P]
        b = [rv[p] / (mf[p] * s[p] + (1.0 - rv[p])) for p in P]
        u = [joined[p] * b[p] for p in P]
        w = [jnp.sum(u[p], 1, keepdims=True) for p in P]
        an = [wv[p] / (nf[p] * w[p] + (1.0 - wv[p])) for p in P]
        for p in P:
            uhist[t, p] = u[p]
            ahist[t + 1, p] = jnp.broadcast_to(an[p], (WORDS, REGIONS))
            trans[p] = u[p] * an[p]
        return 0
    lax.fori_loop(0, ITERS, fwd, 0)
    cols = []
    for p in P:
        joint = wv[p] * rv[p]
        cost = (1.0 - cosr[p]) * joint
        tc = trans[p] * cost
        dist_ref[p] = jnp.sum(tc)
        g = tc * dc[p]
        cols.append(jnp.sum(g, 0, keepdims=True))
        alpha[p] = jnp.broadcast_to(jnp.sum(g, 1, keepdims=True), (WORDS, REGIONS))
        gamma[p] = jnp.zeros((WORDS, REGIONS), f32)
        acc[p] = float(ITERS) * g
    def bwd(i, cols):
        t = ITERS - i
        tf = t.astype(f32)
        u = [uhist[t - 1, p] for p in P]
        x = [nf[p] * alpha[p] * ahist[t, p] for p in P]
        y = [mf[p] * ahist[t - 1, p] for p in P]
        beta = [cols[p] - jnp.sum(u[p] * x[p], 0, keepdims=True) for p in P]
        ub = [u[p] * beta[p] for p in P]
        gm = [-y[p] * jnp.sum(ub[p], 1, keepdims=True) for p in P]
        go = [gamma[p] for p in P]
        ac = [acc[p] for p in P]
        for p in P:
            acc[p] = ac[p] - tf * (u[p] * x[p] + y[p] * ub[p])
            alpha[p] = 2.0 * gm[p] - go[p]
            gamma[p] = gm[p]
        return tuple(jnp.zeros_like(c) for c in cols)
    lax.fori_loop(0, ITERS, bwd, tuple(cols))
    for p in P:
        x = rows_ref[SLOT * p:SLOT * p + WORDS, :]
        y = rows_ref[SLOT * p + WORDS:SLOT * (p + 1), :]
        rx = rxs[p]; ry, ryr = rys[p]
        gc = dc[p] * trans[p] - 2.0 * acc[p]
        gcos = gc * cosr[p]
        m = gc * rx * ryr
        hi = m.astype(bf16)
        lo = (m - hi.astype(f32)).astype(bf16)
        nt = (((1,), (0,)), ((), ())); tn = (((0,), (0,)), ((), ()))
        gx = lax.dot_general(hi, y, nt, preferred_element_type=f32) + lax.dot_general(lo, y, nt, preferred_element_type=f32)
        gy = lax.dot_general(hi, x, tn, preferred_element_type=f32) + lax.dot_general(lo, x, tn, preferred_element_type=f32)
        sx = rx * rx * jnp.sum(gcos, 1, keepdims=True)
        sy = ry * ry * jnp.sum(jnp.where(eye, jnp.sum(gcos, 0, keepdims=True), 0.0), 1, keepdims=True)
        grad_ref[SLOT * p:SLOT * p + WORDS, :] = sx * x.astype(f32) - gx
        grad_ref[SLOT * p + WORDS:SLOT * (p + 1), :] = sy * y.astype(f32) - gy

def scratch(pairs):
    v = lambda *s: pltpu.VMEM(s, f32)
    W = (WORDS, REGIONS)
    return [v(pairs, *W), v(pairs, *W), v(ITERS, pairs, *W), v(ITERS + 1, pairs, *W), v(pairs, *W), v(pairs, *W), v(pairs, *W), v(pairs, *W)]

def align(rows, lengths, dcot, first, interpret=False):
    pairs = rows.shape[0] // SLOT
    def k(rows_ref, len_ref, dcot_ref, grad_ref, dist_ref, *sc):
        align_body(pairs, first(), rows_ref, len_ref, dcot_ref, grad_ref, dist_ref, *sc)
    V = pl.BlockSpec(memory_space=pltpu.VMEM); S = pl.BlockSpec(memory_space=pltpu.SMEM)
    return pl.pallas_call(k, out_shape=(jax.ShapeDtypeStruct((pairs * SLOT, D), f32), jax.ShapeDtypeStruct((pairs,), f32)),
        in_specs=[V, S, S], out_specs=(V, S), scratch_shapes=scratch(pairs), interpret=interpret,
        compiler_params=pltpu.CompilerParams(vmem_limit_bytes=60 * 2**20))(rows, lengths, dcot)


def layer_norm(hidden, gain, shift):
    center = hidden - jnp.mean(hidden, -1, keepdims=True)
    scaled = center * lax.rsqrt(jnp.mean(center * center, -1, keepdims=True) + EPS)
    return scaled * gain + shift


def outer_rows(left_in, right_in):
    return lax.dot_general(left_in, right_in, (((0,), (0,)), ((), ())), preferred_element_type=jnp.float32)


def back_dot(grad_in, weight_in):
    return lax.dot_general(grad_in, weight_in, (((1,), (1,)), ((), ())), preferred_element_type=jnp.float32)


def on_device(ndp, tokens, cotangent, distance_cot, lengths, w_qkv, q_bias, v_bias, w_out, out_bias, ln1_gain, ln1_bias, w_in, in_bias, w_down, down_bias, ln2_gain, ln2_bias):
    slot_rows = SLOT
    local_pairs = tokens.shape[0] // slot_rows
    local_rows = local_pairs * slot_rows
    reg_index = lax.axis_index("reg")
    score_scale = HEAD_DIM ** (-0.5)
    own_lengths = lax.dynamic_slice_in_dim(lengths, reg_index * local_pairs, local_pairs, 0)
    position = jnp.arange(slot_rows)[None, :]
    key_valid = jnp.where(position < WORDS, position < own_lengths[:, 0:1], position - WORDS < own_lengths[:, 1:2])
    bias_full = jnp.concatenate([q_bias, jnp.zeros_like(q_bias), v_bias])
    packed = (jnp.dot(tokens, w_qkv, preferred_element_type=jnp.float32) + bias_full).astype(jnp.bfloat16)
    split_heads = packed.reshape(local_pairs, slot_rows, 3, HEADS, HEAD_DIM)
    queries = split_heads[:, :, 0]
    keys_all = split_heads[:, :, 1]
    values = split_heads[:, :, 2]

    def make_scores():
        raw_scores = jnp.einsum("pqhd,pkhd->phqk", queries, keys_all, preferred_element_type=jnp.float32) * score_scale
        return jnp.where(key_valid[:, None, None, :], raw_scores, -1e30)

    scores = make_scores()
    row_top = jnp.max(scores, -1, keepdims=True)
    exponent = jnp.exp(scores - row_top)
    row_total = jnp.sum(exponent, -1, keepdims=True)
    probs = exponent / row_total
    log_total = row_top + jnp.log(row_total)
    context = jnp.einsum("phqk,pkhd->pqhd", probs.astype(jnp.bfloat16), values, preferred_element_type=jnp.float32)
    context = context.reshape(local_rows, D).astype(jnp.bfloat16)
    attended = jnp.dot(context, w_out, preferred_element_type=jnp.float32) + out_bias
    first_sum = tokens.astype(jnp.float32) + attended
    normed, first_back = jax.vjp(layer_norm, first_sum, ln1_gain, ln1_bias)
    normed_low = normed.astype(jnp.bfloat16)
    inner = jnp.dot(normed_low, w_in, preferred_element_type=jnp.float32) + in_bias
    activated, gelu_back = jax.vjp(functools.partial(jax.nn.gelu, approximate=False), inner)
    activated_low = activated.astype(jnp.bfloat16)
    branch = jnp.dot(activated_low, w_down, preferred_element_type=jnp.float32) + down_bias
    result, second_back = jax.vjp(layer_norm, normed + branch, ln2_gain, ln2_bias)
    result_low = result.astype(jnp.bfloat16)

    grad_rows, distance = align(result_low, lengths, distance_cot, lambda: lax.axis_index("reg") * local_pairs)

    grad_result = cotangent.astype(jnp.float32) + grad_rows
    grad_second, grad_gain2, grad_shift2 = second_back(grad_result)
    grad_branch = grad_second.astype(jnp.bfloat16)
    grad_w_down = outer_rows(activated_low, grad_branch)
    grad_down_bias = jnp.sum(grad_branch.astype(jnp.float32), 0)
    (grad_inner,) = gelu_back(back_dot(grad_branch, w_down))
    grad_inner = grad_inner.astype(jnp.bfloat16)
    grad_w_in = outer_rows(normed_low, grad_inner)
    grad_in_bias = jnp.sum(grad_inner.astype(jnp.float32), 0)
    grad_normed = grad_second + back_dot(grad_inner, w_in)
    grad_first, grad_gain1, grad_shift1 = first_back(grad_normed)
    grad_attended = grad_first.astype(jnp.bfloat16)
    grad_w_out = outer_rows(context, grad_attended)
    grad_out_bias = jnp.sum(grad_attended.astype(jnp.float32), 0)
    grad_context = back_dot(grad_attended, w_out).astype(jnp.bfloat16).reshape(local_pairs, slot_rows, HEADS, HEAD_DIM)
    probs_again = jnp.exp(make_scores() - log_total)
    grad_probs = jnp.einsum("pqhd,pkhd->phqk", grad_context, values, preferred_element_type=jnp.float32)
    grad_values = jnp.einsum("phqk,pqhd->pkhd", probs_again.astype(jnp.bfloat16), grad_context, preferred_element_type=jnp.float32)
    grad_scores = probs_again * (grad_probs - jnp.sum(grad_probs * probs_again, -1, keepdims=True))
    grad_scores = grad_scores.astype(jnp.bfloat16)
    grad_queries = jnp.einsum("phqk,pkhd->pqhd", grad_scores, keys_all, preferred_element_type=jnp.float32) * score_scale
    grad_keys = jnp.einsum("phqk,pqhd->pkhd", grad_scores, queries, preferred_element_type=jnp.float32) * score_scale
    grad_packed = jnp.stack([grad_queries, grad_keys, grad_values], 2).reshape(local_rows, 3 * D).astype(jnp.bfloat16)
    grad_w_qkv = outer_rows(tokens, grad_packed)
    grad_bias_sum = jnp.sum(grad_packed.astype(jnp.float32), 0)
    grad_tokens = grad_first + back_dot(grad_packed, w_qkv)

    table = pack_table(grad_w_qkv, grad_w_out, grad_w_in, grad_w_down)
    singles = [grad_bias_sum[:D], grad_bias_sum[2 * D :], grad_out_bias, grad_gain1, grad_shift1, grad_down_bias, grad_gain2, grad_shift2]
    small = jnp.concatenate([jnp.stack(singles), grad_in_bias.reshape(4, D), jnp.zeros((4, D), f32)])
    table, small = sum_table(table, small, ndp)
    g_qkv, g_out, g_in, g_down = unpack_table(table)
    return (result_low, distance, grad_tokens, g_qkv, small[0], small[1], g_out, small[2], small[3], small[4],
            g_in, small[8:12].reshape(4 * D), g_down, small[5], small[6], small[7])


def solution(mesh):
    rows = P(("dp", "reg"), None)
    return jax.shard_map(
        functools.partial(on_device, mesh.shape["dp"]),
        mesh=mesh,
        in_specs=(rows, rows, P("dp"), P("dp", None)) + (P(),) * 13,
        out_specs=(rows, P(("dp", "reg")), rows) + (P(),) * 13,
        check_vma=False,
    )
```

```python
import functools
import heapq
import math

import jax
import jax.numpy as jnp
from jax import lax
from jax.experimental import pallas as pl
from jax.experimental.pallas import tpu as pltpu
from jax.sharding import PartitionSpec as P

D = 768
HEADS = 12
HEAD_DIM = 64
WORDS = 64
REGIONS = 128
SLOT = WORDS + REGIONS
ITERS = 50
EPS = 1e-06
f32 = jnp.float32
bf16 = jnp.bfloat16
MESH = pl.DeviceIdType.MESH
VMEM_LIMIT = 62 * 2**20

BLK = 1536
COLS = 256
FFB = 512
NBLK = 18
HALVES = 5
RBLK = BLK - (BLK >> HALVES)
ORDERS = (
    ("c", "x", "y", "z0", "z1"),
    ("c", "y", "x", "z0", "z1"),
    ("c", "z0", "x", "y", "z1"),
    ("c", "x", "y", "z0", "z1"),
    ("c", "y", "x", "z0", "z1"),
    ("c", "z0", "y", "x", "z1"),
)


def order_of(block):
    return ORDERS[block % len(ORDERS)]


def plan(pieces, extra, rate=85e3, core_rate=450e3, delay=1.8):
    free = {}
    arrivals = []
    steps = []
    last = 2 * HALVES + extra - 1
    now = 0.0
    count = 0

    def request(block, step, at):
        nonlocal count
        if block == NBLK:
            name = ("c", "x", "y", "z0", "z1")[step] if step < HALVES else "far"
            sent = 16 * D * 4
        elif step < HALVES:
            name, sent = order_of(block)[step], (BLK >> (step + 1)) * COLS * 2
        elif step < HALVES + extra:
            name, sent = "far", (BLK >> HALVES) * COLS * 2
        else:
            name, sent = order_of(block)[last - step], (BLK >> (last - step + 1)) * COLS * 2
        line = "z" if name in ("z0", "z1") else name
        took = sent / core_rate if name == "c" else 2 * sent / rate
        begin = max(at, free.get(line, 0.0))
        free[line] = begin + took
        heapq.heappush(arrivals, (begin + took * (2 if name == "z1" else 1) + delay, count, block, step))
        count += 1

    index = 0
    while index < len(pieces) or arrivals:
        if arrivals and (arrivals[0][0] <= now or index == len(pieces)):
            at, _, block, step = heapq.heappop(arrivals)
            now = max(now, at) + 0.05
            if block < NBLK and step < HALVES:
                now += 0.35 / 2**step
            steps.append((block, step, now))
            if step < (HALVES + extra - 1 if block == NBLK else last):
                request(block, step + 1, now)
        else:
            took, block = pieces[index]
            now += took
            steps.append((-1, index, now))
            if block is not None:
                request(block, 0, now)
            index += 1
    return steps


def mesh_partners(ndp):
    dp = lax.axis_index("dp")
    reg = lax.axis_index("reg")
    names = [("c", "reg", 1), ("x", "reg", 2), ("y", "dp", 1), ("z0", "dp", 2), ("z1", "dp", 4)]
    step = 8
    while step < ndp:
        names.append(("far%d" % step, "dp", step))
        step *= 2
    partners = {}
    for name, axis, step in names:
        at = reg if axis == "reg" else dp
        bit = lax.rem(at // step, 2)
        other = at + step - 2 * step * bit
        partners[name] = (bit, (dp, other) if axis == "reg" else (other, reg))
    return partners


class Exchange:
    def __init__(self, ndp, table, full, landing, far, small, small_in, sems):
        self.partners = mesh_partners(ndp)
        self.fars = [name for name in self.partners if name.startswith("far")]
        self.extra = len(self.fars)
        self.table, self.full, self.landing, self.far = table, full, landing, far
        self.small, self.small_in = small, small_in
        self.rs_send, self.rs_recv, self.ag_send, self.ag_recv, self.far_send, self.far_recv, self.sm_send, self.sm_recv, self.own = sems

    def barrier(self):
        bar = pltpu.get_barrier_semaphore()
        for _, who in self.partners.values():
            pl.semaphore_signal(bar, inc=1, device_id=who, device_id_type=MESH)
        pl.semaphore_wait(bar, len(self.partners))

    def offset(self, block, steps):
        at, size = block * BLK, BLK
        for step in range(steps):
            size //= 2
            at = at + self.partners[order_of(block)[step]][0] * size
        return pl.multiple_of(at, 16) if steps else at

    def halving(self, block, step):
        bit, who = self.partners[order_of(block)[step]]
        size = BLK >> (step + 1)
        src = pl.multiple_of(self.offset(block, step) + (1 - bit) * size, 16)
        land = block * RBLK + (BLK - (BLK >> step))
        return pltpu.make_async_remote_copy(
            self.table.at[pl.ds(src, size)],
            self.landing.at[pl.ds(land, size)],
            self.rs_send.at[block, step],
            self.rs_recv.at[block, step],
            device_id=who,
            device_id_type=MESH,
        )

    def far_step(self, block, index):
        _, who = self.partners[self.fars[index]]
        size = BLK >> HALVES
        src = self.offset(block, HALVES)
        return pltpu.make_async_remote_copy(
            self.table.at[pl.ds(src, size)],
            self.far.at[block, index],
            self.far_send.at[block, index],
            self.far_recv.at[block, index],
            device_id=who,
            device_id_type=MESH,
        )

    def returning(self, block, step):
        _, who = self.partners[order_of(block)[step]]
        size = BLK >> (step + 1)
        src = self.offset(block, step + 1)
        held = self.table if step + 1 == HALVES else self.full
        return pltpu.make_async_remote_copy(
            held.at[pl.ds(src, size)],
            self.full.at[pl.ds(src, size)],
            self.ag_send.at[block, step],
            self.ag_recv.at[block, step],
            device_id=who,
            device_id_type=MESH,
        )

    def keep(self, block):
        at = pl.ds(self.offset(block, HALVES), BLK >> HALVES)
        return pltpu.make_async_copy(self.table.at[at], self.full.at[at], self.own.at[block])

    def produce(self, block):
        if block == NBLK:
            self.small_copy(0).start()
        else:
            self.halving(block, 0).start()

    def start_after(self, block, event):
        step = event + 1
        if step < HALVES:
            self.halving(block, step).start()
        elif step < HALVES + self.extra:
            self.far_step(block, step - HALVES).start()
        elif step < 2 * HALVES + self.extra:
            back = 2 * HALVES + self.extra - 1 - step
            if back + 1 == HALVES:
                self.keep(block).start()
            self.returning(block, back).start()

    def handle(self, block, event):
        if block == NBLK:
            self.small_handle(event)
            return
        if event < HALVES:
            self.halving(block, event).wait_recv()
            size = BLK >> (event + 1)
            off = self.offset(block, event + 1)
            land = block * RBLK + (BLK - (BLK >> event))
            rows = min(size, 192)

            def add(index, carry):
                at = pl.ds(pl.multiple_of(off + index * rows, 16), rows)
                come = self.landing[pl.ds(pl.multiple_of(land + index * rows, 16), rows), :]
                self.table[at, :] = (self.table[at, :].astype(f32) + come.astype(f32)).astype(bf16)
                return carry

            lax.fori_loop(0, size // rows, add, 0)
        elif event < HALVES + self.extra:
            index = event - HALVES
            copy = self.far_step(block, index)
            copy.wait()
            at = pl.ds(self.offset(block, HALVES), BLK >> HALVES)
            self.table[at, :] = (self.table[at, :].astype(f32) + self.far[block, index].astype(f32)).astype(bf16)
        else:
            back = 2 * HALVES + self.extra - 1 - event
            self.returning(block, back).wait_recv()
            if back + 1 == HALVES:
                self.keep(block).wait()
        self.start_after(block, event)

    def small_copy(self, index):
        _, who = self.partners[list(self.partners)[index]]
        return pltpu.make_async_remote_copy(
            self.small,
            self.small_in.at[index],
            self.sm_send.at[index],
            self.sm_recv.at[index],
            device_id=who,
            device_id_type=MESH,
        )

    def small_handle(self, index):
        self.small_copy(index).wait()
        self.small[...] = self.small[...] + self.small_in[index]
        if index + 1 < len(self.partners):
            self.small_copy(index + 1).start()

    def finish(self):
        for block in range(NBLK):
            for step in range(HALVES):
                self.halving(block, step).wait_send()
                self.returning(block, step).wait_send()


def exchange_scratch(ndp):
    extra = max(int(math.log2(ndp)) - 3, 0)
    count = HALVES + extra
    dma = pltpu.SemaphoreType.DMA
    return [
        pltpu.VMEM((NBLK * RBLK, COLS), bf16),
        pltpu.VMEM((NBLK, max(extra, 1), BLK >> HALVES, COLS), bf16),
        pltpu.VMEM((16, D), f32),
        pltpu.VMEM((count, 16, D), f32),
        dma((NBLK, HALVES)),
        dma((NBLK, HALVES)),
        dma((NBLK, HALVES)),
        dma((NBLK, HALVES)),
        dma((NBLK, max(extra, 1))),
        dma((NBLK, max(extra, 1))),
        dma((count,)),
        dma((count,)),
        dma((NBLK,)),
    ]


def align_body(pairs, first, rows_ref, len_ref, dcot_ref, emit, dist_ref, kern, trans, uhist, ahist, acc, alpha, gamma, cosr):
    P = range(pairs)
    eye = lax.broadcasted_iota(jnp.int32, (REGIONS, REGIONS), 0) == lax.broadcasted_iota(jnp.int32, (REGIONS, REGIONS), 1)
    wcol = lax.broadcasted_iota(jnp.int32, (WORDS, 1), 0)
    rrow = lax.broadcasted_iota(jnp.int32, (1, REGIONS), 1)
    nlen = [len_ref[first + p, 0] for p in P]
    mlen = [len_ref[first + p, 1] for p in P]
    nf = [v.astype(f32) for v in nlen]
    mf = [v.astype(f32) for v in mlen]
    dc = [dcot_ref[first + p] for p in P]
    wv = [(wcol < nlen[p]).astype(f32) for p in P]
    rv = [(rrow < mlen[p]).astype(f32) for p in P]
    rxs, rys = [], []
    for p in P:
        x = rows_ref[SLOT * p:SLOT * p + WORDS, :]
        y = rows_ref[SLOT * p + WORDS:SLOT * (p + 1), :]
        xf, yf = x.astype(f32), y.astype(f32)
        rx = lax.rsqrt(jnp.sum(xf * xf, -1, keepdims=True) + EPS)
        ry = lax.rsqrt(jnp.sum(yf * yf, -1, keepdims=True) + EPS)
        ryr = jnp.sum(jnp.where(eye, ry, 0.0), 0, keepdims=True)
        rxs.append(rx); rys.append((ry, ryr))
        cos = lax.dot_general(x, y, (((1,), (1,)), ((), ())), preferred_element_type=f32) * rx * ryr
        joint = wv[p] * rv[p]
        cost = (1.0 - cos) * joint
        cosr[p] = cos
        kern[p] = jnp.exp(-2.0 * cost) * joint
        trans[p] = joint
        ahist[0, p] = jnp.broadcast_to(wv[p] / nf[p], (WORDS, REGIONS))
    def fwd(t, _):
        joined = [kern[p] * trans[p] for p in P]
        a = [ahist[t, p] for p in P]
        s = [jnp.sum(joined[p] * a[p], 0, keepdims=True) for p in P]
        b = [rv[p] / (mf[p] * s[p] + (1.0 - rv[p])) for p in P]
        u = [joined[p] * b[p] for p in P]
        w = [jnp.sum(u[p], 1, keepdims=True) for p in P]
        an = [wv[p] / (nf[p] * w[p] + (1.0 - wv[p])) for p in P]
        for p in P:
            uhist[t, p] = u[p]
            ahist[t + 1, p] = jnp.broadcast_to(an[p], (WORDS, REGIONS))
            trans[p] = u[p] * an[p]
        return 0
    lax.fori_loop(0, ITERS, fwd, 0)
    cols = []
    for p in P:
        joint = wv[p] * rv[p]
        cost = (1.0 - cosr[p]) * joint
        tc = trans[p] * cost
        dist_ref[p] = jnp.sum(tc)
        g = tc * dc[p]
        cols.append(jnp.sum(g, 0, keepdims=True))
        alpha[p] = jnp.broadcast_to(jnp.sum(g, 1, keepdims=True), (WORDS, REGIONS))
        gamma[p] = jnp.zeros((WORDS, REGIONS), f32)
        acc[p] = float(ITERS) * g
    def bwd(i, cols):
        t = ITERS - i
        tf = t.astype(f32)
        u = [uhist[t - 1, p] for p in P]
        x = [nf[p] * alpha[p] * ahist[t, p] for p in P]
        y = [mf[p] * ahist[t - 1, p] for p in P]
        beta = [cols[p] - jnp.sum(u[p] * x[p], 0, keepdims=True) for p in P]
        ub = [u[p] * beta[p] for p in P]
        gm = [-y[p] * jnp.sum(ub[p], 1, keepdims=True) for p in P]
        go = [gamma[p] for p in P]
        ac = [acc[p] for p in P]
        for p in P:
            acc[p] = ac[p] - tf * (u[p] * x[p] + y[p] * ub[p])
            alpha[p] = 2.0 * gm[p] - go[p]
            gamma[p] = gm[p]
        return tuple(jnp.zeros_like(c) for c in cols)
    lax.fori_loop(0, ITERS, bwd, tuple(cols))
    for p in P:
        x = rows_ref[SLOT * p:SLOT * p + WORDS, :]
        y = rows_ref[SLOT * p + WORDS:SLOT * (p + 1), :]
        rx = rxs[p]; ry, ryr = rys[p]
        gc = dc[p] * trans[p] - 2.0 * acc[p]
        gcos = gc * cosr[p]
        m = gc * rx * ryr
        hi = m.astype(bf16)
        lo = (m - hi.astype(f32)).astype(bf16)
        nt = (((1,), (0,)), ((), ())); tn = (((0,), (0,)), ((), ()))
        gx = lax.dot_general(hi, y, nt, preferred_element_type=f32) + lax.dot_general(lo, y, nt, preferred_element_type=f32)
        gy = lax.dot_general(hi, x, tn, preferred_element_type=f32) + lax.dot_general(lo, x, tn, preferred_element_type=f32)
        sx = rx * rx * jnp.sum(gcos, 1, keepdims=True)
        sy = ry * ry * jnp.sum(jnp.where(eye, jnp.sum(gcos, 0, keepdims=True), 0.0), 1, keepdims=True)
        emit(pl.ds(SLOT * p, WORDS), sx * x.astype(f32) - gx)
        emit(pl.ds(SLOT * p + WORDS, REGIONS), sy * y.astype(f32) - gy)

def scratch(pairs):
    v = lambda *s: pltpu.VMEM(s, f32)
    W = (WORDS, REGIONS)
    return [v(pairs, *W), v(pairs, *W), v(ITERS, pairs, *W), v(ITERS + 1, pairs, *W), v(pairs, *W), v(pairs, *W), v(pairs, *W), v(pairs, *W)]


def forward_kernel(pairs, *refs):
    (tok_hbm, cot_hbm, wqkv_hbm, wout_hbm, win_hbm, wdown_hbm, len_ref, dcot_ref, qb_ref, vb_ref, ob_ref, g1_ref, b1_ref, ib_ref, db_ref, g2_ref, b2_ref,
     out_hbm, dist_ref, packed_hbm, ctx_hbm, hat1_hbm, low1_hbm, rstd1_hbm, act_hbm, slope_hbm, gsec_hbm, small_ref,
     tok, cot, wqkv, wout, win, wdown, qkvb, packed, ctx, hat1, low1, rstd1, actb, slopeb, hat2, rstd2, outv, gsec, sums,
     in_sem, out_sem, ff_sem, *align_refs) = refs
    rows = pairs * SLOT
    first = lax.axis_index("reg") * pairs
    loads = [
        pltpu.make_async_copy(src, dst, in_sem.at[i])
        for i, (src, dst) in enumerate(((tok_hbm, tok), (wqkv_hbm, wqkv), (wout_hbm, wout), (win_hbm, win), (wdown_hbm, wdown), (cot_hbm, cot)))
    ]
    for load in loads:
        load.start()
    stores = [
        pltpu.make_async_copy(src, dst, out_sem.at[i])
        for i, (src, dst) in enumerate(((packed, packed_hbm), (ctx, ctx_hbm), (hat1, hat1_hbm), (low1, low1_hbm), (rstd1, rstd1_hbm), (outv, out_hbm), (gsec, gsec_hbm)))
    ]
    qkvb[:, 0:D] = qb_ref[...].reshape(1, D)
    qkvb[:, D : 2 * D] = jnp.zeros((1, D), f32)
    qkvb[:, 2 * D :] = vb_ref[...].reshape(1, D)
    sums[...] = jnp.zeros_like(sums)

    loads[0].wait()
    loads[1].wait()

    def project(n, carry):
        cols = pl.ds(pl.multiple_of(n * D, D), D)
        packed[:, cols] = (jnp.dot(tok[...], wqkv[:, cols], preferred_element_type=f32) + qkvb[:, cols]).astype(bf16)
        return carry

    lax.fori_loop(0, 3, project, 0)
    stores[0].start()
    loads[2].wait()

    lane = lax.broadcasted_iota(jnp.int32, (1, 2 * HEAD_DIM), 1)
    left = jnp.where(lane < HEAD_DIM, HEAD_DIM**-0.5, 0.0).astype(bf16)
    right = jnp.where(lane < HEAD_DIM, 0.0, HEAD_DIM**-0.5).astype(bf16)
    slot = lax.broadcasted_iota(jnp.int32, (1, SLOT), 1)
    nt = (((1,), (1,)), ((), ()))

    def attend(p, carry):
        at = pl.ds(pl.multiple_of(p * SLOT, SLOT), SLOT)
        words, regions = len_ref[first + p, 0], len_ref[first + p, 1]
        shut = jnp.where(jnp.where(slot < WORDS, words, regions + WORDS) > slot, 0.0, -1e30)
        for h in range(HEADS // 2):
            c = h * 2 * HEAD_DIM
            q = packed[at, c : c + 128]
            k = packed[at, D + c : D + c + 128]
            v = packed[at, 2 * D + c : 2 * D + c + 128]
            both = jnp.concatenate([q * left, q * right], 0)
            s = lax.dot_general(both, k, nt, preferred_element_type=f32) + shut
            e = jnp.exp(s - jnp.max(s, -1, keepdims=True))
            pr = (e / jnp.sum(e, -1, keepdims=True)).astype(bf16)
            o = jnp.dot(pr, v, preferred_element_type=f32)
            ctx[at, c : c + 128] = jnp.where(lane < HEAD_DIM, o[:SLOT], o[SLOT:]).astype(bf16)
        hidden = tok[at, :].astype(f32) + (jnp.dot(ctx[at, :], wout[...], preferred_element_type=f32) + ob_ref[...].reshape(1, D))
        center = hidden - jnp.mean(hidden, -1, keepdims=True)
        rstd = lax.rsqrt(jnp.mean(center * center, -1, keepdims=True) + EPS)
        hat = center * rstd
        hat1[at, :] = hat
        rstd1[at, :] = jnp.broadcast_to(rstd, (SLOT, 128))
        low1[at, :] = (hat * g1_ref[...].reshape(1, D) + b1_ref[...].reshape(1, D)).astype(bf16)
        return carry

    lax.fori_loop(0, pairs, attend, 0)
    for i in range(1, 5):
        stores[i].start()
    loads[3].wait()
    loads[4].wait()

    count = 4 * D // FFB

    def ff_copies(j, slot_at):
        cols = pl.ds(pl.multiple_of(j * FFB, FFB), FFB)
        return (
            pltpu.make_async_copy(actb.at[slot_at], act_hbm.at[:, cols], ff_sem.at[0, slot_at]),
            pltpu.make_async_copy(slopeb.at[slot_at], slope_hbm.at[:, cols], ff_sem.at[1, slot_at]),
        )

    for j in range(count):
        slot_at = j % 2
        cols = slice(j * FFB, (j + 1) * FFB)
        if j >= 2:
            for copy in ff_copies(j - 2, slot_at):
                copy.wait()

        def part(m, carry):
            at = pl.ds(pl.multiple_of(m * SLOT, SLOT), SLOT)
            inner = jnp.dot(low1[at, :], win[:, cols], preferred_element_type=f32) + ib_ref[cols].reshape(1, FFB)
            cdf = 0.5 + 0.5 * lax.erf(inner * (2.0**-0.5))
            actb[slot_at, at, :] = (inner * cdf).astype(bf16)
            slopeb[slot_at, at, :] = (cdf + inner * (jnp.exp(inner * inner * -0.5) * ((2.0 * math.pi) ** -0.5))).astype(bf16)
            return carry

        lax.fori_loop(0, pairs, part, 0)
        for copy in ff_copies(j, slot_at):
            copy.start()
        more = jnp.dot(actb[slot_at], wdown[cols, :], preferred_element_type=f32)
        if j == 0:
            hat2[...] = more
        else:
            hat2[...] += more

    def second(m, carry):
        at = pl.ds(pl.multiple_of(m * SLOT, SLOT), SLOT)
        normed = hat1[at, :] * g1_ref[...].reshape(1, D) + b1_ref[...].reshape(1, D)
        hidden = normed + (hat2[at, :] + db_ref[...].reshape(1, D))
        center = hidden - jnp.mean(hidden, -1, keepdims=True)
        rstd = lax.rsqrt(jnp.mean(center * center, -1, keepdims=True) + EPS)
        hat = center * rstd
        hat2[at, :] = hat
        rstd2[at, :] = jnp.broadcast_to(rstd, (SLOT, 128))
        outv[at, :] = (hat * g2_ref[...].reshape(1, D) + b2_ref[...].reshape(1, D)).astype(bf16)
        return carry

    lax.fori_loop(0, pairs, second, 0)
    stores[5].start()
    loads[5].wait()

    def fold(x):
        return jnp.sum(x.reshape(x.shape[0] // 8, 8, D), 0)

    def emit(at, grad):
        total = cot[at, :].astype(f32) + grad
        hat = hat2[at, :]
        sums[0] += fold(total * hat)
        sums[1] += fold(total)
        wide = total * g2_ref[...].reshape(1, D)
        mean = jnp.mean(wide, -1, keepdims=True)
        slope = jnp.mean(wide * hat, -1, keepdims=True)
        grad = rstd2[at, 0:1] * (wide - mean - hat * slope)
        gsec[at, :] = grad
        sums[2] += fold(grad.astype(bf16).astype(f32))

    align_body(pairs, first, outv, len_ref, dcot_ref, emit, dist_ref, *align_refs)
    stores[6].start()
    for i in range(3):
        small_ref[i : i + 1, :] = jnp.sum(sums[i], 0, keepdims=True)
    small_ref[3:, :] = jnp.zeros((5, D), f32)
    for j in range(count - 2, count):
        for copy in ff_copies(j, j % 2):
            copy.wait()
    for store in stores:
        store.wait()


def forward(tokens, cotangent, dcot, lengths, w_qkv, q_bias, v_bias, w_out, out_bias, g1, b1, w_in, in_bias, w_down, down_bias, g2, b2):
    rows = tokens.shape[0]
    pairs = rows // SLOT
    anywhere = pl.BlockSpec(memory_space=pl.ANY)
    vmem = pl.BlockSpec(memory_space=pltpu.VMEM)
    smem = pl.BlockSpec(memory_space=pltpu.SMEM)
    S = jax.ShapeDtypeStruct
    V = pltpu.VMEM
    dma = pltpu.SemaphoreType.DMA
    return pl.pallas_call(
        functools.partial(forward_kernel, pairs),
        out_shape=(
            S((rows, D), bf16), S((pairs,), f32), S((rows, 3 * D), bf16), S((rows, D), bf16), S((rows, D), f32), S((rows, D), bf16),
            S((rows, 128), f32), S((rows, 4 * D), bf16), S((rows, 4 * D), bf16), S((rows, D), f32), S((8, D), f32),
        ),
        in_specs=[anywhere] * 6 + [smem] * 2 + [vmem] * 9,
        out_specs=(anywhere, smem) + (anywhere,) * 8 + (vmem,),
        scratch_shapes=[
            V((rows, D), bf16), V((rows, D), bf16), V((D, 3 * D), bf16), V((D, D), bf16), V((D, 4 * D), bf16), V((4 * D, D), bf16), V((1, 3 * D), f32),
            V((rows, 3 * D), bf16), V((rows, D), bf16), V((rows, D), f32), V((rows, D), bf16), V((rows, 128), f32),
            V((2, rows, FFB), bf16), V((2, rows, FFB), bf16), V((rows, D), f32), V((rows, 128), f32), V((rows, D), bf16), V((rows, D), f32), V((3, 8, D), f32),
            dma((6,)), dma((7,)), dma((2, 2)),
        ] + scratch(pairs),
        compiler_params=pltpu.CompilerParams(vmem_limit_bytes=VMEM_LIMIT),
        name="forward",
    )(tokens, cotangent, w_qkv, w_out, w_in, w_down, lengths, dcot, q_bias, v_bias, out_bias, g1, b1, in_bias, down_bias, g2, b2)


def backward_kernel(pairs, ndp, *refs):
    (gsec_hbm, act_hbm, slope_hbm, low1_hbm, hat1_hbm, rstd1_hbm, ctx_hbm, packed_hbm, tok_hbm, wdown_hbm, win_hbm, wout_hbm, wqkv_hbm, len_ref, g1_ref, small2_ref,
     tgrad_hbm, full_hbm, small_out,
     table, total, low, act, slope, wdown, win, gin, lows, hat1, rstd1, packed, wout, wqkv, gatt, gctx, ffs, lns, qs,
     in_sem, ff_sem, out_sem, landing, far, sbuf, sland, *sems) = refs
    first = lax.axis_index("reg") * pairs
    nt = (((1,), (1,)), ((), ()))
    tn = (((0,), (0,)), ((), ()))
    ex = Exchange(ndp, table, full_hbm, landing, far, sbuf, sland, sems)
    count = 4 * D // FFB
    half = BLK // 2
    third = BLK // 3

    def dot(a, b, dims=(((1,), (0,)), ((), ()))):
        return lax.dot_general(a, b, dims, preferred_element_type=f32)

    def fold(x):
        return jnp.sum(x.reshape(x.shape[0] // 8, 8, x.shape[1]), 0)

    def by_pair(body):
        def run(m, carry):
            body(pl.ds(pl.multiple_of(m * SLOT, SLOT), SLOT))
            return carry

        lax.fori_loop(0, pairs, run, 0)

    def ff_loads(j):
        cols = pl.ds(j * FFB, FFB)
        s = j % 2
        parts = ((act_hbm.at[:, cols], act), (slope_hbm.at[:, cols], slope), (wdown_hbm.at[cols, :], wdown), (win_hbm.at[:, cols], win))
        return [pltpu.make_async_copy(src, dst.at[s], ff_sem.at[i, s]) for i, (src, dst) in enumerate(parts)]

    sources = ((gsec_hbm, total), (low1_hbm, lows), (hat1_hbm, hat1), (rstd1_hbm, rstd1), (packed_hbm, packed), (wout_hbm, wout), (wqkv_hbm, wqkv), (ctx_hbm, low), (tok_hbm, lows))
    loads = [pltpu.make_async_copy(src, dst, in_sem.at[i]) for i, (src, dst) in enumerate(sources)]
    loads[0].start()
    for copy in ff_loads(0):
        copy.start()
    loads[1].start()
    ex.barrier()
    for i in range(2, 7):
        loads[i].start()
    for ref in (ffs, lns, qs):
        ref[...] = jnp.zeros_like(ref)
    loads[0].wait()

    def cast_branch(at):
        low[at, :] = total[at, :].astype(bf16)

    by_pair(cast_branch)
    pieces = []

    def piece(took, block=None):
        def add(body):
            pieces.append((took, block, body))
            return body

        return add

    def store_table(block, start, value):
        table[block * BLK + start : block * BLK + start + value.shape[0], :] = value.astype(bf16)

    def ff_pieces(j):
        s = j % 2

        @piece(1.2, 2 * j)
        def down():
            for copy in ff_loads(j):
                copy.wait()
            if j + 1 < count:
                for copy in ff_loads(j + 1):
                    copy.start()
            if j == 0:
                loads[1].wait()
            for c in range(3):
                store_table(2 * j, c * third, dot(act[s], low[:, c * COLS : (c + 1) * COLS], tn))

        @piece(1.3)
        def inner():
            def body(at):
                grad = (dot(low[at, :], wdown[s], nt) * slope[s, at, :].astype(f32)).astype(bf16)
                gin[at, :] = grad
                ffs[j] += fold(grad.astype(f32))

            by_pair(body)

        @piece(1.1, 2 * j + 1)
        def outer():
            for c in range(2):
                store_table(2 * j + 1, c * half, dot(lows[...], gin[:, c * COLS : (c + 1) * COLS], tn))

        @piece(1.1)
        def back():
            total[...] += dot(gin[...], win[s], nt)

    for j in range(count):
        ff_pieces(j)

    @piece(2.0)
    def norm_back():
        loads[7].start()
        loads[8].start()
        loads[2].wait()
        loads[3].wait()
        gain = g1_ref[...].reshape(1, D)

        def body(at):
            grad = total[at, :]
            hat = hat1[at, :]
            wide = grad * gain
            new = rstd1[at, 0:1] * (wide - jnp.mean(wide, -1, keepdims=True) - hat * jnp.mean(wide * hat, -1, keepdims=True))
            total[at, :] = new
            lowered = new.astype(bf16)
            gatt[at, :] = lowered
            for i, value in enumerate((grad * hat, grad, lowered.astype(f32))):
                lns[i] += fold(value)

        by_pair(body)

    base = 2 * count

    def out_piece(c, block):
        @piece(0.6, block)
        def out():
            if c == 0:
                loads[7].wait()
            at = c * half
            store_table(base + at // BLK, at % BLK, dot(low[...], gatt[:, c * COLS : (c + 1) * COLS], tn))

    out_piece(0, None)
    out_piece(1, base)
    out_piece(2, None)

    @piece(1.4)
    def context_back():
        loads[5].wait()
        gctx[...] = dot(gatt[...], wout[...], nt).astype(bf16)

    lane = lax.broadcasted_iota(jnp.int32, (1, 2 * HEAD_DIM), 1)
    scale = HEAD_DIM**-0.5
    left = jnp.where(lane < HEAD_DIM, 1.0, 0.0).astype(bf16)
    right = jnp.where(lane < HEAD_DIM, 0.0, 1.0).astype(bf16)
    slot = lax.broadcasted_iota(jnp.int32, (1, SLOT), 1)

    def pair_piece(p):
        @piece(3.0)
        def attention_back():
            if p == 0:
                loads[4].wait()
            words, regions = len_ref[first + p, 0], len_ref[first + p, 1]
            shut = jnp.where(jnp.where(slot < WORDS, words, regions + WORDS) > slot, 0.0, -1e30)
            at = slice(p * SLOT, (p + 1) * SLOT)

            def heads(h, carry):
                c = pl.multiple_of(h * 128, 128)
                q = packed[at, pl.ds(c, 128)]
                k = packed[at, pl.ds(D + c, 128)]
                v = packed[at, pl.ds(2 * D + c, 128)]
                g = gctx[at, pl.ds(c, 128)]
                both = jnp.concatenate([q * (left * scale).astype(bf16), q * (right * scale).astype(bf16)], 0)
                grads = jnp.concatenate([g * left, g * right], 0)
                s = dot(both, k, nt) + shut
                e = jnp.exp(s - jnp.max(s, -1, keepdims=True))
                pr = e / jnp.sum(e, -1, keepdims=True)
                gp = dot(grads, v, nt)
                gs = (pr * (gp - jnp.sum(pr * gp, -1, keepdims=True))).astype(bf16)
                gq = dot(gs, k)
                gq = jnp.where(lane < HEAD_DIM, gq[:SLOT], gq[SLOT:]) * scale
                gk = dot(gs, both, tn)
                gv = dot(pr.astype(bf16), grads, tn)
                for i, value in enumerate((gq, gk, gv)):
                    value = value.astype(bf16)
                    packed[at, pl.ds(i * D + c, 128)] = value
                    qs[:, pl.ds(i * D + c, 128)] += fold(value.astype(f32))
                return carry

            lax.fori_loop(0, HEADS // 2, heads, 0)

    for p in range(pairs):
        pair_piece(p)

    @piece(0.5, NBLK)
    def singles():
        def row(i, value):
            sbuf[i : i + 1, :] = value

        def down(x):
            return jnp.sum(x, 0, keepdims=True)

        row(0, down(qs[:, 0:D]))
        row(1, down(qs[:, 2 * D : 3 * D]))
        row(2, down(lns[2]))
        row(3, down(lns[0]))
        row(4, down(lns[1]))
        row(5, small2_ref[2:3, :])
        row(6, small2_ref[0:1, :])
        row(7, small2_ref[1:2, :])
        for j in range(count):
            at = j * FFB
            value = down(ffs[j])
            while value.shape[1]:
                room = min(D - at % D, value.shape[1])
                sbuf[8 + at // D : 9 + at // D, at % D : at % D + room] = value[:, :room]
                at, value = at + room, value[:, room:]
        sbuf[12:16, :] = jnp.zeros((4, D), f32)

    def qkv_piece(c, block):
        @piece(0.6, block)
        def qkv():
            if c == 0:
                loads[8].wait()
            at = (3 + c) * half
            store_table(base + at // BLK, at % BLK, dot(lows[...], packed[:, c * COLS : (c + 1) * COLS], tn))

    for c in range(9):
        qkv_piece(c, base + (3 + c) // 2 if (3 + c) % 2 else None)

    done = []

    def token_piece(c):
        @piece(1.1)
        def tokens_back():
            if c == 0:
                loads[6].wait()
            cols = slice(c * D, (c + 1) * D)
            total[...] += dot(packed[:, cols], wqkv[:, cols], nt)
            if c == 2:
                pltpu.make_async_copy(total, tgrad_hbm, out_sem).start()

    for c in range(3):
        token_piece(c)

    for block, step, _ in plan([(took, block) for took, block, _ in pieces], ex.extra):
        if block < 0:
            _, made, body = pieces[step]
            body()
            if made is not None:
                ex.produce(made)
        else:
            ex.handle(block, step)
    small_out[...] = sbuf[...]
    ex.finish()
    pltpu.make_async_copy(total, tgrad_hbm, out_sem).wait()


def backward(ndp, gsec, act, slope, low1, hat1, rstd1, ctx, packed, tokens, w_down, w_in, w_out, w_qkv, lengths, g1, small2):
    rows = tokens.shape[0]
    pairs = rows // SLOT
    anywhere = pl.BlockSpec(memory_space=pl.ANY)
    vmem = pl.BlockSpec(memory_space=pltpu.VMEM)
    smem = pl.BlockSpec(memory_space=pltpu.SMEM)
    S = jax.ShapeDtypeStruct
    V = pltpu.VMEM
    dma = pltpu.SemaphoreType.DMA
    return pl.pallas_call(
        functools.partial(backward_kernel, pairs, ndp),
        out_shape=(S((rows, D), f32), S((NBLK * BLK, COLS), bf16), S((16, D), f32)),
        in_specs=[anywhere] * 13 + [smem] + [vmem] * 2,
        out_specs=(anywhere, anywhere, vmem),
        scratch_shapes=[
            V((NBLK * BLK, COLS), bf16), V((rows, D), f32), V((rows, D), bf16), V((2, rows, FFB), bf16), V((2, rows, FFB), bf16), V((2, FFB, D), bf16), V((2, D, FFB), bf16),
            V((rows, FFB), bf16), V((rows, D), bf16), V((rows, D), f32), V((rows, 128), f32), V((rows, 3 * D), bf16), V((D, D), bf16), V((D, 3 * D), bf16),
            V((rows, D), bf16), V((rows, D), bf16), V((4 * D // FFB, 8, FFB), f32), V((3, 8, D), f32), V((8, 3 * D), f32),
            dma((9,)), dma((4, 2)), dma,
        ] + exchange_scratch(ndp),
        compiler_params=pltpu.CompilerParams(collective_id=1, has_side_effects=True, vmem_limit_bytes=VMEM_LIMIT),
        name="backward",
    )(gsec, act, slope, low1, hat1, rstd1, ctx, packed, tokens, w_down, w_in, w_out, w_qkv, lengths, g1, small2)


def widen_units():
    units = []
    for j in range(6):
        for r in range(0, 512, 256):
            units.append((3, 512 * j + r, 256, [(2 * j * BLK + 512 * c + r, c) for c in range(3)]))
    for r in range(0, D, 64):
        units.append((2, r, 64, [((2 * (c // 2) + 1) * BLK + D * (c % 2) + r, c) for c in range(12)]))
    for r in range(0, D, 256):
        units.append((1, r, 256, [(12 * BLK + D * c + r, c) for c in range(3)]))
    for r in range(0, D, 96):
        units.append((0, r, 96, [(12 * BLK + D * (3 + c) + r, c) for c in range(9)]))
    return units


def widen_kernel(depth, table, qkv, out, w_in, down, *refs):
    outs = (qkv, out, w_in, down)
    units = widen_units()
    narrow, wide, in_sem, out_sem = refs[0:4], refs[4:8], refs[8], refs[9]

    def ins(u):
        which, row, rows, pieces = units[u]
        return [
            pltpu.make_async_copy(table.at[pl.ds(src, rows)], narrow[which].at[u % depth, :, pl.ds(c * COLS, COLS)], in_sem.at[u % depth, c])
            for src, c in pieces
        ]

    def back(u):
        which, row, rows, _ = units[u]
        return pltpu.make_async_copy(wide[which].at[u % depth], outs[which].at[pl.ds(row, rows)], out_sem.at[u % depth])

    for u in range(len(units) + depth - 1):
        if u < len(units):
            for copy in ins(u):
                copy.start()
        v = u - (depth - 1)
        if v >= 0:
            for copy in ins(v):
                copy.wait()
            if v >= depth:
                back(v - depth).wait()
            which = units[v][0]
            wide[which][v % depth] = narrow[which][v % depth].astype(f32)
            back(v).start()
    for v in range(len(units) - depth, len(units)):
        back(v).wait()


def unpack_table(table):
    anywhere = pl.BlockSpec(memory_space=pl.ANY)
    depth = 4
    shapes = ((96, 3 * D), (256, D), (64, 4 * D), (256, D))
    S = jax.ShapeDtypeStruct
    dma = pltpu.SemaphoreType.DMA
    return pl.pallas_call(
        functools.partial(widen_kernel, depth),
        out_shape=(S((D, 3 * D), f32), S((D, D), f32), S((D, 4 * D), f32), S((4 * D, D), f32)),
        in_specs=[anywhere],
        out_specs=(anywhere,) * 4,
        scratch_shapes=[pltpu.VMEM((depth, *s), bf16) for s in shapes] + [pltpu.VMEM((depth, *s), f32) for s in shapes] + [dma((depth, 12)), dma((depth,))],
        compiler_params=pltpu.CompilerParams(vmem_limit_bytes=VMEM_LIMIT),
        name="widen",
    )(table)


def on_device(ndp, tokens, cotangent, distance_cot, lengths, w_qkv, q_bias, v_bias, w_out, out_bias, ln1_gain, ln1_bias, w_in, in_bias, w_down, down_bias, ln2_gain, ln2_bias):
    result, distance, packed, ctx, hat1, low1, rstd1, act, slope, gsec, small2 = forward(
        tokens, cotangent, distance_cot, lengths, w_qkv, q_bias, v_bias, w_out, out_bias, ln1_gain, ln1_bias, w_in, in_bias, w_down, down_bias, ln2_gain, ln2_bias
    )
    grad_tokens, table, small = backward(ndp, gsec, act, slope, low1, hat1, rstd1, ctx, packed, tokens, w_down, w_in, w_out, w_qkv, lengths, ln1_gain, small2)
    g_qkv, g_out, g_in, g_down = unpack_table(table)
    return (result, distance, grad_tokens, g_qkv, small[0], small[1], g_out, small[2], small[3], small[4],
            g_in, small[8:12].reshape(4 * D), g_down, small[5], small[6], small[7])


def solution(mesh):
    rows = P(("dp", "reg"), None)
    return jax.shard_map(
        functools.partial(on_device, mesh.shape["dp"]),
        mesh=mesh,
        in_specs=(rows, rows, P("dp"), P("dp", None)) + (P(),) * 13,
        out_specs=(rows, P(("dp", "reg")), rows) + (P(),) * 13,
        check_vma=False,
    )
```

```python
import functools
import heapq
import itertools
import math

import jax
import jax.numpy as jnp
from jax import lax
from jax.experimental import pallas as pl
from jax.experimental.pallas import tpu as pltpu
from jax.sharding import PartitionSpec as P

D = 768
HEADS = 12
HEAD_DIM = 64
WORDS = 64
REGIONS = 128
SLOT = WORDS + REGIONS
ITERS = 50
EPS = 1e-06
f32 = jnp.float32
bf16 = jnp.bfloat16
MESH = pl.DeviceIdType.MESH
VMEM_LIMIT = 62 * 2**20

BLK = 1536
COLS = 128
FFB = 512
NBLK = 36
HALVES = 5
RBLK = BLK - (BLK >> HALVES)
ORDERS = (
    ("c", "x", "y", "z0", "z1"),
    ("c", "y", "x", "z0", "z1"),
    ("c", "z0", "x", "y", "z1"),
    ("c", "z0", "y", "x", "z1"),
    ("c", "x", "z0", "y", "z1"),
    ("c", "y", "z0", "x", "z1"),
    ("c", "z0", "z1", "x", "y"),
    ("c", "z0", "z1", "y", "x"),
)
TAKES = (5, 4, 0, 5, 4, 1, 4, 4, 1, 3, 1, 0, 1, 5, 2, 0, 5, 0, 1, 5, 0, 1, 0, 0, 0, 0, 2, 1, 5, 0, 3, 3, 3, 5, 4, 4)


def order_of(block):
    return ORDERS[TAKES[block]]


def plan(pieces, extra, rate=80e3, core_rate=450e3, delay=2.4, ahead=3.0, add=0.075):
    last = 2 * HALVES + extra - 1
    block_bytes = BLK * COLS * 2
    lines = ("c", "x", "y", "z", "far")
    free = dict.fromkeys(lines, 0.0)
    waiting = {line: [] for line in lines}
    arrivals = []
    steps = []
    ticket = itertools.count()
    now = 0.0

    def facts(block, step):
        if block == NBLK:
            return ("c", "x", "y", "z0", "z1")[step] if step < HALVES else "far", 16 * D * 4
        if step < HALVES:
            return order_of(block)[step], block_bytes >> (step + 1)
        if step < HALVES + extra:
            return "far", block_bytes >> HALVES
        return order_of(block)[last - step], block_bytes >> (last - step + 1)

    def ask(block, step):
        name = facts(block, step)[0]
        line = "z" if name in ("z0", "z1") else name
        heapq.heappush(waiting[line], (step >= HALVES and block < NBLK, next(ticket), block, step))

    index = 0
    while index < len(pieces) or arrivals or any(waiting.values()):
        if arrivals and (arrivals[0][0] <= now or index == len(pieces)):
            at, _, block, step = heapq.heappop(arrivals)
            now = max(now, at) + 0.05
            if block < NBLK and step < HALVES:
                now += add / 2**step
            steps.append(("handle", block, step, now))
            if step < (HALVES + extra - 1 if block == NBLK else last):
                ask(block, step + 1)
        else:
            took, made = pieces[index]
            now += took
            steps.append(("piece", index, 0, now))
            for block in made:
                ask(block, 0)
            index += 1
        for line, queue in waiting.items():
            while queue and free[line] - now < ahead:
                _, _, block, step = heapq.heappop(queue)
                name, sent = facts(block, step)
                took = sent / core_rate if name == "c" else 2 * sent / rate
                free[line] = max(now, free[line]) + took
                heapq.heappush(arrivals, (free[line] + (took if name == "z1" else 0.0) + delay, next(ticket), block, step))
                steps.append(("start", block, step, now))
    return steps


def mesh_partners(ndp):
    dp = lax.axis_index("dp")
    reg = lax.axis_index("reg")
    names = [("c", "reg", 1), ("x", "reg", 2), ("y", "dp", 1), ("z0", "dp", 2), ("z1", "dp", 4)]
    step = 8
    while step < ndp:
        names.append(("far%d" % step, "dp", step))
        step *= 2
    partners = {}
    for name, axis, step in names:
        at = reg if axis == "reg" else dp
        bit = lax.rem(at // step, 2)
        other = at + step - 2 * step * bit
        partners[name] = (bit, (dp, other) if axis == "reg" else (other, reg))
    return partners


class Exchange:
    def __init__(self, ndp, table, full, landing, far, small, small_in, sems):
        self.partners = mesh_partners(ndp)
        self.fars = [name for name in self.partners if name.startswith("far")]
        self.extra = len(self.fars)
        self.table, self.full, self.landing, self.far = table, full, landing, far
        self.small, self.small_in = small, small_in
        self.rs_send, self.rs_recv, self.ag_send, self.ag_recv, self.far_send, self.far_recv, self.sm_send, self.sm_recv, self.own = sems

    def barrier(self):
        bar = pltpu.get_barrier_semaphore()
        for _, who in self.partners.values():
            pl.semaphore_signal(bar, inc=1, device_id=who, device_id_type=MESH)
        pl.semaphore_wait(bar, len(self.partners))

    def offset(self, block, steps):
        at, size = block * BLK, BLK
        for step in range(steps):
            size //= 2
            at = at + self.partners[order_of(block)[step]][0] * size
        return pl.multiple_of(at, 16) if steps else at

    def halving(self, block, step):
        bit, who = self.partners[order_of(block)[step]]
        size = BLK >> (step + 1)
        src = pl.multiple_of(self.offset(block, step) + (1 - bit) * size, 16)
        land = block * RBLK + (BLK - (BLK >> step))
        return pltpu.make_async_remote_copy(
            self.table.at[pl.ds(src, size)],
            self.landing.at[pl.ds(land, size)],
            self.rs_send.at[block, step],
            self.rs_recv.at[block, step],
            device_id=who,
            device_id_type=MESH,
        )

    def far_step(self, block, index):
        _, who = self.partners[self.fars[index]]
        size = BLK >> HALVES
        src = self.offset(block, HALVES)
        return pltpu.make_async_remote_copy(
            self.table.at[pl.ds(src, size)],
            self.far.at[block, index],
            self.far_send.at[block, index],
            self.far_recv.at[block, index],
            device_id=who,
            device_id_type=MESH,
        )

    def returning(self, block, step):
        _, who = self.partners[order_of(block)[step]]
        size = BLK >> (step + 1)
        src = self.offset(block, step + 1)
        held = self.table if step + 1 == HALVES else self.full
        return pltpu.make_async_remote_copy(
            held.at[pl.ds(src, size)],
            self.full.at[pl.ds(src, size)],
            self.ag_send.at[block, step],
            self.ag_recv.at[block, step],
            device_id=who,
            device_id_type=MESH,
        )

    def keep(self, block):
        at = pl.ds(self.offset(block, HALVES), BLK >> HALVES)
        return pltpu.make_async_copy(self.table.at[at], self.full.at[at], self.own.at[block])

    def start(self, block, step):
        if block == NBLK:
            self.small_copy(step).start()
        elif step < HALVES:
            self.halving(block, step).start()
        elif step < HALVES + self.extra:
            self.far_step(block, step - HALVES).start()
        else:
            back = 2 * HALVES + self.extra - 1 - step
            if back + 1 == HALVES:
                self.keep(block).start()
            self.returning(block, back).start()

    def handle(self, block, event):
        if block == NBLK:
            self.small_handle(event)
            return
        if event < HALVES:
            self.halving(block, event).wait_recv()
            size = BLK >> (event + 1)
            off = self.offset(block, event + 1)
            land = block * RBLK + (BLK - (BLK >> event))
            rows = min(size, 192)

            def add(index, carry):
                at = pl.ds(pl.multiple_of(off + index * rows, 16), rows)
                self.table[at, :] += self.landing[pl.ds(pl.multiple_of(land + index * rows, 16), rows), :]
                return carry

            lax.fori_loop(0, size // rows, add, 0)
        elif event < HALVES + self.extra:
            index = event - HALVES
            copy = self.far_step(block, index)
            copy.wait()
            at = pl.ds(self.offset(block, HALVES), BLK >> HALVES)
            self.table[at, :] += self.far[block, index]
        else:
            back = 2 * HALVES + self.extra - 1 - event
            self.returning(block, back).wait_recv()
            if back + 1 == HALVES:
                self.keep(block).wait()

    def small_copy(self, index):
        _, who = self.partners[list(self.partners)[index]]
        return pltpu.make_async_remote_copy(
            self.small,
            self.small_in.at[index],
            self.sm_send.at[index],
            self.sm_recv.at[index],
            device_id=who,
            device_id_type=MESH,
        )

    def small_handle(self, index):
        self.small_copy(index).wait()
        self.small[...] = self.small[...] + self.small_in[index]

    def finish(self):
        for block in range(NBLK):
            for step in range(HALVES):
                self.halving(block, step).wait_send()
                self.returning(block, step).wait_send()


def exchange_scratch(ndp):
    extra = max(int(math.log2(ndp)) - 3, 0)
    count = HALVES + extra
    dma = pltpu.SemaphoreType.DMA
    return [
        pltpu.VMEM((NBLK * RBLK, COLS), bf16),
        pltpu.VMEM((NBLK, max(extra, 1), BLK >> HALVES, COLS), bf16),
        pltpu.VMEM((16, D), f32),
        pltpu.VMEM((count, 16, D), f32),
        dma((NBLK, HALVES)),
        dma((NBLK, HALVES)),
        dma((NBLK, HALVES)),
        dma((NBLK, HALVES)),
        dma((NBLK, max(extra, 1))),
        dma((NBLK, max(extra, 1))),
        dma((count,)),
        dma((count,)),
        dma((NBLK,)),
    ]


def align_body(pairs, first, rows_ref, len_ref, dcot_ref, emit, dist_ref, kern, trans, uhist, acur, acc, alpha, gamma, cosr):
    P = range(pairs)
    eye = lax.broadcasted_iota(jnp.int32, (REGIONS, REGIONS), 0) == lax.broadcasted_iota(jnp.int32, (REGIONS, REGIONS), 1)
    wcol = lax.broadcasted_iota(jnp.int32, (WORDS, 1), 0)
    rrow = lax.broadcasted_iota(jnp.int32, (1, REGIONS), 1)
    nlen = [len_ref[0, first + p] for p in P]
    mlen = [len_ref[1, first + p] for p in P]
    nf = [v.astype(f32) for v in nlen]
    mf = [v.astype(f32) for v in mlen]
    dc = [dcot_ref[first + p] for p in P]
    wv = [(wcol < nlen[p]).astype(f32) for p in P]
    rv = [(rrow < mlen[p]).astype(f32) for p in P]
    rxs, rys = [], []
    for p in P:
        x = rows_ref[SLOT * p:SLOT * p + WORDS, :]
        y = rows_ref[SLOT * p + WORDS:SLOT * (p + 1), :]
        xf, yf = x.astype(f32), y.astype(f32)
        rx = lax.rsqrt(jnp.sum(xf * xf, -1, keepdims=True) + EPS)
        ry = lax.rsqrt(jnp.sum(yf * yf, -1, keepdims=True) + EPS)
        ryr = jnp.sum(jnp.where(eye, ry, 0.0), 0, keepdims=True)
        rxs.append(rx); rys.append((ry, ryr))
        cos = lax.dot_general(x, y, (((1,), (1,)), ((), ())), preferred_element_type=f32) * rx * ryr
        joint = wv[p] * rv[p]
        cost = (1.0 - cos) * joint
        cosr[p] = cos
        kern[p] = jnp.exp(-2.0 * cost) * joint
        trans[p] = joint
        acur[p] = jnp.broadcast_to(wv[p] / nf[p], (WORDS, REGIONS))
        uhist[0, p] = jnp.where(rrow == 0, wv[p], 0.0)
    def fwd(t, _):
        joined = [kern[p] * trans[p] for p in P]
        a = [acur[p] for p in P]
        s = [jnp.sum(joined[p] * a[p], 0, keepdims=True) for p in P]
        b = [rv[p] / (mf[p] * s[p] + (1.0 - rv[p])) for p in P]
        u = [joined[p] * b[p] for p in P]
        w = [jnp.sum(u[p], 1, keepdims=True) for p in P]
        an = [wv[p] / (nf[p] * w[p] + (1.0 - wv[p])) for p in P]
        for p in P:
            uhist[t + 1, p] = u[p]
            acur[p] = jnp.broadcast_to(an[p], (WORDS, REGIONS))
            trans[p] = u[p] * an[p]
        return 0
    lax.fori_loop(0, ITERS, fwd, 0)
    cols = []
    for p in P:
        joint = wv[p] * rv[p]
        cost = (1.0 - cosr[p]) * joint
        tc = trans[p] * cost
        dist_ref[p] = jnp.sum(tc)
        g = tc * dc[p]
        cols.append(jnp.sum(g, 0, keepdims=True))
        alpha[p] = jnp.broadcast_to(jnp.sum(g, 1, keepdims=True), (WORDS, REGIONS))
        gamma[p] = jnp.zeros((WORDS, REGIONS), f32)
        acc[p] = float(ITERS) * g
    def bwd(i, cols):
        t = ITERS - i
        tf = t.astype(f32)
        u = [uhist[t, p] for p in P]
        before = [uhist[t - 1, p] for p in P]
        x = [nf[p] * alpha[p] * acur[p] for p in P]
        ap = [wv[p] / (nf[p] * jnp.sum(before[p], 1, keepdims=True) + (1.0 - wv[p])) for p in P]
        y = [mf[p] * ap[p] for p in P]
        beta = [cols[p] - jnp.sum(u[p] * x[p], 0, keepdims=True) for p in P]
        ub = [u[p] * beta[p] for p in P]
        gm = [jnp.broadcast_to(-y[p] * jnp.sum(ub[p], 1, keepdims=True), (WORDS, REGIONS)) for p in P]
        go = [gamma[p] for p in P]
        ac = [acc[p] for p in P]
        for p in P:
            acc[p] = ac[p] - tf * (u[p] * x[p] + y[p] * ub[p])
            alpha[p] = 2.0 * gm[p] - go[p]
            gamma[p] = gm[p]
            acur[p] = jnp.broadcast_to(ap[p], (WORDS, REGIONS))
        return tuple(jnp.zeros_like(c) for c in cols)
    lax.fori_loop(0, ITERS, bwd, tuple(cols))
    for p in P:
        x = rows_ref[SLOT * p:SLOT * p + WORDS, :]
        y = rows_ref[SLOT * p + WORDS:SLOT * (p + 1), :]
        rx = rxs[p]; ry, ryr = rys[p]
        gc = dc[p] * trans[p] - 2.0 * acc[p]
        gcos = gc * cosr[p]
        m = gc * rx * ryr
        hi = m.astype(bf16)
        lo = (m - hi.astype(f32)).astype(bf16)
        nt = (((1,), (0,)), ((), ())); tn = (((0,), (0,)), ((), ()))
        gx = lax.dot_general(hi, y, nt, preferred_element_type=f32) + lax.dot_general(lo, y, nt, preferred_element_type=f32)
        gy = lax.dot_general(hi, x, tn, preferred_element_type=f32) + lax.dot_general(lo, x, tn, preferred_element_type=f32)
        sx = rx * rx * jnp.sum(gcos, 1, keepdims=True)
        sy = ry * ry * jnp.sum(jnp.where(eye, jnp.sum(gcos, 0, keepdims=True), 0.0), 1, keepdims=True)
        emit(p, pl.ds(SLOT * p, WORDS), sx * x.astype(f32) - gx)
        emit(p, pl.ds(SLOT * p + WORDS, REGIONS), sy * y.astype(f32) - gy)

def scratch(pairs):
    v = lambda *s: pltpu.VMEM(s, f32)
    W = (WORDS, REGIONS)
    return [v(pairs, *W), v(pairs, *W), v(ITERS + 1, pairs, *W), v(pairs, *W), v(pairs, *W), v(pairs, *W), v(pairs, *W), v(pairs, *W)]


def forward_kernel(pairs, *refs):
    (tok_hbm, cot_hbm, wqkv_hbm, wout_hbm, win_hbm, wdown_hbm, len_ref, dcot_ref, qb_ref, vb_ref, ob_ref, g1_ref, b1_ref, ib_ref, db_ref, g2_ref, b2_ref,
     out_hbm, dist_ref, packed_hbm, ctx_hbm, hat1_hbm, low1_hbm, rstd1_hbm, act_hbm, slope_hbm, gsec_hbm, small_ref,
     tok, cot, wqkv, wout, win, wdown, qkvb, packed, ctx, hat1, low1, rstd1, actb, slopeb, hat2, rstd2, outv, gsec, sums,
     in_sem, out_sem, ff_sem, pair_sem, *align_refs) = refs
    rows = pairs * SLOT
    first = lax.axis_index("reg") * pairs
    loads = [
        pltpu.make_async_copy(src, dst, in_sem.at[i])
        for i, (src, dst) in enumerate(((tok_hbm, tok), (wqkv_hbm, wqkv), (wout_hbm, wout), (win_hbm, win), (wdown_hbm, wdown), (cot_hbm, cot)))
    ]
    loads[0].start()
    loads[1].start()
    stores = [
        pltpu.make_async_copy(src, dst, out_sem.at[i])
        for i, (src, dst) in enumerate(((packed, packed_hbm), (ctx, ctx_hbm), (hat1, hat1_hbm), (low1, low1_hbm), (rstd1, rstd1_hbm), (outv, out_hbm)))
    ]
    qkvb[:, 0:D] = qb_ref[...].reshape(1, D)
    qkvb[:, D : 2 * D] = jnp.zeros((1, D), f32)
    qkvb[:, 2 * D :] = vb_ref[...].reshape(1, D)
    sums[...] = jnp.zeros_like(sums)

    loads[0].wait()
    loads[1].wait()
    for load in loads[2:]:
        load.start()

    def project(n, carry):
        cols = pl.ds(pl.multiple_of(n * D, D), D)
        packed[:, cols] = (jnp.dot(tok[...], wqkv[:, cols], preferred_element_type=f32) + qkvb[:, cols]).astype(bf16)
        return carry

    lax.fori_loop(0, 3, project, 0)
    stores[0].start()
    loads[2].wait()

    lane = lax.broadcasted_iota(jnp.int32, (1, 2 * HEAD_DIM), 1)
    left = jnp.where(lane < HEAD_DIM, HEAD_DIM**-0.5, 0.0).astype(bf16)
    right = jnp.where(lane < HEAD_DIM, 0.0, HEAD_DIM**-0.5).astype(bf16)
    slot = lax.broadcasted_iota(jnp.int32, (1, SLOT), 1)
    nt = (((1,), (1,)), ((), ()))

    def attend(p, carry):
        at = pl.ds(pl.multiple_of(p * SLOT, SLOT), SLOT)
        words, regions = len_ref[0, first + p], len_ref[1, first + p]
        shut = jnp.where(jnp.where(slot < WORDS, words, regions + WORDS) > slot, 0.0, -1e30)
        for h in range(HEADS // 2):
            c = h * 2 * HEAD_DIM
            q = packed[at, c : c + 128]
            k = packed[at, D + c : D + c + 128]
            v = packed[at, 2 * D + c : 2 * D + c + 128]
            both = jnp.concatenate([q * left, q * right], 0)
            s = lax.dot_general(both, k, nt, preferred_element_type=f32) + shut
            e = jnp.exp(s - jnp.max(s, -1, keepdims=True))
            pr = (e / jnp.sum(e, -1, keepdims=True)).astype(bf16)
            o = jnp.dot(pr, v, preferred_element_type=f32)
            ctx[at, c : c + 128] = jnp.where(lane < HEAD_DIM, o[:SLOT], o[SLOT:]).astype(bf16)
        return carry

    lax.fori_loop(0, pairs, attend, 0, unroll=True)
    stores[1].start()

    def norm(p, carry):
        at = pl.ds(pl.multiple_of(p * SLOT, SLOT), SLOT)
        hidden = tok[at, :].astype(f32) + (jnp.dot(ctx[at, :], wout[...], preferred_element_type=f32) + ob_ref[...].reshape(1, D))
        center = hidden - jnp.mean(hidden, -1, keepdims=True)
        rstd = lax.rsqrt(jnp.mean(center * center, -1, keepdims=True) + EPS)
        hat = center * rstd
        hat1[at, :] = hat
        rstd1[at, :] = jnp.broadcast_to(rstd, (SLOT, 128))
        low1[at, :] = (hat * g1_ref[...].reshape(1, D) + b1_ref[...].reshape(1, D)).astype(bf16)
        return carry

    lax.fori_loop(0, pairs, norm, 0, unroll=True)
    for i in range(2, 5):
        stores[i].start()
    loads[3].wait()
    loads[4].wait()

    count = 4 * D // FFB

    def ff_copies(j, slot_at):
        cols = pl.ds(pl.multiple_of(j * FFB, FFB), FFB)
        return (
            pltpu.make_async_copy(actb.at[slot_at], act_hbm.at[:, cols], ff_sem.at[0, slot_at]),
            pltpu.make_async_copy(slopeb.at[slot_at], slope_hbm.at[:, cols], ff_sem.at[1, slot_at]),
        )

    for j in range(count):
        slot_at = j
        cols = slice(j * FFB, (j + 1) * FFB)

        def part(m, carry):
            at = pl.ds(pl.multiple_of(m * SLOT, SLOT), SLOT)
            inner = jnp.dot(low1[at, :], win[:, cols], preferred_element_type=f32) + ib_ref[cols].reshape(1, FFB)
            cdf = 0.5 + 0.5 * lax.erf(inner * (2.0**-0.5))
            actb[slot_at, at, :] = (inner * cdf).astype(bf16)
            slopeb[slot_at, at, :] = (cdf + inner * (jnp.exp(inner * inner * -0.5) * ((2.0 * math.pi) ** -0.5))).astype(bf16)
            return carry

        lax.fori_loop(0, pairs, part, 0, unroll=True)
        for copy in ff_copies(j, slot_at):
            copy.start()
        more = jnp.dot(actb[slot_at], wdown[cols, :], preferred_element_type=f32)
        if j == 0:
            hat2[...] = more
        else:
            hat2[...] += more

    def second(m, carry):
        at = pl.ds(pl.multiple_of(m * SLOT, SLOT), SLOT)
        normed = hat1[at, :] * g1_ref[...].reshape(1, D) + b1_ref[...].reshape(1, D)
        hidden = normed + (hat2[at, :] + db_ref[...].reshape(1, D))
        center = hidden - jnp.mean(hidden, -1, keepdims=True)
        rstd = lax.rsqrt(jnp.mean(center * center, -1, keepdims=True) + EPS)
        hat = center * rstd
        hat2[at, :] = hat
        rstd2[at, :] = jnp.broadcast_to(rstd, (SLOT, 128))
        outv[at, :] = (hat * g2_ref[...].reshape(1, D) + b2_ref[...].reshape(1, D)).astype(bf16)
        return carry

    lax.fori_loop(0, pairs, second, 0, unroll=True)
    stores[5].start()
    loads[5].wait()

    def fold(x):
        return jnp.sum(x.reshape(x.shape[0] // 8, 8, D), 0)

    def gsec_copy(p):
        at = pl.ds(p * SLOT, SLOT)
        return pltpu.make_async_copy(gsec.at[at], gsec_hbm.at[at], pair_sem.at[p])

    def emit(p, at, grad):
        total = cot[at, :].astype(f32) + grad
        hat = hat2[at, :]
        sums[0] += fold(total * hat)
        sums[1] += fold(total)
        wide = total * g2_ref[...].reshape(1, D)
        mean = jnp.mean(wide, -1, keepdims=True)
        slope = jnp.mean(wide * hat, -1, keepdims=True)
        grad = rstd2[at, 0:1] * (wide - mean - hat * slope)
        gsec[at, :] = grad
        sums[2] += fold(grad.astype(bf16).astype(f32))
        if at.start % SLOT:
            gsec_copy(p).start()

    align_body(pairs, first, outv, len_ref, dcot_ref, emit, dist_ref, *align_refs)
    for i in range(3):
        small_ref[i : i + 1, :] = jnp.sum(sums[i], 0, keepdims=True)
    small_ref[3:, :] = jnp.zeros((5, D), f32)
    for j in range(count):
        for copy in ff_copies(j, j):
            copy.wait()
    for store in stores:
        store.wait()
    for p in range(pairs):
        gsec_copy(p).wait()


def forward(tokens, cotangent, dcot, lengths, w_qkv, q_bias, v_bias, w_out, out_bias, g1, b1, w_in, in_bias, w_down, down_bias, g2, b2):
    rows = tokens.shape[0]
    pairs = rows // SLOT
    anywhere = pl.BlockSpec(memory_space=pl.ANY)
    vmem = pl.BlockSpec(memory_space=pltpu.VMEM)
    smem = pl.BlockSpec(memory_space=pltpu.SMEM)
    S = jax.ShapeDtypeStruct
    V = pltpu.VMEM
    dma = pltpu.SemaphoreType.DMA
    return pl.pallas_call(
        functools.partial(forward_kernel, pairs),
        out_shape=(
            S((rows, D), bf16), S((pairs,), f32), S((rows, 3 * D), bf16), S((rows, D), bf16), S((rows, D), f32), S((rows, D), bf16),
            S((rows, 128), f32), S((rows, 4 * D), bf16), S((rows, 4 * D), bf16), S((rows, D), f32), S((8, D), f32),
        ),
        in_specs=[anywhere] * 6 + [smem] * 2 + [vmem] * 9,
        out_specs=(anywhere, smem) + (anywhere,) * 8 + (vmem,),
        scratch_shapes=[
            V((rows, D), bf16), V((rows, D), bf16), V((D, 3 * D), bf16), V((D, D), bf16), V((D, 4 * D), bf16), V((4 * D, D), bf16), V((1, 3 * D), f32),
            V((rows, 3 * D), bf16), V((rows, D), bf16), V((rows, D), f32), V((rows, D), bf16), V((rows, 128), f32),
            V((4 * D // FFB, rows, FFB), bf16), V((4 * D // FFB, rows, FFB), bf16), V((rows, D), f32), V((rows, 128), f32), V((rows, D), bf16), V((rows, D), f32), V((3, 8, D), f32),
            dma((6,)), dma((6,)), dma((2, 4 * D // FFB)), dma((pairs,)),
        ] + scratch(pairs),
        compiler_params=pltpu.CompilerParams(vmem_limit_bytes=VMEM_LIMIT),
        name="forward",
    )(tokens, cotangent, w_qkv, w_out, w_in, w_down, lengths, dcot, q_bias, v_bias, out_bias, g1, b1, in_bias, down_bias, g2, b2)


def backward_kernel(pairs, ndp, *refs):
    (gsec_hbm, act_hbm, slope_hbm, low1_hbm, hat1_hbm, rstd1_hbm, ctx_hbm, packed_hbm, tok_hbm, wdown_hbm, win_hbm, wout_hbm, wqkv_hbm, len_ref, g1_ref, small2_ref,
     tgrad_hbm, full_hbm, small_out,
     table, total, low, act, slope, wdown, win, gin, lows, hat1, rstd1, packed, wout, wqkv, gatt, gctx, ffs, lns, qs,
     in_sem, ff_sem, out_sem, landing, far, sbuf, sland, *sems) = refs
    first = lax.axis_index("reg") * pairs
    nt = (((1,), (1,)), ((), ()))
    tn = (((0,), (0,)), ((), ()))
    ex = Exchange(ndp, table, full_hbm, landing, far, sbuf, sland, sems)
    count = 4 * D // FFB
    half = BLK // 2
    third = BLK // 3

    def dot(a, b, dims=(((1,), (0,)), ((), ()))):
        return lax.dot_general(a, b, dims, preferred_element_type=f32)

    def fold(x):
        return jnp.sum(x.reshape(x.shape[0] // 8, 8, x.shape[1]), 0)

    def by_pair(body):
        def run(m, carry):
            body(pl.ds(pl.multiple_of(m * SLOT, SLOT), SLOT))
            return carry

        lax.fori_loop(0, pairs, run, 0, unroll=True)

    def ff_loads(j):
        cols = pl.ds(j * FFB, FFB)
        s = j % 2
        parts = ((act_hbm.at[:, cols], act), (slope_hbm.at[:, cols], slope), (wdown_hbm.at[cols, :], wdown), (win_hbm.at[:, cols], win))
        return [pltpu.make_async_copy(src, dst.at[s], ff_sem.at[i, s]) for i, (src, dst) in enumerate(parts)]

    sources = ((gsec_hbm, total), (low1_hbm, lows), (hat1_hbm, hat1), (rstd1_hbm, rstd1), (packed_hbm, packed), (wout_hbm, wout), (wqkv_hbm, wqkv), (ctx_hbm, low), (tok_hbm, lows))
    loads = [pltpu.make_async_copy(src, dst, in_sem.at[i]) for i, (src, dst) in enumerate(sources)]
    loads[0].start()
    for copy in ff_loads(0):
        copy.start()
    ex.barrier()
    for ref in (ffs, lns, qs):
        ref[...] = jnp.zeros_like(ref)
    loads[0].wait()
    for i in range(1, 7):
        loads[i].start()

    def cast_branch(at):
        low[at, :] = total[at, :].astype(bf16)

    by_pair(cast_branch)
    pieces = []

    def piece(took, *made):
        def add(body):
            pieces.append((took, made, body))
            return body

        return add

    def store_table(block, start, value):
        table[block * BLK + start : block * BLK + start + value.shape[0], :] = value.astype(bf16)

    def ff_pieces(j):
        s = j % 2

        @piece(1.2, 4 * j, 4 * j + 1)
        def down():
            for copy in ff_loads(j):
                copy.wait()
            if j + 1 < count:
                for copy in ff_loads(j + 1):
                    copy.start()
            if j == 0:
                loads[1].wait()
            for c in range(3):
                value = dot(act[s], low[:, c * 256 : (c + 1) * 256], tn)
                for i in range(2):
                    g = 2 * c + i
                    store_table(4 * j + g // 3, g % 3 * third, value[:, i * COLS : (i + 1) * COLS])

        @piece(1.15)
        def inner():
            def body(at):
                grad = (dot(low[at, :], wdown[s], nt) * slope[s, at, :].astype(f32)).astype(bf16)
                gin[at, :] = grad
                ffs[j] += fold(grad.astype(f32))

            by_pair(body)

        @piece(1.2, 4 * j + 2, 4 * j + 3)
        def outer():
            for c in range(2):
                value = dot(lows[...], gin[:, c * 256 : (c + 1) * 256], tn)
                for i in range(2):
                    store_table(4 * j + 2 + c, i * half, value[:, i * COLS : (i + 1) * COLS])

        @piece(1.15)
        def back():
            total[...] += dot(gin[...], win[s], nt)

    for j in range(count):
        ff_pieces(j)

    @piece(1.5)
    def norm_back():
        loads[7].start()
        loads[8].start()
        loads[2].wait()
        loads[3].wait()
        gain = g1_ref[...].reshape(1, D)

        def body(at):
            grad = total[at, :]
            hat = hat1[at, :]
            wide = grad * gain
            new = rstd1[at, 0:1] * (wide - jnp.mean(wide, -1, keepdims=True) - hat * jnp.mean(wide * hat, -1, keepdims=True))
            total[at, :] = new
            lowered = new.astype(bf16)
            gatt[at, :] = lowered
            for i, value in enumerate((grad * hat, grad, lowered.astype(f32))):
                lns[i] += fold(value)

        by_pair(body)

    base = 4 * count

    def out_piece(c):
        @piece(0.45, base + c)
        def out():
            if c == 0:
                loads[7].wait()
            value = dot(low[...], gatt[:, c * 256 : (c + 1) * 256], tn)
            for i in range(2):
                store_table(base + c, i * half, value[:, i * COLS : (i + 1) * COLS])

    for c in range(3):
        out_piece(c)

    @piece(2.0)
    def context_back():
        loads[5].wait()
        gctx[...] = dot(gatt[...], wout[...], nt).astype(bf16)

    lane = lax.broadcasted_iota(jnp.int32, (1, 2 * HEAD_DIM), 1)
    scale = HEAD_DIM**-0.5
    left = jnp.where(lane < HEAD_DIM, 1.0, 0.0).astype(bf16)
    right = jnp.where(lane < HEAD_DIM, 0.0, 1.0).astype(bf16)
    slot = lax.broadcasted_iota(jnp.int32, (SLOT, 1), 0)

    def pair_piece(p, part):
        @piece(1.9)
        def attention_back():
            if p == 0 and part == 0:
                loads[4].wait()
            words, regions = len_ref[0, first + p], len_ref[1, first + p]
            shut = jnp.where(jnp.where(slot < WORDS, words, regions + WORDS) > slot, 0.0, -1e30)
            at = slice(p * SLOT, (p + 1) * SLOT)
            for h in range(part * HEADS // 4, (part + 1) * HEADS // 4):
                c = h * 128
                q = packed[at, c : c + 128]
                k = packed[at, D + c : D + c + 128]
                v = packed[at, 2 * D + c : 2 * D + c + 128]
                g = gctx[at, c : c + 128]
                both = jnp.concatenate([q * (left * scale).astype(bf16), q * (right * scale).astype(bf16)], 0)
                grads = jnp.concatenate([g * left, g * right], 0)
                s = dot(k, both, nt) + shut
                e = jnp.exp(s - jnp.max(s, 0, keepdims=True))
                pr = e * (1.0 / jnp.sum(e, 0, keepdims=True))
                gp = dot(v, grads, nt)
                gs = (pr * (gp - jnp.sum(pr * gp, 0, keepdims=True))).astype(bf16)
                gq = dot(gs, k, tn)
                gq = jnp.where(lane < HEAD_DIM, gq[:SLOT], gq[SLOT:]) * scale
                gk = dot(gs, both)
                gv = dot(pr.astype(bf16), grads)
                for i, value in enumerate((gq, gk, gv)):
                    value = value.astype(bf16)
                    packed[at, i * D + c : i * D + c + 128] = value
                    if i != 1:
                        qs[:, i * D + c : i * D + c + 128] += fold(value.astype(f32))

    for p in range(pairs):
        for part in range(2):
            pair_piece(p, part)

    @piece(0.3, NBLK)
    def singles():
        def row(i, value):
            sbuf[i : i + 1, :] = value

        def down(x):
            return jnp.sum(x, 0, keepdims=True)

        row(0, down(qs[:, 0:D]))
        row(1, down(qs[:, 2 * D : 3 * D]))
        row(2, down(lns[2]))
        row(3, down(lns[0]))
        row(4, down(lns[1]))
        row(5, small2_ref[2:3, :])
        row(6, small2_ref[0:1, :])
        row(7, small2_ref[1:2, :])
        for j in range(count):
            at = j * FFB
            value = down(ffs[j])
            while value.shape[1]:
                room = min(D - at % D, value.shape[1])
                sbuf[8 + at // D : 9 + at // D, at % D : at % D + room] = value[:, :room]
                at, value = at + room, value[:, room:]
        sbuf[12:16, :] = jnp.zeros((4, D), f32)

    def qkv_piece(c):
        @piece(0.45, base + 3 + c)
        def qkv():
            if c == 0:
                loads[8].wait()
            value = dot(lows[...], packed[:, c * 256 : (c + 1) * 256], tn)
            for i in range(2):
                store_table(base + 3 + c, i * half, value[:, i * COLS : (i + 1) * COLS])

    for c in range(9):
        qkv_piece(c)

    def token_piece(c):
        @piece(1.5)
        def tokens_back():
            if c == 0:
                loads[6].wait()
            cols = slice(c * D, (c + 1) * D)
            total[...] += dot(packed[:, cols], wqkv[:, cols], nt)
            if c == 2:
                pltpu.make_async_copy(total, tgrad_hbm, out_sem).start()

    for c in range(3):
        token_piece(c)

    for what, block, step, _ in plan([(took, made) for took, made, _ in pieces], ex.extra):
        if what == "piece":
            pieces[block][2]()
        elif what == "start":
            ex.start(block, step)
        else:
            ex.handle(block, step)
    small_out[...] = sbuf[...]
    ex.finish()
    pltpu.make_async_copy(total, tgrad_hbm, out_sem).wait()


def backward(ndp, gsec, act, slope, low1, hat1, rstd1, ctx, packed, tokens, w_down, w_in, w_out, w_qkv, lengths, g1, small2):
    rows = tokens.shape[0]
    pairs = rows // SLOT
    anywhere = pl.BlockSpec(memory_space=pl.ANY)
    vmem = pl.BlockSpec(memory_space=pltpu.VMEM)
    smem = pl.BlockSpec(memory_space=pltpu.SMEM)
    S = jax.ShapeDtypeStruct
    V = pltpu.VMEM
    dma = pltpu.SemaphoreType.DMA
    return pl.pallas_call(
        functools.partial(backward_kernel, pairs, ndp),
        out_shape=(S((rows, D), f32), S((NBLK * BLK, COLS), bf16), S((16, D), f32)),
        in_specs=[anywhere] * 13 + [smem] + [vmem] * 2,
        out_specs=(anywhere, anywhere, vmem),
        scratch_shapes=[
            V((NBLK * BLK, COLS), bf16), V((rows, D), f32), V((rows, D), bf16), V((2, rows, FFB), bf16), V((2, rows, FFB), bf16), V((2, FFB, D), bf16), V((2, D, FFB), bf16),
            V((rows, FFB), bf16), V((rows, D), bf16), V((rows, D), f32), V((rows, 128), f32), V((rows, 3 * D), bf16), V((D, D), bf16), V((D, 3 * D), bf16),
            V((rows, D), bf16), V((rows, D), bf16), V((4 * D // FFB, 8, FFB), f32), V((3, 8, D), f32), V((8, 3 * D), f32),
            dma((9,)), dma((4, 2)), dma,
        ] + exchange_scratch(ndp),
        compiler_params=pltpu.CompilerParams(collective_id=1, has_side_effects=True, vmem_limit_bytes=VMEM_LIMIT),
        name="backward",
    )(gsec, act, slope, low1, hat1, rstd1, ctx, packed, tokens, w_down, w_in, w_out, w_qkv, lengths, g1, small2)


WIDE = (192, 384, 128, 512)


def widen_units():
    units = [(3, FFB * j + r, r, 12 * j) for j in range(6) for r in range(0, FFB, WIDE[3])]
    units += [(2, r, r, 0) for r in range(0, D, WIDE[2])]
    units += [(0, r, r, 54) for r in range(0, D, WIDE[0])]
    units += [(1, r, r, 48) for r in range(0, D, WIDE[1])]
    return units


def widen_kernel(depth, thirds, halves, eighths, small, tgrad, *refs):
    outs, singles, tgrad_out = refs[0:4], refs[4:13], refs[13]
    narrow, wide, held, in_sem, out_sem, own_sem = refs[14:18], refs[18:22], refs[22], refs[23], refs[24], refs[25]
    units = widen_units()
    take = pltpu.make_async_copy(tgrad, held, own_sem.at[0])
    move = pltpu.make_async_copy(held, tgrad_out, own_sem.at[1])

    def into(u):
        which, _, row, at = units[u]
        dst = narrow[which].at[u % depth]
        rows = pl.ds(row, WIDE[which])
        if which == 2:
            src = eighths.at[0:6, 4:8, rows]
        elif which == 3:
            src = thirds.at[pl.ds(at, 6), rows]
        else:
            src = halves.at[pl.ds(at, 18 if which == 0 else 6), rows]
        return pltpu.make_async_copy(src, dst, in_sem.at[u % depth])

    def back(u):
        which, row, _, _ = units[u]
        return pltpu.make_async_copy(wide[which].at[u % depth], outs[which].at[pl.ds(row, WIDE[which])], out_sem.at[u % depth])

    for u in range(depth - 1):
        into(u).start()
    for i in range(8):
        singles[i][...] = small[i, :]
    singles[8][...] = jnp.concatenate([small[i : i + 1, :] for i in range(8, 12)], 1).reshape(4 * D)
    for v in range(len(units)):
        if v + depth - 1 < len(units):
            into(v + depth - 1).start()
        if v == 0:
            take.start()
        if v == 4:
            take.wait()
            move.start()
        into(v).wait()
        if v >= depth:
            back(v - depth).wait()
        which, s = units[v][0], v % depth
        for c in range(wide[which].shape[2] // COLS):
            piece = narrow[which][s, c // 4, c % 4] if which == 2 else narrow[which][s, c]
            wide[which][s, :, c * COLS : (c + 1) * COLS] = piece.astype(f32)
        back(v).start()
    for v in range(len(units) - depth, len(units)):
        back(v).wait()
    move.wait()


def unpack_table(table, small, tgrad):
    anywhere = pl.BlockSpec(memory_space=pl.ANY)
    vmem = pl.BlockSpec(memory_space=pltpu.VMEM)
    depth = 3
    S = jax.ShapeDtypeStruct
    V = pltpu.VMEM
    dma = pltpu.SemaphoreType.DMA
    return pl.pallas_call(
        functools.partial(widen_kernel, depth),
        out_shape=(S((D, 3 * D), f32), S((D, D), f32), S((D, 4 * D), f32), S((4 * D, D), f32)) + (S((D,), f32),) * 8 + (S((4 * D,), f32), S(tgrad.shape, f32)),
        in_specs=[anywhere] * 3 + [vmem, anywhere],
        out_specs=(anywhere,) * 4 + (vmem,) * 9 + (anywhere,),
        scratch_shapes=[
            V((depth, 18, WIDE[0], COLS), bf16), V((depth, 6, WIDE[1], COLS), bf16), V((depth, 6, 4, WIDE[2], COLS), bf16), V((depth, 6, WIDE[3], COLS), bf16),
            V((depth, WIDE[0], 3 * D), f32), V((depth, WIDE[1], D), f32), V((depth, WIDE[2], 4 * D), f32), V((depth, WIDE[3], D), f32), V(tgrad.shape, f32),
            dma((depth,)), dma((depth,)), dma((2,)),
        ],
        compiler_params=pltpu.CompilerParams(vmem_limit_bytes=VMEM_LIMIT),
        name="widen",
    )(table.reshape(108, 512, COLS), table.reshape(72, D, COLS), table.reshape(9, 8, D, COLS), small, tgrad)


def on_device(ndp, tokens, cotangent, distance_cot, lengths, w_qkv, q_bias, v_bias, w_out, out_bias, ln1_gain, ln1_bias, w_in, in_bias, w_down, down_bias, ln2_gain, ln2_bias):
    sizes = jnp.transpose(lengths)
    result, distance, packed, ctx, hat1, low1, rstd1, act, slope, gsec, small2 = forward(
        tokens, cotangent, distance_cot, sizes, w_qkv, q_bias, v_bias, w_out, out_bias, ln1_gain, ln1_bias, w_in, in_bias, w_down, down_bias, ln2_gain, ln2_bias
    )
    grad_tokens, table, small = backward(ndp, gsec, act, slope, low1, hat1, rstd1, ctx, packed, tokens, w_down, w_in, w_out, w_qkv, sizes, ln1_gain, small2)
    g_qkv, g_out, g_in, g_down, g_qb, g_vb, g_ob, g_g1, g_b1, g_db, g_g2, g_b2, g_ib, grad_tokens = unpack_table(table, small, grad_tokens)
    return result, distance, grad_tokens, g_qkv, g_qb, g_vb, g_out, g_ob, g_g1, g_b1, g_in, g_ib, g_down, g_db, g_g2, g_b2


def solution(mesh):
    rows = P(("dp", "reg"), None)
    return jax.shard_map(
        functools.partial(on_device, mesh.shape["dp"]),
        mesh=mesh,
        in_specs=(rows, rows, P("dp"), P("dp", None)) + (P(),) * 13,
        out_specs=(rows, P(("dp", "reg")), rows) + (P(),) * 13,
        check_vma=False,
    )
```

```python
import functools
import heapq
import itertools
import math

import jax
import jax.numpy as jnp
from jax import lax
from jax.experimental import pallas as pl
from jax.experimental.pallas import tpu as pltpu
from jax.sharding import PartitionSpec as P

D = 768
HEADS = 12
HEAD_DIM = 64
WORDS = 64
REGIONS = 128
SLOT = WORDS + REGIONS
ITERS = 50
EPS = 1e-06
f32 = jnp.float32
bf16 = jnp.bfloat16
MESH = pl.DeviceIdType.MESH
VMEM_LIMIT = 62 * 2**20

BLK = 1536
COLS = 128
FFB = 512
NBLK = 36
HALVES = 5
RBLK = BLK - (BLK >> HALVES)
ORDERS = (
    ("c", "x", "y", "z0", "z1"),
    ("c", "y", "x", "z0", "z1"),
    ("c", "z0", "x", "y", "z1"),
    ("c", "z0", "y", "x", "z1"),
    ("c", "x", "z0", "y", "z1"),
    ("c", "y", "z0", "x", "z1"),
    ("c", "z0", "z1", "x", "y"),
    ("c", "z0", "z1", "y", "x"),
)
TAKES = (5, 4, 0, 5, 4, 1, 4, 4, 1, 3, 1, 0, 1, 5, 2, 0, 5, 0, 1, 5, 0, 1, 0, 0, 0, 0, 2, 1, 5, 0, 3, 3, 3, 5, 4, 4)


def order_of(block):
    return ORDERS[TAKES[block]]


def plan(pieces, extra, rate=80e3, core_rate=450e3, delay=2.4, ahead=3.0, add=0.075):
    last = 2 * HALVES + extra - 1
    block_bytes = BLK * COLS * 2
    lines = ("c", "x", "y", "z", "far")
    free = dict.fromkeys(lines, 0.0)
    waiting = {line: [] for line in lines}
    arrivals = []
    steps = []
    ticket = itertools.count()
    now = 0.0

    def facts(block, step):
        if block == NBLK:
            return ("c", "x", "y", "z0", "z1")[step] if step < HALVES else "far", 16 * D * 4
        if step < HALVES:
            return order_of(block)[step], block_bytes >> (step + 1)
        if step < HALVES + extra:
            return "far", block_bytes >> HALVES
        return order_of(block)[last - step], block_bytes >> (last - step + 1)

    def ask(block, step):
        name = facts(block, step)[0]
        line = "z" if name in ("z0", "z1") else name
        heapq.heappush(waiting[line], (step >= HALVES and block < NBLK, next(ticket), block, step))

    index = 0
    while index < len(pieces) or arrivals or any(waiting.values()):
        if arrivals and (arrivals[0][0] <= now or index == len(pieces)):
            at, _, block, step = heapq.heappop(arrivals)
            now = max(now, at) + 0.05
            if block < NBLK and step < HALVES:
                now += add / 2**step
            steps.append(("handle", block, step, now))
            if step < (HALVES + extra - 1 if block == NBLK else last):
                ask(block, step + 1)
        else:
            took, made = pieces[index]
            now += took
            steps.append(("piece", index, 0, now))
            for block in made:
                ask(block, 0)
            index += 1
        for line, queue in waiting.items():
            while queue and free[line] - now < ahead:
                _, _, block, step = heapq.heappop(queue)
                name, sent = facts(block, step)
                took = sent / core_rate if name == "c" else 2 * sent / rate
                free[line] = max(now, free[line]) + took
                heapq.heappush(arrivals, (free[line] + (took if name == "z1" else 0.0) + delay, next(ticket), block, step))
                steps.append(("start", block, step, now))
    return steps


def mesh_partners(ndp):
    dp = lax.axis_index("dp")
    reg = lax.axis_index("reg")
    names = [("c", "reg", 1), ("x", "reg", 2), ("y", "dp", 1), ("z0", "dp", 2), ("z1", "dp", 4)]
    step = 8
    while step < ndp:
        names.append(("far%d" % step, "dp", step))
        step *= 2
    partners = {}
    for name, axis, step in names:
        at = reg if axis == "reg" else dp
        bit = lax.rem(at // step, 2)
        other = at + step - 2 * step * bit
        partners[name] = (bit, (dp, other) if axis == "reg" else (other, reg))
    return partners


class Exchange:
    def __init__(self, ndp, table, full, landing, far, small, small_in, sems):
        self.partners = mesh_partners(ndp)
        self.fars = [name for name in self.partners if name.startswith("far")]
        self.extra = len(self.fars)
        self.table, self.full, self.landing, self.far = table, full, landing, far
        self.small, self.small_in = small, small_in
        self.rs_send, self.rs_recv, self.ag_send, self.ag_recv, self.far_send, self.far_recv, self.sm_send, self.sm_recv, self.own = sems

    def barrier(self):
        bar = pltpu.get_barrier_semaphore()
        for _, who in self.partners.values():
            pl.semaphore_signal(bar, inc=1, device_id=who, device_id_type=MESH)
        pl.semaphore_wait(bar, len(self.partners))

    def offset(self, block, steps):
        at, size = block * BLK, BLK
        for step in range(steps):
            size //= 2
            at = at + self.partners[order_of(block)[step]][0] * size
        return pl.multiple_of(at, 16) if steps else at

    def halving(self, block, step):
        bit, who = self.partners[order_of(block)[step]]
        size = BLK >> (step + 1)
        src = pl.multiple_of(self.offset(block, step) + (1 - bit) * size, 16)
        land = block * RBLK + (BLK - (BLK >> step))
        return pltpu.make_async_remote_copy(
            self.table.at[pl.ds(src, size)],
            self.landing.at[pl.ds(land, size)],
            self.rs_send.at[block, step],
            self.rs_recv.at[block, step],
            device_id=who,
            device_id_type=MESH,
        )

    def far_step(self, block, index):
        _, who = self.partners[self.fars[index]]
        size = BLK >> HALVES
        src = self.offset(block, HALVES)
        return pltpu.make_async_remote_copy(
            self.table.at[pl.ds(src, size)],
            self.far.at[block, index],
            self.far_send.at[block, index],
            self.far_recv.at[block, index],
            device_id=who,
            device_id_type=MESH,
        )

    def image(self, block, steps):
        at = self.offset(block, steps) - self.offset(block, 1) + block * RBLK
        return self.landing.at[pl.ds(pl.multiple_of(at, 16), BLK >> steps)]

    def returning(self, block, step):
        _, who = self.partners[order_of(block)[step]]
        own = pl.ds(self.offset(block, step + 1), BLK >> (step + 1))
        return pltpu.make_async_remote_copy(
            self.table.at[own] if step + 1 == HALVES else self.image(block, step + 1),
            self.image(block, step + 1) if step else self.full.at[own],
            self.ag_send.at[block, step],
            self.ag_recv.at[block, step],
            device_id=who,
            device_id_type=MESH,
        )

    def keep(self, block):
        at = pl.ds(self.offset(block, HALVES), BLK >> HALVES)
        return pltpu.make_async_copy(self.table.at[at], self.image(block, HALVES), self.own.at[block, 0])

    def place(self, block):
        at = pl.ds(self.offset(block, 1), BLK // 2)
        return pltpu.make_async_copy(self.image(block, 1), self.full.at[at], self.own.at[block, 1])

    def start(self, block, step):
        if block == NBLK:
            self.small_copy(step).start()
        elif step < HALVES:
            self.halving(block, step).start()
        elif step < HALVES + self.extra:
            self.far_step(block, step - HALVES).start()
        else:
            back = 2 * HALVES + self.extra - 1 - step
            if back + 1 == HALVES:
                self.keep(block).start()
            self.returning(block, back).start()
            if back == 0:
                self.place(block).start()

    def handle(self, block, event):
        if block == NBLK:
            self.small_handle(event)
            return
        if event < HALVES:
            self.halving(block, event).wait_recv()
            size = BLK >> (event + 1)
            off = self.offset(block, event + 1)
            land = block * RBLK + (BLK - (BLK >> event))
            rows = min(size, 192)

            def add(index, carry):
                at = pl.ds(pl.multiple_of(off + index * rows, 16), rows)
                self.table[at, :] += self.landing[pl.ds(pl.multiple_of(land + index * rows, 16), rows), :]
                return carry

            lax.fori_loop(0, size // rows, add, 0)
        elif event < HALVES + self.extra:
            index = event - HALVES
            copy = self.far_step(block, index)
            copy.wait()
            at = pl.ds(self.offset(block, HALVES), BLK >> HALVES)
            self.table[at, :] += self.far[block, index]
        else:
            back = 2 * HALVES + self.extra - 1 - event
            self.returning(block, back).wait_recv()
            if back + 1 == HALVES:
                self.keep(block).wait()

    def small_copy(self, index):
        _, who = self.partners[list(self.partners)[index]]
        return pltpu.make_async_remote_copy(
            self.small,
            self.small_in.at[index],
            self.sm_send.at[index],
            self.sm_recv.at[index],
            device_id=who,
            device_id_type=MESH,
        )

    def small_handle(self, index):
        self.small_copy(index).wait()
        self.small[...] = self.small[...] + self.small_in[index]

    def finish(self):
        for block in range(NBLK):
            for step in range(HALVES):
                self.halving(block, step).wait_send()
                self.returning(block, step).wait_send()
            self.place(block).wait()


def exchange_scratch(ndp):
    extra = max(int(math.log2(ndp)) - 3, 0)
    count = HALVES + extra
    dma = pltpu.SemaphoreType.DMA
    return [
        pltpu.VMEM((NBLK * RBLK, COLS), bf16),
        pltpu.VMEM((NBLK, max(extra, 1), BLK >> HALVES, COLS), bf16),
        pltpu.VMEM((16, D), f32),
        pltpu.VMEM((count, 16, D), f32),
        dma((NBLK, HALVES)),
        dma((NBLK, HALVES)),
        dma((NBLK, HALVES)),
        dma((NBLK, HALVES)),
        dma((NBLK, max(extra, 1))),
        dma((NBLK, max(extra, 1))),
        dma((count,)),
        dma((count,)),
        dma((NBLK, 2)),
    ]


def align_body(pairs, first, rows_ref, len_ref, dcot_ref, emit, dist_ref, kern, trans, uhist, acur, acc, alpha, gamma, cosr):
    P = range(pairs)
    eye = lax.broadcasted_iota(jnp.int32, (REGIONS, REGIONS), 0) == lax.broadcasted_iota(jnp.int32, (REGIONS, REGIONS), 1)
    wcol = lax.broadcasted_iota(jnp.int32, (WORDS, 1), 0)
    rrow = lax.broadcasted_iota(jnp.int32, (1, REGIONS), 1)
    nlen = [len_ref[0, first + p] for p in P]
    mlen = [len_ref[1, first + p] for p in P]
    nf = [v.astype(f32) for v in nlen]
    mf = [v.astype(f32) for v in mlen]
    dc = [dcot_ref[first + p] for p in P]
    wv = [(wcol < nlen[p]).astype(f32) for p in P]
    rv = [(rrow < mlen[p]).astype(f32) for p in P]
    rxs, rys = [], []
    for p in P:
        x = rows_ref[SLOT * p:SLOT * p + WORDS, :]
        y = rows_ref[SLOT * p + WORDS:SLOT * (p + 1), :]
        xf, yf = x.astype(f32), y.astype(f32)
        rx = lax.rsqrt(jnp.sum(xf * xf, -1, keepdims=True) + EPS)
        ry = lax.rsqrt(jnp.sum(yf * yf, -1, keepdims=True) + EPS)
        ryr = jnp.sum(jnp.where(eye, ry, 0.0), 0, keepdims=True)
        rxs.append(rx); rys.append((ry, ryr))
        cos = lax.dot_general(x, y, (((1,), (1,)), ((), ())), preferred_element_type=f32) * rx * ryr
        joint = wv[p] * rv[p]
        cost = (1.0 - cos) * joint
        cosr[p] = cos
        kern[p] = jnp.exp(-2.0 * cost) * joint
        trans[p] = joint
        acur[p] = jnp.broadcast_to(wv[p] / nf[p], (WORDS, REGIONS))
        uhist[0, p] = jnp.where(rrow == 0, wv[p], 0.0)
    def fwd(t, _):
        joined = [kern[p] * trans[p] for p in P]
        a = [acur[p] for p in P]
        s = [jnp.sum(joined[p] * a[p], 0, keepdims=True) for p in P]
        b = [rv[p] / (mf[p] * s[p] + (1.0 - rv[p])) for p in P]
        u = [joined[p] * b[p] for p in P]
        w = [jnp.sum(u[p], 1, keepdims=True) for p in P]
        an = [wv[p] / (nf[p] * w[p] + (1.0 - wv[p])) for p in P]
        for p in P:
            uhist[t + 1, p] = u[p]
            acur[p] = jnp.broadcast_to(an[p], (WORDS, REGIONS))
            trans[p] = u[p] * an[p]
        return 0
    lax.fori_loop(0, ITERS, fwd, 0)
    cols = []
    for p in P:
        joint = wv[p] * rv[p]
        cost = (1.0 - cosr[p]) * joint
        tc = trans[p] * cost
        dist_ref[p] = jnp.sum(tc)
        g = tc * dc[p]
        cols.append(jnp.sum(g, 0, keepdims=True))
        alpha[p] = jnp.broadcast_to(jnp.sum(g, 1, keepdims=True), (WORDS, REGIONS))
        gamma[p] = jnp.zeros((WORDS, REGIONS), f32)
        acc[p] = float(ITERS) * g
    def bwd(i, cols):
        t = ITERS - i
        tf = t.astype(f32)
        u = [uhist[t, p] for p in P]
        before = [uhist[t - 1, p] for p in P]
        x = [nf[p] * alpha[p] * acur[p] for p in P]
        ap = [wv[p] / (nf[p] * jnp.sum(before[p], 1, keepdims=True) + (1.0 - wv[p])) for p in P]
        y = [mf[p] * ap[p] for p in P]
        beta = [cols[p] - jnp.sum(u[p] * x[p], 0, keepdims=True) for p in P]
        ub = [u[p] * beta[p] for p in P]
        gm = [jnp.broadcast_to(-y[p] * jnp.sum(ub[p], 1, keepdims=True), (WORDS, REGIONS)) for p in P]
        go = [gamma[p] for p in P]
        ac = [acc[p] for p in P]
        for p in P:
            acc[p] = ac[p] - tf * (u[p] * x[p] + y[p] * ub[p])
            alpha[p] = 2.0 * gm[p] - go[p]
            gamma[p] = gm[p]
            acur[p] = jnp.broadcast_to(ap[p], (WORDS, REGIONS))
        return tuple(jnp.zeros_like(c) for c in cols)
    lax.fori_loop(0, ITERS, bwd, tuple(cols))
    for p in P:
        x = rows_ref[SLOT * p:SLOT * p + WORDS, :]
        y = rows_ref[SLOT * p + WORDS:SLOT * (p + 1), :]
        rx = rxs[p]; ry, ryr = rys[p]
        gc = dc[p] * trans[p] - 2.0 * acc[p]
        gcos = gc * cosr[p]
        m = gc * rx * ryr
        hi = m.astype(bf16)
        lo = (m - hi.astype(f32)).astype(bf16)
        nt = (((1,), (0,)), ((), ())); tn = (((0,), (0,)), ((), ()))
        gx = lax.dot_general(hi, y, nt, preferred_element_type=f32) + lax.dot_general(lo, y, nt, preferred_element_type=f32)
        gy = lax.dot_general(hi, x, tn, preferred_element_type=f32) + lax.dot_general(lo, x, tn, preferred_element_type=f32)
        sx = rx * rx * jnp.sum(gcos, 1, keepdims=True)
        sy = ry * ry * jnp.sum(jnp.where(eye, jnp.sum(gcos, 0, keepdims=True), 0.0), 1, keepdims=True)
        emit(p, pl.ds(SLOT * p, WORDS), sx * x.astype(f32) - gx)
        emit(p, pl.ds(SLOT * p + WORDS, REGIONS), sy * y.astype(f32) - gy)

def scratch(pairs):
    v = lambda *s: pltpu.VMEM(s, f32)
    W = (WORDS, REGIONS)
    return [v(pairs, *W), v(pairs, *W), v(ITERS + 1, pairs, *W), v(pairs, *W), v(pairs, *W), v(pairs, *W), v(pairs, *W), v(pairs, *W)]


def forward_kernel(pairs, *refs):
    (tok_hbm, cot_hbm, wqkv_hbm, wout_hbm, win_hbm, wdown_hbm, len_ref, dcot_ref, qb_ref, vb_ref, ob_ref, g1_ref, b1_ref, ib_ref, db_ref, g2_ref, b2_ref,
     out_hbm, dist_ref, packed_hbm, ctx_hbm, hat1_hbm, low1_hbm, rstd1_hbm, act_hbm, slope_hbm, gsec_hbm, small_ref,
     tok, cot, wqkv, wout, win, wdown, qkvb, packed, ctx, hat1, low1, rstd1, actb, slopeb, hat2, rstd2, outv, gsec, sums,
     in_sem, out_sem, ff_sem, pair_sem, *align_refs) = refs
    rows = pairs * SLOT
    first = lax.axis_index("reg") * pairs
    loads = [
        pltpu.make_async_copy(src, dst, in_sem.at[i])
        for i, (src, dst) in enumerate(((tok_hbm, tok), (wqkv_hbm, wqkv), (wout_hbm, wout), (win_hbm, win), (wdown_hbm, wdown), (cot_hbm, cot)))
    ]
    loads[0].start()
    loads[1].start()
    stores = [
        pltpu.make_async_copy(src, dst, out_sem.at[i])
        for i, (src, dst) in enumerate(((packed, packed_hbm), (ctx, ctx_hbm), (hat1, hat1_hbm), (low1, low1_hbm), (rstd1, rstd1_hbm), (outv, out_hbm)))
    ]
    qkvb[:, 0:D] = qb_ref[...].reshape(1, D)
    qkvb[:, D : 2 * D] = jnp.zeros((1, D), f32)
    qkvb[:, 2 * D :] = vb_ref[...].reshape(1, D)
    sums[...] = jnp.zeros_like(sums)

    loads[0].wait()
    loads[1].wait()
    for load in loads[2:]:
        load.start()

    def project(n, carry):
        cols = pl.ds(pl.multiple_of(n * D, D), D)
        packed[:, cols] = (jnp.dot(tok[...], wqkv[:, cols], preferred_element_type=f32) + qkvb[:, cols]).astype(bf16)
        return carry

    lax.fori_loop(0, 3, project, 0)
    stores[0].start()
    loads[2].wait()

    lane = lax.broadcasted_iota(jnp.int32, (1, 2 * HEAD_DIM), 1)
    left = jnp.where(lane < HEAD_DIM, HEAD_DIM**-0.5, 0.0).astype(bf16)
    right = jnp.where(lane < HEAD_DIM, 0.0, HEAD_DIM**-0.5).astype(bf16)
    slot = lax.broadcasted_iota(jnp.int32, (1, SLOT), 1)
    nt = (((1,), (1,)), ((), ()))

    def attend(p, carry):
        at = pl.ds(pl.multiple_of(p * SLOT, SLOT), SLOT)
        words, regions = len_ref[0, first + p], len_ref[1, first + p]
        shut = jnp.where(jnp.where(slot < WORDS, words, regions + WORDS) > slot, 0.0, -1e30)
        for h in range(HEADS // 2):
            c = h * 2 * HEAD_DIM
            q = packed[at, c : c + 128]
            k = packed[at, D + c : D + c + 128]
            v = packed[at, 2 * D + c : 2 * D + c + 128]
            both = jnp.concatenate([q * left, q * right], 0)
            s = lax.dot_general(both, k, nt, preferred_element_type=f32) + shut
            e = jnp.exp(s - jnp.max(s, -1, keepdims=True))
            pr = (e / jnp.sum(e, -1, keepdims=True)).astype(bf16)
            o = jnp.dot(pr, v, preferred_element_type=f32)
            ctx[at, c : c + 128] = jnp.where(lane < HEAD_DIM, o[:SLOT], o[SLOT:]).astype(bf16)
        return carry

    lax.fori_loop(0, pairs, attend, 0, unroll=True)
    stores[1].start()

    def norm(p, carry):
        at = pl.ds(pl.multiple_of(p * SLOT, SLOT), SLOT)
        hidden = tok[at, :].astype(f32) + (jnp.dot(ctx[at, :], wout[...], preferred_element_type=f32) + ob_ref[...].reshape(1, D))
        center = hidden - jnp.mean(hidden, -1, keepdims=True)
        rstd = lax.rsqrt(jnp.mean(center * center, -1, keepdims=True) + EPS)
        hat = center * rstd
        hat1[at, :] = hat
        rstd1[at, :] = jnp.broadcast_to(rstd, (SLOT, 128))
        low1[at, :] = (hat * g1_ref[...].reshape(1, D) + b1_ref[...].reshape(1, D)).astype(bf16)
        return carry

    lax.fori_loop(0, pairs, norm, 0, unroll=True)
    for i in range(2, 5):
        stores[i].start()
    loads[3].wait()
    loads[4].wait()

    count = 4 * D // FFB

    def ff_copies(j, slot_at):
        cols = pl.ds(pl.multiple_of(j * FFB, FFB), FFB)
        return (
            pltpu.make_async_copy(actb.at[slot_at], act_hbm.at[:, cols], ff_sem.at[0, slot_at]),
            pltpu.make_async_copy(slopeb.at[slot_at], slope_hbm.at[:, cols], ff_sem.at[1, slot_at]),
        )

    for j in range(count):
        slot_at = j
        cols = slice(j * FFB, (j + 1) * FFB)

        def part(m, carry):
            at = pl.ds(pl.multiple_of(m * SLOT, SLOT), SLOT)
            inner = jnp.dot(low1[at, :], win[:, cols], preferred_element_type=f32) + ib_ref[cols].reshape(1, FFB)
            cdf = 0.5 + 0.5 * lax.erf(inner * (2.0**-0.5))
            actb[slot_at, at, :] = (inner * cdf).astype(bf16)
            slopeb[slot_at, at, :] = (cdf + inner * (jnp.exp(inner * inner * -0.5) * ((2.0 * math.pi) ** -0.5))).astype(bf16)
            return carry

        lax.fori_loop(0, pairs, part, 0, unroll=True)
        for copy in ff_copies(j, slot_at):
            copy.start()
        more = jnp.dot(actb[slot_at], wdown[cols, :], preferred_element_type=f32)
        if j == 0:
            hat2[...] = more
        else:
            hat2[...] += more

    def second(m, carry):
        at = pl.ds(pl.multiple_of(m * SLOT, SLOT), SLOT)
        normed = hat1[at, :] * g1_ref[...].reshape(1, D) + b1_ref[...].reshape(1, D)
        hidden = normed + (hat2[at, :] + db_ref[...].reshape(1, D))
        center = hidden - jnp.mean(hidden, -1, keepdims=True)
        rstd = lax.rsqrt(jnp.mean(center * center, -1, keepdims=True) + EPS)
        hat = center * rstd
        hat2[at, :] = hat
        rstd2[at, :] = jnp.broadcast_to(rstd, (SLOT, 128))
        outv[at, :] = (hat * g2_ref[...].reshape(1, D) + b2_ref[...].reshape(1, D)).astype(bf16)
        return carry

    lax.fori_loop(0, pairs, second, 0, unroll=True)
    stores[5].start()
    loads[5].wait()

    def fold(x):
        return jnp.sum(x.reshape(x.shape[0] // 8, 8, D), 0)

    def gsec_copy(p):
        at = pl.ds(p * SLOT, SLOT)
        return pltpu.make_async_copy(gsec.at[at], gsec_hbm.at[at], pair_sem.at[p])

    def emit(p, at, grad):
        total = cot[at, :].astype(f32) + grad
        hat = hat2[at, :]
        sums[0] += fold(total * hat)
        sums[1] += fold(total)
        wide = total * g2_ref[...].reshape(1, D)
        mean = jnp.mean(wide, -1, keepdims=True)
        slope = jnp.mean(wide * hat, -1, keepdims=True)
        grad = rstd2[at, 0:1] * (wide - mean - hat * slope)
        gsec[at, :] = grad
        sums[2] += fold(grad.astype(bf16).astype(f32))
        if at.start % SLOT:
            gsec_copy(p).start()

    align_body(pairs, first, outv, len_ref, dcot_ref, emit, dist_ref, *align_refs)
    for i in range(3):
        small_ref[i : i + 1, :] = jnp.sum(sums[i], 0, keepdims=True)
    small_ref[3:, :] = jnp.zeros((5, D), f32)
    for j in range(count):
        for copy in ff_copies(j, j):
            copy.wait()
    for store in stores:
        store.wait()
    for p in range(pairs):
        gsec_copy(p).wait()


def forward(tokens, cotangent, dcot, lengths, w_qkv, q_bias, v_bias, w_out, out_bias, g1, b1, w_in, in_bias, w_down, down_bias, g2, b2):
    rows = tokens.shape[0]
    pairs = rows // SLOT
    anywhere = pl.BlockSpec(memory_space=pl.ANY)
    vmem = pl.BlockSpec(memory_space=pltpu.VMEM)
    smem = pl.BlockSpec(memory_space=pltpu.SMEM)
    S = jax.ShapeDtypeStruct
    V = pltpu.VMEM
    dma = pltpu.SemaphoreType.DMA
    return pl.pallas_call(
        functools.partial(forward_kernel, pairs),
        out_shape=(
            S((rows, D), bf16), S((pairs,), f32), S((rows, 3 * D), bf16), S((rows, D), bf16), S((rows, D), f32), S((rows, D), bf16),
            S((rows, 128), f32), S((rows, 4 * D), bf16), S((rows, 4 * D), bf16), S((rows, D), f32), S((8, D), f32),
        ),
        in_specs=[anywhere] * 6 + [smem] * 2 + [vmem] * 9,
        out_specs=(anywhere, smem) + (anywhere,) * 8 + (vmem,),
        scratch_shapes=[
            V((rows, D), bf16), V((rows, D), bf16), V((D, 3 * D), bf16), V((D, D), bf16), V((D, 4 * D), bf16), V((4 * D, D), bf16), V((1, 3 * D), f32),
            V((rows, 3 * D), bf16), V((rows, D), bf16), V((rows, D), f32), V((rows, D), bf16), V((rows, 128), f32),
            V((4 * D // FFB, rows, FFB), bf16), V((4 * D // FFB, rows, FFB), bf16), V((rows, D), f32), V((rows, 128), f32), V((rows, D), bf16), V((rows, D), f32), V((3, 8, D), f32),
            dma((6,)), dma((6,)), dma((2, 4 * D // FFB)), dma((pairs,)),
        ] + scratch(pairs),
        compiler_params=pltpu.CompilerParams(vmem_limit_bytes=VMEM_LIMIT),
        name="forward",
    )(tokens, cotangent, w_qkv, w_out, w_in, w_down, lengths, dcot, q_bias, v_bias, out_bias, g1, b1, in_bias, down_bias, g2, b2)


def backward_kernel(pairs, ndp, *refs):
    (gsec_hbm, act_hbm, slope_hbm, low1_hbm, hat1_hbm, rstd1_hbm, ctx_hbm, packed_hbm, tok_hbm, wdown_hbm, win_hbm, wout_hbm, wqkv_hbm, len_ref, g1_ref, small2_ref,
     tgrad_hbm, full_hbm, small_out,
     table, total, low, act, slope, wdown, win, gin, lows, hat1, rstd1, packed, wout, wqkv, gatt, gctx, ffs, lns, qs,
     in_sem, ff_sem, out_sem, landing, far, sbuf, sland, *sems) = refs
    first = lax.axis_index("reg") * pairs
    nt = (((1,), (1,)), ((), ()))
    tn = (((0,), (0,)), ((), ()))
    ex = Exchange(ndp, table, full_hbm, landing, far, sbuf, sland, sems)
    count = 4 * D // FFB
    half = BLK // 2
    third = BLK // 3

    def dot(a, b, dims=(((1,), (0,)), ((), ()))):
        return lax.dot_general(a, b, dims, preferred_element_type=f32)

    def fold(x):
        return jnp.sum(x.reshape(x.shape[0] // 8, 8, x.shape[1]), 0)

    def by_pair(body):
        def run(m, carry):
            body(pl.ds(pl.multiple_of(m * SLOT, SLOT), SLOT))
            return carry

        lax.fori_loop(0, pairs, run, 0, unroll=True)

    def ff_loads(j):
        cols = pl.ds(j * FFB, FFB)
        s = j % 2
        parts = ((act_hbm.at[:, cols], act), (slope_hbm.at[:, cols], slope), (wdown_hbm.at[cols, :], wdown), (win_hbm.at[:, cols], win))
        return [pltpu.make_async_copy(src, dst.at[s], ff_sem.at[i, s]) for i, (src, dst) in enumerate(parts)]

    sources = ((gsec_hbm, total), (low1_hbm, lows), (hat1_hbm, hat1), (rstd1_hbm, rstd1), (packed_hbm, packed), (wout_hbm, wout), (wqkv_hbm, wqkv), (ctx_hbm, low), (tok_hbm, lows))
    loads = [pltpu.make_async_copy(src, dst, in_sem.at[i]) for i, (src, dst) in enumerate(sources)]
    loads[0].start()
    for copy in ff_loads(0):
        copy.start()
    ex.barrier()
    for ref in (ffs, lns, qs):
        ref[...] = jnp.zeros_like(ref)
    loads[0].wait()
    for i in range(1, 7):
        loads[i].start()

    def cast_branch(at):
        low[at, :] = total[at, :].astype(bf16)

    by_pair(cast_branch)
    pieces = []

    def piece(took, *made):
        def add(body):
            pieces.append((took, made, body))
            return body

        return add

    def store_table(block, start, value):
        table[block * BLK + start : block * BLK + start + value.shape[0], :] = value.astype(bf16)

    def ff_pieces(j):
        s = j % 2

        @piece(1.2, 4 * j, 4 * j + 1)
        def down():
            for copy in ff_loads(j):
                copy.wait()
            if j + 1 < count:
                for copy in ff_loads(j + 1):
                    copy.start()
            if j == 0:
                loads[1].wait()
            for c in range(3):
                value = dot(act[s], low[:, c * 256 : (c + 1) * 256], tn)
                for i in range(2):
                    g = 2 * c + i
                    store_table(4 * j + g // 3, g % 3 * third, value[:, i * COLS : (i + 1) * COLS])

        @piece(1.15)
        def inner():
            def body(at):
                grad = (dot(low[at, :], wdown[s], nt) * slope[s, at, :].astype(f32)).astype(bf16)
                gin[at, :] = grad
                ffs[j] += fold(grad.astype(f32))

            by_pair(body)

        @piece(1.2, 4 * j + 2, 4 * j + 3)
        def outer():
            for c in range(2):
                value = dot(lows[...], gin[:, c * 256 : (c + 1) * 256], tn)
                for i in range(2):
                    store_table(4 * j + 2 + c, i * half, value[:, i * COLS : (i + 1) * COLS])

        @piece(1.15)
        def back():
            total[...] += dot(gin[...], win[s], nt)

    for j in range(count):
        ff_pieces(j)

    @piece(1.5)
    def norm_back():
        loads[7].start()
        loads[8].start()
        loads[2].wait()
        loads[3].wait()
        gain = g1_ref[...].reshape(1, D)

        def body(at):
            grad = total[at, :]
            hat = hat1[at, :]
            wide = grad * gain
            new = rstd1[at, 0:1] * (wide - jnp.mean(wide, -1, keepdims=True) - hat * jnp.mean(wide * hat, -1, keepdims=True))
            total[at, :] = new
            lowered = new.astype(bf16)
            gatt[at, :] = lowered
            for i, value in enumerate((grad * hat, grad, lowered.astype(f32))):
                lns[i] += fold(value)

        by_pair(body)

    base = 4 * count

    def out_piece(c):
        @piece(0.45, base + c)
        def out():
            if c == 0:
                loads[7].wait()
            value = dot(low[...], gatt[:, c * 256 : (c + 1) * 256], tn)
            for i in range(2):
                store_table(base + c, i * half, value[:, i * COLS : (i + 1) * COLS])

    for c in range(3):
        out_piece(c)

    @piece(2.0)
    def context_back():
        loads[5].wait()
        gctx[...] = dot(gatt[...], wout[...], nt).astype(bf16)

    lane = lax.broadcasted_iota(jnp.int32, (1, 2 * HEAD_DIM), 1)
    scale = HEAD_DIM**-0.5
    left = jnp.where(lane < HEAD_DIM, 1.0, 0.0).astype(bf16)
    right = jnp.where(lane < HEAD_DIM, 0.0, 1.0).astype(bf16)
    slot = lax.broadcasted_iota(jnp.int32, (SLOT, 1), 0)

    def pair_piece(p, part):
        @piece(1.9)
        def attention_back():
            if p == 0 and part == 0:
                loads[4].wait()
            words, regions = len_ref[0, first + p], len_ref[1, first + p]
            shut = jnp.where(jnp.where(slot < WORDS, words, regions + WORDS) > slot, 0.0, -1e30)
            at = slice(p * SLOT, (p + 1) * SLOT)
            for h in range(part * HEADS // 4, (part + 1) * HEADS // 4):
                c = h * 128
                q = packed[at, c : c + 128]
                k = packed[at, D + c : D + c + 128]
                v = packed[at, 2 * D + c : 2 * D + c + 128]
                g = gctx[at, c : c + 128]
                both = jnp.concatenate([q * (left * scale).astype(bf16), q * (right * scale).astype(bf16)], 0)
                grads = jnp.concatenate([g * left, g * right], 0)
                s = dot(k, both, nt) + shut
                e = jnp.exp(s - jnp.max(s, 0, keepdims=True))
                pr = e * (1.0 / jnp.sum(e, 0, keepdims=True))
                gp = dot(v, grads, nt)
                gs = (pr * (gp - jnp.sum(pr * gp, 0, keepdims=True))).astype(bf16)
                gq = dot(gs, k, tn)
                gq = jnp.where(lane < HEAD_DIM, gq[:SLOT], gq[SLOT:]) * scale
                gk = dot(gs, both)
                gv = dot(pr.astype(bf16), grads)
                for i, value in enumerate((gq, gk, gv)):
                    value = value.astype(bf16)
                    packed[at, i * D + c : i * D + c + 128] = value
                    if i != 1:
                        qs[:, i * D + c : i * D + c + 128] += fold(value.astype(f32))

    for p in range(pairs):
        for part in range(2):
            pair_piece(p, part)

    @piece(0.3, NBLK)
    def singles():
        def row(i, value):
            sbuf[i : i + 1, :] = value

        def down(x):
            return jnp.sum(x, 0, keepdims=True)

        row(0, down(qs[:, 0:D]))
        row(1, down(qs[:, 2 * D : 3 * D]))
        row(2, down(lns[2]))
        row(3, down(lns[0]))
        row(4, down(lns[1]))
        row(5, small2_ref[2:3, :])
        row(6, small2_ref[0:1, :])
        row(7, small2_ref[1:2, :])
        for j in range(count):
            at = j * FFB
            value = down(ffs[j])
            while value.shape[1]:
                room = min(D - at % D, value.shape[1])
                sbuf[8 + at // D : 9 + at // D, at % D : at % D + room] = value[:, :room]
                at, value = at + room, value[:, room:]
        sbuf[12:16, :] = jnp.zeros((4, D), f32)

    def qkv_piece(c):
        @piece(0.45, base + 3 + c)
        def qkv():
            if c == 0:
                loads[8].wait()
            value = dot(lows[...], packed[:, c * 256 : (c + 1) * 256], tn)
            for i in range(2):
                store_table(base + 3 + c, i * half, value[:, i * COLS : (i + 1) * COLS])

    for c in range(9):
        qkv_piece(c)

    def token_piece(c):
        @piece(1.5)
        def tokens_back():
            if c == 0:
                loads[6].wait()
            cols = slice(c * D, (c + 1) * D)
            total[...] += dot(packed[:, cols], wqkv[:, cols], nt)
            if c == 2:
                pltpu.make_async_copy(total, tgrad_hbm, out_sem).start()

    for c in range(3):
        token_piece(c)

    for what, block, step, _ in plan([(took, made) for took, made, _ in pieces], ex.extra):
        if what == "piece":
            pieces[block][2]()
        elif what == "start":
            ex.start(block, step)
        else:
            ex.handle(block, step)
    small_out[...] = sbuf[...]
    ex.finish()
    pltpu.make_async_copy(total, tgrad_hbm, out_sem).wait()


def backward(ndp, gsec, act, slope, low1, hat1, rstd1, ctx, packed, tokens, w_down, w_in, w_out, w_qkv, lengths, g1, small2):
    rows = tokens.shape[0]
    pairs = rows // SLOT
    anywhere = pl.BlockSpec(memory_space=pl.ANY)
    vmem = pl.BlockSpec(memory_space=pltpu.VMEM)
    smem = pl.BlockSpec(memory_space=pltpu.SMEM)
    S = jax.ShapeDtypeStruct
    V = pltpu.VMEM
    dma = pltpu.SemaphoreType.DMA
    return pl.pallas_call(
        functools.partial(backward_kernel, pairs, ndp),
        out_shape=(S((rows, D), f32), S((NBLK * BLK, COLS), bf16), S((16, D), f32)),
        in_specs=[anywhere] * 13 + [smem] + [vmem] * 2,
        out_specs=(anywhere, anywhere, vmem),
        scratch_shapes=[
            V((NBLK * BLK, COLS), bf16), V((rows, D), f32), V((rows, D), bf16), V((2, rows, FFB), bf16), V((2, rows, FFB), bf16), V((2, FFB, D), bf16), V((2, D, FFB), bf16),
            V((rows, FFB), bf16), V((rows, D), bf16), V((rows, D), f32), V((rows, 128), f32), V((rows, 3 * D), bf16), V((D, D), bf16), V((D, 3 * D), bf16),
            V((rows, D), bf16), V((rows, D), bf16), V((4 * D // FFB, 8, FFB), f32), V((3, 8, D), f32), V((8, 3 * D), f32),
            dma((9,)), dma((4, 2)), dma,
        ] + exchange_scratch(ndp),
        compiler_params=pltpu.CompilerParams(collective_id=1, has_side_effects=True, vmem_limit_bytes=VMEM_LIMIT),
        name="backward",
    )(gsec, act, slope, low1, hat1, rstd1, ctx, packed, tokens, w_down, w_in, w_out, w_qkv, lengths, g1, small2)


WIDE = (192, 384, 128, 512)


def widen_units():
    units = [(3, FFB * j + r, r, 12 * j) for j in range(6) for r in range(0, FFB, WIDE[3])]
    units += [(2, r, r, 0) for r in range(0, D, WIDE[2])]
    units += [(0, r, r, 54) for r in range(0, D, WIDE[0])]
    units += [(1, r, r, 48) for r in range(0, D, WIDE[1])]
    return units


def widen_kernel(depth, thirds, halves, eighths, small, tgrad, *refs):
    outs, singles, tgrad_out = refs[0:4], refs[4:13], refs[13]
    narrow, wide, held, in_sem, out_sem, own_sem = refs[14:18], refs[18:22], refs[22], refs[23], refs[24], refs[25]
    units = widen_units()
    take = pltpu.make_async_copy(tgrad, held, own_sem.at[0])
    move = pltpu.make_async_copy(held, tgrad_out, own_sem.at[1])

    def into(u):
        which, _, row, at = units[u]
        dst = narrow[which].at[u % depth]
        rows = pl.ds(row, WIDE[which])
        if which == 2:
            src = eighths.at[0:6, 4:8, rows]
        elif which == 3:
            src = thirds.at[pl.ds(at, 6), rows]
        else:
            src = halves.at[pl.ds(at, 18 if which == 0 else 6), rows]
        return pltpu.make_async_copy(src, dst, in_sem.at[u % depth])

    def back(u):
        which, row, _, _ = units[u]
        return pltpu.make_async_copy(wide[which].at[u % depth], outs[which].at[pl.ds(row, WIDE[which])], out_sem.at[u % depth])

    for u in range(depth - 1):
        into(u).start()
    for i in range(8):
        singles[i][...] = small[i, :]
    singles[8][...] = jnp.concatenate([small[i : i + 1, :] for i in range(8, 12)], 1).reshape(4 * D)
    for v in range(len(units)):
        if v + depth - 1 < len(units):
            into(v + depth - 1).start()
        if v == 0:
            take.start()
        if v == 4:
            take.wait()
            move.start()
        into(v).wait()
        if v >= depth:
            back(v - depth).wait()
        which, s = units[v][0], v % depth
        for c in range(wide[which].shape[2] // COLS):
            piece = narrow[which][s, c // 4, c % 4] if which == 2 else narrow[which][s, c]
            wide[which][s, :, c * COLS : (c + 1) * COLS] = piece.astype(f32)
        back(v).start()
    for v in range(len(units) - depth, len(units)):
        back(v).wait()
    move.wait()


def unpack_table(table, small, tgrad):
    anywhere = pl.BlockSpec(memory_space=pl.ANY)
    vmem = pl.BlockSpec(memory_space=pltpu.VMEM)
    depth = 3
    S = jax.ShapeDtypeStruct
    V = pltpu.VMEM
    dma = pltpu.SemaphoreType.DMA
    return pl.pallas_call(
        functools.partial(widen_kernel, depth),
        out_shape=(S((D, 3 * D), f32), S((D, D), f32), S((D, 4 * D), f32), S((4 * D, D), f32)) + (S((D,), f32),) * 8 + (S((4 * D,), f32), S(tgrad.shape, f32)),
        in_specs=[anywhere] * 3 + [vmem, anywhere],
        out_specs=(anywhere,) * 4 + (vmem,) * 9 + (anywhere,),
        scratch_shapes=[
            V((depth, 18, WIDE[0], COLS), bf16), V((depth, 6, WIDE[1], COLS), bf16), V((depth, 6, 4, WIDE[2], COLS), bf16), V((depth, 6, WIDE[3], COLS), bf16),
            V((depth, WIDE[0], 3 * D), f32), V((depth, WIDE[1], D), f32), V((depth, WIDE[2], 4 * D), f32), V((depth, WIDE[3], D), f32), V(tgrad.shape, f32),
            dma((depth,)), dma((depth,)), dma((2,)),
        ],
        compiler_params=pltpu.CompilerParams(vmem_limit_bytes=VMEM_LIMIT),
        name="widen",
    )(table.reshape(108, 512, COLS), table.reshape(72, D, COLS), table.reshape(9, 8, D, COLS), small, tgrad)


def on_device(ndp, tokens, cotangent, distance_cot, lengths, w_qkv, q_bias, v_bias, w_out, out_bias, ln1_gain, ln1_bias, w_in, in_bias, w_down, down_bias, ln2_gain, ln2_bias):
    sizes = jnp.transpose(lengths)
    result, distance, packed, ctx, hat1, low1, rstd1, act, slope, gsec, small2 = forward(
        tokens, cotangent, distance_cot, sizes, w_qkv, q_bias, v_bias, w_out, out_bias, ln1_gain, ln1_bias, w_in, in_bias, w_down, down_bias, ln2_gain, ln2_bias
    )
    grad_tokens, table, small = backward(ndp, gsec, act, slope, low1, hat1, rstd1, ctx, packed, tokens, w_down, w_in, w_out, w_qkv, sizes, ln1_gain, small2)
    g_qkv, g_out, g_in, g_down, g_qb, g_vb, g_ob, g_g1, g_b1, g_db, g_g2, g_b2, g_ib, grad_tokens = unpack_table(table, small, grad_tokens)
    return result, distance, grad_tokens, g_qkv, g_qb, g_vb, g_out, g_ob, g_g1, g_b1, g_in, g_ib, g_down, g_db, g_g2, g_b2


def solution(mesh):
    rows = P(("dp", "reg"), None)
    return jax.shard_map(
        functools.partial(on_device, mesh.shape["dp"]),
        mesh=mesh,
        in_specs=(rows, rows, P("dp"), P("dp", None)) + (P(),) * 13,
        out_specs=(rows, P(("dp", "reg")), rows) + (P(),) * 13,
        check_vma=False,
    )
```

```python
import functools
import heapq
import itertools
import math

import jax
import jax.numpy as jnp
from jax import lax
from jax.experimental import pallas as pl
from jax.experimental.pallas import tpu as pltpu
from jax.sharding import PartitionSpec as P

D = 768
HEADS = 12
HEAD_DIM = 64
WORDS = 64
REGIONS = 128
SLOT = WORDS + REGIONS
ITERS = 50
EPS = 1e-06
f32 = jnp.float32
bf16 = jnp.bfloat16
MESH = pl.DeviceIdType.MESH
VMEM_LIMIT = 62 * 2**20

BLK = 1536
COLS = 128
FFB = 512
NBLK = 36
HALVES = 5
RBLK = BLK - (BLK >> HALVES)
ORDERS = (
    ("c", "x", "y", "z0", "z1"),
    ("c", "y", "x", "z0", "z1"),
    ("c", "z0", "x", "y", "z1"),
    ("c", "z0", "y", "x", "z1"),
    ("c", "x", "z0", "y", "z1"),
    ("c", "y", "z0", "x", "z1"),
    ("c", "z0", "z1", "x", "y"),
    ("c", "z0", "z1", "y", "x"),
)
TAKES = (5, 4, 0, 5, 4, 1, 4, 4, 1, 3, 1, 0, 1, 5, 2, 0, 5, 0, 1, 5, 0, 1, 0, 0, 0, 0, 2, 1, 5, 0, 3, 3, 3, 5, 4, 4)


def order_of(block):
    return ORDERS[TAKES[block]]


def plan(pieces, extra, rate=80e3, core_rate=450e3, delay=2.4, ahead=3.0, add=0.075):
    last = 2 * HALVES + extra - 1
    block_bytes = BLK * COLS * 2
    lines = ("c", "x", "y", "z", "far")
    free = dict.fromkeys(lines, 0.0)
    waiting = {line: [] for line in lines}
    arrivals = []
    steps = []
    ticket = itertools.count()
    now = 0.0

    def facts(block, step):
        if block == NBLK:
            return ("c", "x", "y", "z0", "z1")[step] if step < HALVES else "far", 16 * D * 4
        if step < HALVES:
            return order_of(block)[step], block_bytes >> (step + 1)
        if step < HALVES + extra:
            return "far", block_bytes >> HALVES
        return order_of(block)[last - step], block_bytes >> (last - step + 1)

    def ask(block, step):
        name = facts(block, step)[0]
        line = "z" if name in ("z0", "z1") else name
        heapq.heappush(waiting[line], (step >= HALVES and block < NBLK, next(ticket), block, step))

    index = 0
    while index < len(pieces) or arrivals or any(waiting.values()):
        if arrivals and (arrivals[0][0] <= now or index == len(pieces)):
            at, _, block, step = heapq.heappop(arrivals)
            now = max(now, at) + 0.05
            if block < NBLK and step < HALVES:
                now += add / 2**step
            steps.append(("handle", block, step, now))
            if step < (HALVES + extra - 1 if block == NBLK else last):
                ask(block, step + 1)
        else:
            took, made = pieces[index]
            now += took
            steps.append(("piece", index, 0, now))
            for block in made:
                ask(block, 0)
            index += 1
        for line, queue in waiting.items():
            while queue and free[line] - now < ahead:
                _, _, block, step = heapq.heappop(queue)
                name, sent = facts(block, step)
                took = sent / core_rate if name == "c" else 2 * sent / rate
                free[line] = max(now, free[line]) + took
                heapq.heappush(arrivals, (free[line] + (took if name == "z1" else 0.0) + delay, next(ticket), block, step))
                steps.append(("start", block, step, now))
    return steps


def mesh_partners(ndp):
    dp = lax.axis_index("dp")
    reg = lax.axis_index("reg")
    names = [("c", "reg", 1), ("x", "reg", 2), ("y", "dp", 1), ("z0", "dp", 2), ("z1", "dp", 4)]
    step = 8
    while step < ndp:
        names.append(("far%d" % step, "dp", step))
        step *= 2
    partners = {}
    for name, axis, step in names:
        at = reg if axis == "reg" else dp
        bit = lax.rem(at // step, 2)
        other = at + step - 2 * step * bit
        partners[name] = (bit, (dp, other) if axis == "reg" else (other, reg))
    return partners


class Exchange:
    def __init__(self, ndp, table, full, landing, far, small, small_in, sems):
        self.partners = mesh_partners(ndp)
        self.fars = [name for name in self.partners if name.startswith("far")]
        self.extra = len(self.fars)
        self.table, self.full, self.landing, self.far = table, full, landing, far
        self.small, self.small_in = small, small_in
        self.rs_send, self.rs_recv, self.ag_send, self.ag_recv, self.far_send, self.far_recv, self.sm_send, self.sm_recv, self.own = sems

    def barrier(self):
        bar = pltpu.get_barrier_semaphore()
        for _, who in self.partners.values():
            pl.semaphore_signal(bar, inc=1, device_id=who, device_id_type=MESH)
        pl.semaphore_wait(bar, len(self.partners))

    def offset(self, block, steps):
        at, size = block * BLK, BLK
        for step in range(steps):
            size //= 2
            at = at + self.partners[order_of(block)[step]][0] * size
        return pl.multiple_of(at, 16) if steps else at

    def halving(self, block, step):
        bit, who = self.partners[order_of(block)[step]]
        size = BLK >> (step + 1)
        src = pl.multiple_of(self.offset(block, step) + (1 - bit) * size, 16)
        land = block * RBLK + (BLK - (BLK >> step))
        return pltpu.make_async_remote_copy(
            self.table.at[pl.ds(src, size)],
            self.landing.at[pl.ds(land, size)],
            self.rs_send.at[block, step],
            self.rs_recv.at[block, step],
            device_id=who,
            device_id_type=MESH,
        )

    def far_step(self, block, index):
        _, who = self.partners[self.fars[index]]
        size = BLK >> HALVES
        src = self.offset(block, HALVES)
        return pltpu.make_async_remote_copy(
            self.table.at[pl.ds(src, size)],
            self.far.at[block, index],
            self.far_send.at[block, index],
            self.far_recv.at[block, index],
            device_id=who,
            device_id_type=MESH,
        )

    def image(self, block, steps):
        at = self.offset(block, steps) - self.offset(block, 1) + block * RBLK
        return self.landing.at[pl.ds(pl.multiple_of(at, 16), BLK >> steps)]

    def returning(self, block, step):
        _, who = self.partners[order_of(block)[step]]
        own = pl.ds(self.offset(block, step + 1), BLK >> (step + 1))
        return pltpu.make_async_remote_copy(
            self.table.at[own] if step + 1 == HALVES else self.image(block, step + 1),
            self.image(block, step + 1) if step else self.full.at[own],
            self.ag_send.at[block, step],
            self.ag_recv.at[block, step],
            device_id=who,
            device_id_type=MESH,
        )

    def keep(self, block):
        at = pl.ds(self.offset(block, HALVES), BLK >> HALVES)
        return pltpu.make_async_copy(self.table.at[at], self.image(block, HALVES), self.own.at[block, 0])

    def place(self, block):
        at = pl.ds(self.offset(block, 1), BLK // 2)
        return pltpu.make_async_copy(self.image(block, 1), self.full.at[at], self.own.at[block, 1])

    def start(self, block, step):
        if block == NBLK:
            self.small_copy(step).start()
        elif step < HALVES:
            self.halving(block, step).start()
        elif step < HALVES + self.extra:
            self.far_step(block, step - HALVES).start()
        else:
            back = 2 * HALVES + self.extra - 1 - step
            if back + 1 == HALVES:
                self.keep(block).start()
            self.returning(block, back).start()
            if back == 0:
                self.place(block).start()

    def handle(self, block, event):
        if block == NBLK:
            self.small_handle(event)
            return
        if event < HALVES:
            self.halving(block, event).wait_recv()
            size = BLK >> (event + 1)
            off = self.offset(block, event + 1)
            land = block * RBLK + (BLK - (BLK >> event))
            rows = min(size, 192)

            def add(index, carry):
                at = pl.ds(pl.multiple_of(off + index * rows, 16), rows)
                self.table[at, :] += self.landing[pl.ds(pl.multiple_of(land + index * rows, 16), rows), :]
                return carry

            lax.fori_loop(0, size // rows, add, 0)
        elif event < HALVES + self.extra:
            index = event - HALVES
            copy = self.far_step(block, index)
            copy.wait()
            at = pl.ds(self.offset(block, HALVES), BLK >> HALVES)
            self.table[at, :] += self.far[block, index]
        else:
            back = 2 * HALVES + self.extra - 1 - event
            self.returning(block, back).wait_recv()
            if back + 1 == HALVES:
                self.keep(block).wait()

    def small_copy(self, index):
        _, who = self.partners[list(self.partners)[index]]
        return pltpu.make_async_remote_copy(
            self.small,
            self.small_in.at[index],
            self.sm_send.at[index],
            self.sm_recv.at[index],
            device_id=who,
            device_id_type=MESH,
        )

    def small_handle(self, index):
        self.small_copy(index).wait()
        self.small[...] = self.small[...] + self.small_in[index]

    def finish(self):
        for block in range(NBLK):
            for step in range(HALVES):
                self.halving(block, step).wait_send()
                self.returning(block, step).wait_send()
            self.place(block).wait()


def exchange_scratch(ndp):
    extra = max(int(math.log2(ndp)) - 3, 0)
    count = HALVES + extra
    dma = pltpu.SemaphoreType.DMA
    return [
        pltpu.VMEM((NBLK * RBLK, COLS), bf16),
        pltpu.VMEM((NBLK, max(extra, 1), BLK >> HALVES, COLS), bf16),
        pltpu.VMEM((16, D), f32),
        pltpu.VMEM((count, 16, D), f32),
        dma((NBLK, HALVES)),
        dma((NBLK, HALVES)),
        dma((NBLK, HALVES)),
        dma((NBLK, HALVES)),
        dma((NBLK, max(extra, 1))),
        dma((NBLK, max(extra, 1))),
        dma((count,)),
        dma((count,)),
        dma((NBLK, 2)),
    ]


def align_body(pairs, first, rows_ref, len_ref, dcot_ref, emit, dist_ref, kern, trans, uhist, acur, acc, alpha, gamma, cosr):
    P = range(pairs)
    eye = lax.broadcasted_iota(jnp.int32, (REGIONS, REGIONS), 0) == lax.broadcasted_iota(jnp.int32, (REGIONS, REGIONS), 1)
    wcol = lax.broadcasted_iota(jnp.int32, (WORDS, 1), 0)
    rrow = lax.broadcasted_iota(jnp.int32, (1, REGIONS), 1)
    nlen = [len_ref[0, first + p] for p in P]
    mlen = [len_ref[1, first + p] for p in P]
    nf = [v.astype(f32) for v in nlen]
    mf = [v.astype(f32) for v in mlen]
    dc = [dcot_ref[first + p] for p in P]
    wv = [(wcol < nlen[p]).astype(f32) for p in P]
    rv = [(rrow < mlen[p]).astype(f32) for p in P]
    rxs, rys, starts = [], [], []
    for p in P:
        x = rows_ref[SLOT * p:SLOT * p + WORDS, :]
        y = rows_ref[SLOT * p + WORDS:SLOT * (p + 1), :]
        xf, yf = x.astype(f32), y.astype(f32)
        rx = lax.rsqrt(jnp.sum(xf * xf, -1, keepdims=True) + EPS)
        ry = lax.rsqrt(jnp.sum(yf * yf, -1, keepdims=True) + EPS)
        ryr = jnp.sum(jnp.where(eye, ry, 0.0), 0, keepdims=True)
        rxs.append(rx); rys.append((ry, ryr))
        cos = lax.dot_general(x, y, (((1,), (1,)), ((), ())), preferred_element_type=f32) * rx * ryr
        joint = wv[p] * rv[p]
        cost = (1.0 - cos) * joint
        cosr[p] = cos
        kernel = jnp.exp(-2.0 * cost) * joint
        kern[p] = kernel
        trans[p] = kernel * joint
        starts.append(jnp.sum(kernel * joint * (wv[p] / nf[p]), 0, keepdims=True))
        acur[p] = jnp.broadcast_to(wv[p] / nf[p], (WORDS, REGIONS))
        uhist[0, p] = jnp.where(rrow == 0, wv[p], 0.0)
    def fwd(t, s):
        joined = [trans[p] for p in P]
        b = [rv[p] / (mf[p] * s[p] + (1.0 - rv[p])) for p in P]
        u = [joined[p] * b[p] for p in P]
        w = [jnp.sum(u[p], 1, keepdims=True) for p in P]
        ku = [kern[p] * u[p] for p in P]
        an = [wv[p] / (nf[p] * w[p] + (1.0 - wv[p])) for p in P]
        later = [ku[p] * an[p] for p in P]
        for p in P:
            uhist[t + 1, p] = u[p]
            acur[p] = jnp.broadcast_to(an[p], (WORDS, REGIONS))
            trans[p] = later[p]
        return tuple(jnp.sum(later[p] * an[p], 0, keepdims=True) for p in P)
    lax.fori_loop(0, ITERS, fwd, tuple(starts))
    for p in P:
        trans[p] = uhist[ITERS, p] * acur[p]
    cols = []
    for p in P:
        joint = wv[p] * rv[p]
        cost = (1.0 - cosr[p]) * joint
        tc = trans[p] * cost
        dist_ref[p] = jnp.sum(tc)
        g = tc * dc[p]
        cols.append(jnp.sum(g, 0, keepdims=True))
        alpha[p] = jnp.broadcast_to(jnp.sum(g, 1, keepdims=True), (WORDS, REGIONS))
        gamma[p] = jnp.zeros((WORDS, REGIONS), f32)
        acc[p] = float(ITERS) * g
    def bwd(i, cols):
        t = ITERS - i
        tf = t.astype(f32)
        u = [uhist[t, p] for p in P]
        before = [uhist[t - 1, p] for p in P]
        x = [alpha[p] * (nf[p] * acur[p]) for p in P]
        ap = [wv[p] / (nf[p] * jnp.sum(before[p], 1, keepdims=True) + (1.0 - wv[p])) for p in P]
        y = [mf[p] * ap[p] for p in P]
        beta = [cols[p] - jnp.sum(u[p] * x[p], 0, keepdims=True) for p in P]
        ub = [u[p] * beta[p] for p in P]
        gm = [jnp.broadcast_to(-y[p] * jnp.sum(ub[p], 1, keepdims=True), (WORDS, REGIONS)) for p in P]
        go = [gamma[p] for p in P]
        ac = [acc[p] for p in P]
        for p in P:
            acc[p] = ac[p] - tf * (u[p] * x[p] + y[p] * ub[p])
            alpha[p] = 2.0 * gm[p] - go[p]
            gamma[p] = gm[p]
            acur[p] = jnp.broadcast_to(ap[p], (WORDS, REGIONS))
        return tuple(jnp.zeros_like(c) for c in cols)
    lax.fori_loop(0, ITERS, bwd, tuple(cols))
    for p in P:
        x = rows_ref[SLOT * p:SLOT * p + WORDS, :]
        y = rows_ref[SLOT * p + WORDS:SLOT * (p + 1), :]
        rx = rxs[p]; ry, ryr = rys[p]
        gc = dc[p] * trans[p] - 2.0 * acc[p]
        gcos = gc * cosr[p]
        m = gc * rx * ryr
        hi = m.astype(bf16)
        lo = (m - hi.astype(f32)).astype(bf16)
        nt = (((1,), (0,)), ((), ())); tn = (((0,), (0,)), ((), ()))
        gx = lax.dot_general(hi, y, nt, preferred_element_type=f32) + lax.dot_general(lo, y, nt, preferred_element_type=f32)
        gy = lax.dot_general(hi, x, tn, preferred_element_type=f32) + lax.dot_general(lo, x, tn, preferred_element_type=f32)
        sx = rx * rx * jnp.sum(gcos, 1, keepdims=True)
        sy = ry * ry * jnp.sum(jnp.where(eye, jnp.sum(gcos, 0, keepdims=True), 0.0), 1, keepdims=True)
        emit(p, pl.ds(SLOT * p, WORDS), sx * x.astype(f32) - gx)
        emit(p, pl.ds(SLOT * p + WORDS, REGIONS), sy * y.astype(f32) - gy)

def scratch(pairs):
    v = lambda *s: pltpu.VMEM(s, f32)
    W = (WORDS, REGIONS)
    return [v(pairs, *W), v(pairs, *W), v(ITERS + 1, pairs, *W), v(pairs, *W), v(pairs, *W), v(pairs, *W), v(pairs, *W), v(pairs, *W)]


def forward_kernel(pairs, *refs):
    (tok_hbm, cot_hbm, wqkv_hbm, wout_hbm, win_hbm, wdown_hbm, len_ref, dcot_ref, qb_ref, vb_ref, ob_ref, g1_ref, b1_ref, ib_ref, db_ref, g2_ref, b2_ref,
     out_hbm, dist_ref, packed_hbm, ctx_hbm, hat1_hbm, low1_hbm, rstd1_hbm, act_hbm, slope_hbm, gsec_hbm, small_ref,
     tok, cot, wqkv, wout, win, wdown, qkvb, packed, ctx, hat1, low1, rstd1, actb, slopeb, hat2, rstd2, outv, gsec, sums,
     in_sem, out_sem, ff_sem, pair_sem, *align_refs) = refs
    rows = pairs * SLOT
    first = lax.axis_index("reg") * pairs
    loads = [
        pltpu.make_async_copy(src, dst, in_sem.at[i])
        for i, (src, dst) in enumerate(((tok_hbm, tok), (wqkv_hbm, wqkv), (wout_hbm, wout), (win_hbm, win), (wdown_hbm, wdown), (cot_hbm, cot)))
    ]
    loads[0].start()
    loads[1].start()
    stores = [
        pltpu.make_async_copy(src, dst, out_sem.at[i])
        for i, (src, dst) in enumerate(((packed, packed_hbm), (ctx, ctx_hbm), (hat1, hat1_hbm), (low1, low1_hbm), (rstd1, rstd1_hbm), (outv, out_hbm)))
    ]
    qkvb[:, 0:D] = qb_ref[...].reshape(1, D)
    qkvb[:, D : 2 * D] = jnp.zeros((1, D), f32)
    qkvb[:, 2 * D :] = vb_ref[...].reshape(1, D)
    sums[...] = jnp.zeros_like(sums)

    loads[0].wait()
    loads[1].wait()
    for load in loads[2:]:
        load.start()

    def project(n, carry):
        cols = pl.ds(pl.multiple_of(n * D, D), D)
        packed[:, cols] = (jnp.dot(tok[...], wqkv[:, cols], preferred_element_type=f32) + qkvb[:, cols]).astype(bf16)
        return carry

    lax.fori_loop(0, 3, project, 0)
    stores[0].start()
    loads[2].wait()

    lane = lax.broadcasted_iota(jnp.int32, (1, 2 * HEAD_DIM), 1)
    left = jnp.where(lane < HEAD_DIM, HEAD_DIM**-0.5, 0.0).astype(bf16)
    right = jnp.where(lane < HEAD_DIM, 0.0, HEAD_DIM**-0.5).astype(bf16)
    slot = lax.broadcasted_iota(jnp.int32, (1, SLOT), 1)
    nt = (((1,), (1,)), ((), ()))

    def attend(p, carry):
        at = pl.ds(pl.multiple_of(p * SLOT, SLOT), SLOT)
        words, regions = len_ref[0, first + p], len_ref[1, first + p]
        shut = jnp.where(jnp.where(slot < WORDS, words, regions + WORDS) > slot, 0.0, -1e30)
        for h in range(HEADS // 2):
            c = h * 2 * HEAD_DIM
            q = packed[at, c : c + 128]
            k = packed[at, D + c : D + c + 128]
            v = packed[at, 2 * D + c : 2 * D + c + 128]
            both = jnp.concatenate([q * left, q * right], 0)
            s = lax.dot_general(both, k, nt, preferred_element_type=f32) + shut
            e = jnp.exp(s - jnp.max(s, -1, keepdims=True))
            pr = (e / jnp.sum(e, -1, keepdims=True)).astype(bf16)
            o = jnp.dot(pr, v, preferred_element_type=f32)
            ctx[at, c : c + 128] = jnp.where(lane < HEAD_DIM, o[:SLOT], o[SLOT:]).astype(bf16)
        return carry

    lax.fori_loop(0, pairs, attend, 0, unroll=True)
    stores[1].start()

    def norm(p, carry):
        at = pl.ds(pl.multiple_of(p * SLOT, SLOT), SLOT)
        hidden = tok[at, :].astype(f32) + (jnp.dot(ctx[at, :], wout[...], preferred_element_type=f32) + ob_ref[...].reshape(1, D))
        center = hidden - jnp.mean(hidden, -1, keepdims=True)
        rstd = lax.rsqrt(jnp.mean(center * center, -1, keepdims=True) + EPS)
        hat = center * rstd
        hat1[at, :] = hat
        rstd1[at, :] = jnp.broadcast_to(rstd, (SLOT, 128))
        low1[at, :] = (hat * g1_ref[...].reshape(1, D) + b1_ref[...].reshape(1, D)).astype(bf16)
        return carry

    lax.fori_loop(0, pairs, norm, 0, unroll=True)
    for i in range(2, 5):
        stores[i].start()
    loads[3].wait()
    loads[4].wait()

    count = 4 * D // FFB

    def ff_copies(j, slot_at):
        cols = pl.ds(pl.multiple_of(j * FFB, FFB), FFB)
        return (
            pltpu.make_async_copy(actb.at[slot_at], act_hbm.at[:, cols], ff_sem.at[0, slot_at]),
            pltpu.make_async_copy(slopeb.at[slot_at], slope_hbm.at[:, cols], ff_sem.at[1, slot_at]),
        )

    for j in range(count):
        slot_at = j
        cols = slice(j * FFB, (j + 1) * FFB)

        def part(m, carry):
            at = pl.ds(pl.multiple_of(m * SLOT, SLOT), SLOT)
            inner = jnp.dot(low1[at, :], win[:, cols], preferred_element_type=f32) + ib_ref[cols].reshape(1, FFB)
            cdf = 0.5 + 0.5 * lax.erf(inner * (2.0**-0.5))
            actb[slot_at, at, :] = (inner * cdf).astype(bf16)
            slopeb[slot_at, at, :] = (cdf + inner * (jnp.exp(inner * inner * -0.5) * ((2.0 * math.pi) ** -0.5))).astype(bf16)
            return carry

        lax.fori_loop(0, pairs, part, 0, unroll=True)
        for copy in ff_copies(j, slot_at):
            copy.start()
        more = jnp.dot(actb[slot_at], wdown[cols, :], preferred_element_type=f32)
        if j == 0:
            hat2[...] = more
        else:
            hat2[...] += more

    def second(m, carry):
        at = pl.ds(pl.multiple_of(m * SLOT, SLOT), SLOT)
        normed = hat1[at, :] * g1_ref[...].reshape(1, D) + b1_ref[...].reshape(1, D)
        hidden = normed + (hat2[at, :] + db_ref[...].reshape(1, D))
        center = hidden - jnp.mean(hidden, -1, keepdims=True)
        rstd = lax.rsqrt(jnp.mean(center * center, -1, keepdims=True) + EPS)
        hat = center * rstd
        hat2[at, :] = hat
        rstd2[at, :] = jnp.broadcast_to(rstd, (SLOT, 128))
        outv[at, :] = (hat * g2_ref[...].reshape(1, D) + b2_ref[...].reshape(1, D)).astype(bf16)
        return carry

    lax.fori_loop(0, pairs, second, 0, unroll=True)
    stores[5].start()
    loads[5].wait()

    def fold(x):
        return jnp.sum(x.reshape(x.shape[0] // 8, 8, D), 0)

    def gsec_copy(p):
        at = pl.ds(p * SLOT, SLOT)
        return pltpu.make_async_copy(gsec.at[at], gsec_hbm.at[at], pair_sem.at[p])

    def emit(p, at, grad):
        total = cot[at, :].astype(f32) + grad
        hat = hat2[at, :]
        sums[0] += fold(total * hat)
        sums[1] += fold(total)
        wide = total * g2_ref[...].reshape(1, D)
        mean = jnp.mean(wide, -1, keepdims=True)
        slope = jnp.mean(wide * hat, -1, keepdims=True)
        grad = rstd2[at, 0:1] * (wide - mean - hat * slope)
        gsec[at, :] = grad
        sums[2] += fold(grad.astype(bf16).astype(f32))
        if at.start % SLOT:
            gsec_copy(p).start()

    align_body(pairs, first, outv, len_ref, dcot_ref, emit, dist_ref, *align_refs)
    for i in range(3):
        small_ref[i : i + 1, :] = jnp.sum(sums[i], 0, keepdims=True)
    small_ref[3:, :] = jnp.zeros((5, D), f32)
    for j in range(count):
        for copy in ff_copies(j, j):
            copy.wait()
    for store in stores:
        store.wait()
    for p in range(pairs):
        gsec_copy(p).wait()


def forward(tokens, cotangent, dcot, lengths, w_qkv, q_bias, v_bias, w_out, out_bias, g1, b1, w_in, in_bias, w_down, down_bias, g2, b2):
    rows = tokens.shape[0]
    pairs = rows // SLOT
    anywhere = pl.BlockSpec(memory_space=pl.ANY)
    vmem = pl.BlockSpec(memory_space=pltpu.VMEM)
    smem = pl.BlockSpec(memory_space=pltpu.SMEM)
    S = jax.ShapeDtypeStruct
    V = pltpu.VMEM
    dma = pltpu.SemaphoreType.DMA
    return pl.pallas_call(
        functools.partial(forward_kernel, pairs),
        out_shape=(
            S((rows, D), bf16), S((pairs,), f32), S((rows, 3 * D), bf16), S((rows, D), bf16), S((rows, D), f32), S((rows, D), bf16),
            S((rows, 128), f32), S((rows, 4 * D), bf16), S((rows, 4 * D), bf16), S((rows, D), f32), S((8, D), f32),
        ),
        in_specs=[anywhere] * 6 + [smem] * 2 + [vmem] * 9,
        out_specs=(anywhere, smem) + (anywhere,) * 8 + (vmem,),
        scratch_shapes=[
            V((rows, D), bf16), V((rows, D), bf16), V((D, 3 * D), bf16), V((D, D), bf16), V((D, 4 * D), bf16), V((4 * D, D), bf16), V((1, 3 * D), f32),
            V((rows, 3 * D), bf16), V((rows, D), bf16), V((rows, D), f32), V((rows, D), bf16), V((rows, 128), f32),
            V((4 * D // FFB, rows, FFB), bf16), V((4 * D // FFB, rows, FFB), bf16), V((rows, D), f32), V((rows, 128), f32), V((rows, D), bf16), V((rows, D), f32), V((3, 8, D), f32),
            dma((6,)), dma((6,)), dma((2, 4 * D // FFB)), dma((pairs,)),
        ] + scratch(pairs),
        compiler_params=pltpu.CompilerParams(vmem_limit_bytes=VMEM_LIMIT),
        name="forward",
    )(tokens, cotangent, w_qkv, w_out, w_in, w_down, lengths, dcot, q_bias, v_bias, out_bias, g1, b1, in_bias, down_bias, g2, b2)


def backward_kernel(pairs, ndp, *refs):
    (gsec_hbm, act_hbm, slope_hbm, low1_hbm, hat1_hbm, rstd1_hbm, ctx_hbm, packed_hbm, tok_hbm, wdown_hbm, win_hbm, wout_hbm, wqkv_hbm, len_ref, g1_ref, small2_ref,
     tgrad_hbm, full_hbm, small_out,
     table, total, low, act, slope, wdown, win, gin, lows, hat1, rstd1, packed, wout, wqkv, gatt, gctx, ffs, lns, qs,
     in_sem, ff_sem, out_sem, landing, far, sbuf, sland, *sems) = refs
    first = lax.axis_index("reg") * pairs
    nt = (((1,), (1,)), ((), ()))
    tn = (((0,), (0,)), ((), ()))
    ex = Exchange(ndp, table, full_hbm, landing, far, sbuf, sland, sems)
    count = 4 * D // FFB
    half = BLK // 2
    third = BLK // 3

    def dot(a, b, dims=(((1,), (0,)), ((), ()))):
        return lax.dot_general(a, b, dims, preferred_element_type=f32)

    def fold(x):
        return jnp.sum(x.reshape(x.shape[0] // 8, 8, x.shape[1]), 0)

    def by_pair(body):
        def run(m, carry):
            body(pl.ds(pl.multiple_of(m * SLOT, SLOT), SLOT))
            return carry

        lax.fori_loop(0, pairs, run, 0, unroll=True)

    def ff_loads(j):
        cols = pl.ds(j * FFB, FFB)
        s = j % 2
        parts = ((act_hbm.at[:, cols], act), (slope_hbm.at[:, cols], slope), (wdown_hbm.at[cols, :], wdown), (win_hbm.at[:, cols], win))
        return [pltpu.make_async_copy(src, dst.at[s], ff_sem.at[i, s]) for i, (src, dst) in enumerate(parts)]

    sources = ((gsec_hbm, total), (low1_hbm, lows), (hat1_hbm, hat1), (rstd1_hbm, rstd1), (packed_hbm, packed), (wout_hbm, wout), (wqkv_hbm, wqkv), (ctx_hbm, low), (tok_hbm, lows))
    loads = [pltpu.make_async_copy(src, dst, in_sem.at[i]) for i, (src, dst) in enumerate(sources)]
    loads[0].start()
    for copy in ff_loads(0):
        copy.start()
    ex.barrier()
    for ref in (ffs, lns, qs):
        ref[...] = jnp.zeros_like(ref)
    loads[0].wait()
    for i in range(1, 7):
        loads[i].start()

    def cast_branch(at):
        low[at, :] = total[at, :].astype(bf16)

    by_pair(cast_branch)
    pieces = []

    def piece(took, *made):
        def add(body):
            pieces.append((took, made, body))
            return body

        return add

    def store_table(block, start, value):
        table[block * BLK + start : block * BLK + start + value.shape[0], :] = value.astype(bf16)

    def ff_pieces(j):
        s = j % 2

        @piece(1.2, 4 * j, 4 * j + 1)
        def down():
            for copy in ff_loads(j):
                copy.wait()
            if j + 1 < count:
                for copy in ff_loads(j + 1):
                    copy.start()
            if j == 0:
                loads[1].wait()
            for c in range(3):
                value = dot(act[s], low[:, c * 256 : (c + 1) * 256], tn)
                for i in range(2):
                    g = 2 * c + i
                    store_table(4 * j + g // 3, g % 3 * third, value[:, i * COLS : (i + 1) * COLS])

        @piece(1.15)
        def inner():
            def body(at):
                grad = (dot(low[at, :], wdown[s], nt) * slope[s, at, :].astype(f32)).astype(bf16)
                gin[at, :] = grad
                ffs[j] += fold(grad.astype(f32))

            by_pair(body)

        @piece(1.2, 4 * j + 2, 4 * j + 3)
        def outer():
            for c in range(2):
                value = dot(lows[...], gin[:, c * 256 : (c + 1) * 256], tn)
                for i in range(2):
                    store_table(4 * j + 2 + c, i * half, value[:, i * COLS : (i + 1) * COLS])

        @piece(1.15)
        def back():
            total[...] += dot(gin[...], win[s], nt)

    for j in range(count):
        ff_pieces(j)

    @piece(1.5)
    def norm_back():
        loads[7].start()
        loads[8].start()
        loads[2].wait()
        loads[3].wait()
        gain = g1_ref[...].reshape(1, D)

        def body(at):
            grad = total[at, :]
            hat = hat1[at, :]
            wide = grad * gain
            new = rstd1[at, 0:1] * (wide - jnp.mean(wide, -1, keepdims=True) - hat * jnp.mean(wide * hat, -1, keepdims=True))
            total[at, :] = new
            lowered = new.astype(bf16)
            gatt[at, :] = lowered
            for i, value in enumerate((grad * hat, grad, lowered.astype(f32))):
                lns[i] += fold(value)

        by_pair(body)

    base = 4 * count

    def out_piece(c):
        @piece(0.45, base + c)
        def out():
            if c == 0:
                loads[7].wait()
            value = dot(low[...], gatt[:, c * 256 : (c + 1) * 256], tn)
            for i in range(2):
                store_table(base + c, i * half, value[:, i * COLS : (i + 1) * COLS])

    for c in range(3):
        out_piece(c)

    @piece(2.0)
    def context_back():
        loads[5].wait()
        gctx[...] = dot(gatt[...], wout[...], nt).astype(bf16)

    lane = lax.broadcasted_iota(jnp.int32, (1, 2 * HEAD_DIM), 1)
    scale = HEAD_DIM**-0.5
    left = jnp.where(lane < HEAD_DIM, 1.0, 0.0).astype(bf16)
    right = jnp.where(lane < HEAD_DIM, 0.0, 1.0).astype(bf16)
    slot = lax.broadcasted_iota(jnp.int32, (SLOT, 1), 0)

    def pair_piece(p, part):
        @piece(1.9)
        def attention_back():
            if p == 0 and part == 0:
                loads[4].wait()
            words, regions = len_ref[0, first + p], len_ref[1, first + p]
            shut = jnp.where(jnp.where(slot < WORDS, words, regions + WORDS) > slot, 0.0, -1e30)
            at = slice(p * SLOT, (p + 1) * SLOT)
            for h in range(part * HEADS // 4, (part + 1) * HEADS // 4):
                c = h * 128
                q = packed[at, c : c + 128]
                k = packed[at, D + c : D + c + 128]
                v = packed[at, 2 * D + c : 2 * D + c + 128]
                g = gctx[at, c : c + 128]
                both = jnp.concatenate([q * (left * scale).astype(bf16), q * (right * scale).astype(bf16)], 0)
                grads = jnp.concatenate([g * left, g * right], 0)
                s = dot(k, both, nt) + shut
                e = jnp.exp(s - jnp.max(s, 0, keepdims=True))
                pr = e * (1.0 / jnp.sum(e, 0, keepdims=True))
                gp = dot(v, grads, nt)
                gs = (pr * (gp - jnp.sum(pr * gp, 0, keepdims=True))).astype(bf16)
                gq = dot(gs, k, tn)
                gq = jnp.where(lane < HEAD_DIM, gq[:SLOT], gq[SLOT:]) * scale
                gk = dot(gs, both)
                gv = dot(pr.astype(bf16), grads)
                for i, value in enumerate((gq, gk, gv)):
                    value = value.astype(bf16)
                    packed[at, i * D + c : i * D + c + 128] = value
                    if i != 1:
                        qs[:, i * D + c : i * D + c + 128] += fold(value.astype(f32))

    for p in range(pairs):
        for part in range(2):
            pair_piece(p, part)

    @piece(0.3, NBLK)
    def singles():
        def row(i, value):
            sbuf[i : i + 1, :] = value

        def down(x):
            return jnp.sum(x, 0, keepdims=True)

        row(0, down(qs[:, 0:D]))
        row(1, down(qs[:, 2 * D : 3 * D]))
        row(2, down(lns[2]))
        row(3, down(lns[0]))
        row(4, down(lns[1]))
        row(5, small2_ref[2:3, :])
        row(6, small2_ref[0:1, :])
        row(7, small2_ref[1:2, :])
        for j in range(count):
            at = j * FFB
            value = down(ffs[j])
            while value.shape[1]:
                room = min(D - at % D, value.shape[1])
                sbuf[8 + at // D : 9 + at // D, at % D : at % D + room] = value[:, :room]
                at, value = at + room, value[:, room:]
        sbuf[12:16, :] = jnp.zeros((4, D), f32)

    def qkv_piece(c):
        @piece(0.45, base + 3 + c)
        def qkv():
            if c == 0:
                loads[8].wait()
            value = dot(lows[...], packed[:, c * 256 : (c + 1) * 256], tn)
            for i in range(2):
                store_table(base + 3 + c, i * half, value[:, i * COLS : (i + 1) * COLS])

    for c in range(9):
        qkv_piece(c)

    def token_piece(c):
        @piece(1.5)
        def tokens_back():
            if c == 0:
                loads[6].wait()
            cols = slice(c * D, (c + 1) * D)
            total[...] += dot(packed[:, cols], wqkv[:, cols], nt)
            if c == 2:
                pltpu.make_async_copy(total, tgrad_hbm, out_sem).start()

    for c in range(3):
        token_piece(c)

    for what, block, step, _ in plan([(took, made) for took, made, _ in pieces], ex.extra):
        if what == "piece":
            pieces[block][2]()
        elif what == "start":
            ex.start(block, step)
        else:
            ex.handle(block, step)
    small_out[...] = sbuf[...]
    ex.finish()
    pltpu.make_async_copy(total, tgrad_hbm, out_sem).wait()


def backward(ndp, gsec, act, slope, low1, hat1, rstd1, ctx, packed, tokens, w_down, w_in, w_out, w_qkv, lengths, g1, small2):
    rows = tokens.shape[0]
    pairs = rows // SLOT
    anywhere = pl.BlockSpec(memory_space=pl.ANY)
    vmem = pl.BlockSpec(memory_space=pltpu.VMEM)
    smem = pl.BlockSpec(memory_space=pltpu.SMEM)
    S = jax.ShapeDtypeStruct
    V = pltpu.VMEM
    dma = pltpu.SemaphoreType.DMA
    return pl.pallas_call(
        functools.partial(backward_kernel, pairs, ndp),
        out_shape=(S((rows, D), f32), S((NBLK * BLK, COLS), bf16), S((16, D), f32)),
        in_specs=[anywhere] * 13 + [smem] + [vmem] * 2,
        out_specs=(anywhere, anywhere, vmem),
        scratch_shapes=[
            V((NBLK * BLK, COLS), bf16), V((rows, D), f32), V((rows, D), bf16), V((2, rows, FFB), bf16), V((2, rows, FFB), bf16), V((2, FFB, D), bf16), V((2, D, FFB), bf16),
            V((rows, FFB), bf16), V((rows, D), bf16), V((rows, D), f32), V((rows, 128), f32), V((rows, 3 * D), bf16), V((D, D), bf16), V((D, 3 * D), bf16),
            V((rows, D), bf16), V((rows, D), bf16), V((4 * D // FFB, 8, FFB), f32), V((3, 8, D), f32), V((8, 3 * D), f32),
            dma((9,)), dma((4, 2)), dma,
        ] + exchange_scratch(ndp),
        compiler_params=pltpu.CompilerParams(collective_id=1, has_side_effects=True, vmem_limit_bytes=VMEM_LIMIT),
        name="backward",
    )(gsec, act, slope, low1, hat1, rstd1, ctx, packed, tokens, w_down, w_in, w_out, w_qkv, lengths, g1, small2)


WIDE = (192, 384, 128, 512)


def widen_units():
    units = [(3, FFB * j + r, r, 12 * j) for j in range(6) for r in range(0, FFB, WIDE[3])]
    units += [(2, r, r, 0) for r in range(0, D, WIDE[2])]
    units += [(0, r, r, 54) for r in range(0, D, WIDE[0])]
    units += [(1, r, r, 48) for r in range(0, D, WIDE[1])]
    return units


def widen_kernel(depth, thirds, halves, eighths, small, tgrad, *refs):
    outs, singles, tgrad_out = refs[0:4], refs[4:13], refs[13]
    narrow, wide, held, in_sem, out_sem, own_sem = refs[14:18], refs[18:22], refs[22], refs[23], refs[24], refs[25]
    units = widen_units()
    take = pltpu.make_async_copy(tgrad, held, own_sem.at[0])
    move = pltpu.make_async_copy(held, tgrad_out, own_sem.at[1])

    def into(u):
        which, _, row, at = units[u]
        dst = narrow[which].at[u % depth]
        rows = pl.ds(row, WIDE[which])
        if which == 2:
            src = eighths.at[0:6, 4:8, rows]
        elif which == 3:
            src = thirds.at[pl.ds(at, 6), rows]
        else:
            src = halves.at[pl.ds(at, 18 if which == 0 else 6), rows]
        return pltpu.make_async_copy(src, dst, in_sem.at[u % depth])

    def back(u):
        which, row, _, _ = units[u]
        return pltpu.make_async_copy(wide[which].at[u % depth], outs[which].at[pl.ds(row, WIDE[which])], out_sem.at[u % depth])

    for u in range(depth - 1):
        into(u).start()
    for i in range(8):
        singles[i][...] = small[i, :]
    singles[8][...] = jnp.concatenate([small[i : i + 1, :] for i in range(8, 12)], 1).reshape(4 * D)
    for v in range(len(units)):
        if v + depth - 1 < len(units):
            into(v + depth - 1).start()
        if v == 0:
            take.start()
        if v == 4:
            take.wait()
            move.start()
        into(v).wait()
        if v >= depth:
            back(v - depth).wait()
        which, s = units[v][0], v % depth
        for c in range(wide[which].shape[2] // COLS):
            piece = narrow[which][s, c // 4, c % 4] if which == 2 else narrow[which][s, c]
            wide[which][s, :, c * COLS : (c + 1) * COLS] = piece.astype(f32)
        back(v).start()
    for v in range(len(units) - depth, len(units)):
        back(v).wait()
    move.wait()


def unpack_table(table, small, tgrad):
    anywhere = pl.BlockSpec(memory_space=pl.ANY)
    vmem = pl.BlockSpec(memory_space=pltpu.VMEM)
    depth = 3
    S = jax.ShapeDtypeStruct
    V = pltpu.VMEM
    dma = pltpu.SemaphoreType.DMA
    return pl.pallas_call(
        functools.partial(widen_kernel, depth),
        out_shape=(S((D, 3 * D), f32), S((D, D), f32), S((D, 4 * D), f32), S((4 * D, D), f32)) + (S((D,), f32),) * 8 + (S((4 * D,), f32), S(tgrad.shape, f32)),
        in_specs=[anywhere] * 3 + [vmem, anywhere],
        out_specs=(anywhere,) * 4 + (vmem,) * 9 + (anywhere,),
        scratch_shapes=[
            V((depth, 18, WIDE[0], COLS), bf16), V((depth, 6, WIDE[1], COLS), bf16), V((depth, 6, 4, WIDE[2], COLS), bf16), V((depth, 6, WIDE[3], COLS), bf16),
            V((depth, WIDE[0], 3 * D), f32), V((depth, WIDE[1], D), f32), V((depth, WIDE[2], 4 * D), f32), V((depth, WIDE[3], D), f32), V(tgrad.shape, f32),
            dma((depth,)), dma((depth,)), dma((2,)),
        ],
        compiler_params=pltpu.CompilerParams(vmem_limit_bytes=VMEM_LIMIT),
        name="widen",
    )(table.reshape(108, 512, COLS), table.reshape(72, D, COLS), table.reshape(9, 8, D, COLS), small, tgrad)


def on_device(ndp, tokens, cotangent, distance_cot, lengths, w_qkv, q_bias, v_bias, w_out, out_bias, ln1_gain, ln1_bias, w_in, in_bias, w_down, down_bias, ln2_gain, ln2_bias):
    sizes = jnp.transpose(lengths)
    result, distance, packed, ctx, hat1, low1, rstd1, act, slope, gsec, small2 = forward(
        tokens, cotangent, distance_cot, sizes, w_qkv, q_bias, v_bias, w_out, out_bias, ln1_gain, ln1_bias, w_in, in_bias, w_down, down_bias, ln2_gain, ln2_bias
    )
    grad_tokens, table, small = backward(ndp, gsec, act, slope, low1, hat1, rstd1, ctx, packed, tokens, w_down, w_in, w_out, w_qkv, sizes, ln1_gain, small2)
    g_qkv, g_out, g_in, g_down, g_qb, g_vb, g_ob, g_g1, g_b1, g_db, g_g2, g_b2, g_ib, grad_tokens = unpack_table(table, small, grad_tokens)
    return result, distance, grad_tokens, g_qkv, g_qb, g_vb, g_out, g_ob, g_g1, g_b1, g_in, g_ib, g_down, g_db, g_g2, g_b2


def solution(mesh):
    rows = P(("dp", "reg"), None)
    return jax.shard_map(
        functools.partial(on_device, mesh.shape["dp"]),
        mesh=mesh,
        in_specs=(rows, rows, P("dp"), P("dp", None)) + (P(),) * 13,
        out_specs=(rows, P(("dp", "reg")), rows) + (P(),) * 13,
        check_vma=False,
    )
```
